32 devices in a mesh: dp: 8 (over z, x), tensor: 4 (over y, core).
Axes of the slice: x: 2, y: 2, z: 4, core: 2. Of those that a mesh axis runs over, the one named last changes fastest.
Arguments:
- inputs: bfloat16 [12288, 1024], P(('dp', 'tensor')), may hold values from -6 to 6
- output_grad: bfloat16 [12288, 1024], P(('dp', 'tensor')), may hold values from -12 to 12
- input_project: bfloat16 [3, 1024, 1024], P(None, None, 'tensor'), may hold values from -0.1875 to 0.1875
- output_project: bfloat16 [1024, 1024], P('tensor'), may hold values from -2 to 2
- expand_weight: bfloat16 [1024, 4096], P(None, 'tensor'), may hold values from -0.1875 to 0.1875
- reduce_weight: bfloat16 [4096, 1024], P('tensor'), may hold values from -0.09375 to 0.09375
- first_gain: float32 [1024], replicated, may hold values from 0.5 to 1.5
- second_gain: float32 [1024], replicated, may hold values from 0.5 to 1.5
- biases: float32 [160, 64], replicated, may hold values from -1.2 to 1.2
- first_moment: float32 [160, 64], replicated, may hold values from -1 to 1
- second_moment: float32 [160, 64], replicated, may hold values from 0.004003906 to 0.016113281
- left_pairs: float32 [32, 32], replicated, may hold values from -1 to 1, as said below
- left_hidden: float32 [64, 64], replicated, may hold values from -1 to 1, as said below
- left_small: float32 [4, 16, 16], replicated, may hold values from -1 to 1, as said below
- right_bases: float32 [6, 64, 64], replicated, may hold values from -1 to 1, as said below
- segment_number: int32 [12288], P('dp'), may hold values from 0 to 511, as said below
- token_mask: int32 [12288], P('dp'), may hold values from 0 to 1, as said below
- owners: int32 [6], replicated, may hold values from 0 to 7, as said below
Outputs:
- layer_out: bfloat16 [12288, 1024], P(('dp', 'tensor'))
- input_grad: bfloat16 [12288, 1024], P(('dp', 'tensor'))
- bias_grads: float32 [160, 64], replicated
- clip_norm: float32 [1], replicated
- new_biases: float32 [1280, 64], P('dp')
- bias_copies: bfloat16 [160, 64], replicated
- new_first: float32 [1280, 64], P('dp')
- new_second: float32 [1280, 64], P('dp')
The draws below stay inside these ranges and needn't reach their ends.
Inputs may be any that keep to these rules, and one draw needn't show every extreme that they name: `segment_number`: within each packed row of 512 tokens the numbers start at 0 and never fall; the padding tail of a row, where token_mask is 0, has a number of its own. In one packed row every real token is a document of its own. `token_mask`: in each packed row the zeros form the tail. `owners`: six different dp indices, one for each bias matrix in the order of the views; 0, 4 and 7 are always among them. `left_pairs`: Orthogonal. `left_hidden`: Orthogonal. `left_small`: each matrix is orthogonal. `right_bases`: each matrix is orthogonal.
All inputs are finite; a program needn't handle non-finite values.
Results may differ from the reference program's by a relative error of at most 0.018.
Values may be sent and summed in bfloat16 or wider, within the bound.
A program may use at most 128 MiB of HBM per device.

```python
import math
import jax
import jax.numpy as jnp
from jax import lax

D = 1024
HEADS = 16
HD = 64
FF = 4096
SEQ = 512
STEP = 10
TOKENS = 12288
FR = 64
DR = 16
BROWS = 160
DP_RANKS = 8


def packing_layout(key):
    packed = TOKENS // SEQ
    length_key, start_key, pick_key = jax.random.split(key, 3)
    padding = jax.random.randint(length_key, (packed, 1), 0, SEQ // 4 + 1)
    places = jnp.arange(SEQ, dtype=jnp.int32)[None, :]
    starts = (jax.random.randint(start_key, (packed, SEQ), 0, SEQ) < 4) & (places > 0)
    picked_row = jax.random.randint(pick_key, (), 0, packed)
    is_picked = jnp.arange(packed, dtype=jnp.int32)[:, None] == picked_row
    starts = jnp.where(is_picked, places > 0, starts)
    padding = jnp.where(is_picked, 1, padding)
    valid = places < SEQ - padding
    numbers = jnp.cumsum((starts & valid).astype(jnp.int32), axis=1)
    numbers = jnp.where(valid, numbers, jnp.max(numbers, axis=1, keepdims=True) + 1)
    return (numbers.reshape(TOKENS).astype(jnp.int32), valid.astype(jnp.int32).reshape(TOKENS))


def orthogonal_set(key, amount, order):
    sign_key, order_key = jax.random.split(key)
    signs = jnp.where(jax.random.randint(sign_key, (amount, order, 1), 0, 2) == 0, -1.0, 1.0)

    def column_order(single):
        return jax.random.permutation(single, order)
    columns = jax.vmap(column_order)(jax.random.split(order_key, amount)).astype(jnp.int32)
    row_places = jnp.arange(order, dtype=jnp.int32)[None, :, None]
    common = jnp.bitwise_and(row_places, columns[:, None, :])
    parity = jnp.zeros_like(common)
    for level in range(order.bit_length() - 1):
        parity = parity + jnp.bitwise_and(jnp.right_shift(common, level), 1)
    entries = jnp.where(jnp.bitwise_and(parity, 1) == 0, 1.0, -1.0)
    return (entries * signs / math.sqrt(order)).astype(jnp.float32)


def draw_segment_number(key, part):
    numbers, valid = packing_layout(key)
    return numbers


def draw_token_mask(key, part):
    numbers, valid = packing_layout(key)
    return valid


def draw_owners(key, part):
    key = jax.random.fold_in(key, 11)
    first_key, second_key = jax.random.split(key)
    middle = jax.random.permutation(first_key, DP_RANKS - 3)[:3].astype(jnp.int32) + 1
    middle = middle + (middle >= DP_RANKS // 2).astype(jnp.int32)
    chosen = jnp.concatenate([jnp.array([0, DP_RANKS // 2, DP_RANKS - 1], jnp.int32), middle])
    return jax.random.permutation(second_key, chosen).astype(jnp.int32)


def draw_output_grad(key, part):
    key = jax.random.fold_in(key, 7)
    places = jnp.arange(TOKENS, dtype=jnp.float32)[:, None] / (TOKENS - 1)
    noise = jnp.clip(jax.random.normal(key, (TOKENS, D), jnp.float32), -4.0, 4.0)
    return (noise * (1.0 + 2.0 * places)).astype(jnp.bfloat16)


def draw_left_pairs(key, part):
    key = jax.random.fold_in(key, 21)
    return orthogonal_set(key, 1, 2 * HEADS)[0]


def draw_left_hidden(key, part):
    key = jax.random.fold_in(key, 22)
    return orthogonal_set(key, 1, FR)[0]


def draw_left_small(key, part):
    key = jax.random.fold_in(key, 23)
    return orthogonal_set(key, 4, DR)


def draw_right_bases(key, part):
    key = jax.random.fold_in(key, 24)
    return orthogonal_set(key, 6, HD)


def steps_of(own_key, shape, shards, low, top_value):
    loudness, own = 1.0, jax.random.fold_in(own_key, 6)
    for axis_at, parts in shards:
        heights = jnp.exp(jax.random.uniform(jax.random.fold_in(own, axis_at), (parts,), jnp.float32, low / len(shards), top_value / len(shards)))
        loudness = loudness * jnp.repeat(heights, shape[axis_at] // parts).reshape([-1 if axis == axis_at else 1 for axis in range(len(shape))])
    return loudness


def scatter_about(rng, shape, scale, most, pieces=(), kind=jnp.bfloat16):
    drawn = jax.random.normal(rng, shape, jnp.float32) * scale
    if len(pieces) > 0:
        drawn = steps_of(rng, shape, pieces, -0.22, 0.18) * drawn
    return jnp.clip(drawn, min=-most, max=most).astype(kind)


def setup_inputs(seed: int = 0) -> dict:
    streams_of = jax.random.split(jax.random.key(seed), 19)
    inputs = scatter_about(streams_of[0], (TOKENS, D), 1.0, 6.0, ((0, 32),))
    output_grad = draw_output_grad(jax.random.fold_in(streams_of[18], 71), 0)
    input_project = scatter_about(streams_of[2], (3, D, D), D ** -0.5, 0.1875, ((2, 4),))
    output_project = scatter_about(streams_of[3], (D, D), (D * 5 // SEQ) ** -0.5, 2.0, ((0, 4),))
    expand_weight = scatter_about(streams_of[4], (D, FF), D ** -0.5, 0.1875, ((1, 4),))
    reduce_weight = scatter_about(streams_of[5], (FF, D), FF ** -0.5, 0.09375, ((0, 4),))
    first_gain = jnp.clip(1.0 + 0.1 * jax.random.normal(streams_of[6], (D,), jnp.float32), 0.5, 1.5)
    second_gain = jnp.clip(1.0 + 0.1 * jax.random.normal(streams_of[7], (D,), jnp.float32), 0.5, 1.5)
    biases = scatter_about(streams_of[8], (BROWS, HD), 0.2, 1.2, (), jnp.float32)
    first_moment = scatter_about(streams_of[9], (BROWS, HD), (7.1 / (BROWS * HD) ** 0.5), 1.0, (), jnp.float32)
    second_moment = jnp.clip(jnp.exp(jax.random.uniform(streams_of[10], (BROWS, HD), jnp.float32, math.log(0.004003906), math.log(0.016113281))), 0.004003906, 0.016113281)
    left_pairs = draw_left_pairs(jax.random.fold_in(streams_of[18], 71), 0)
    left_hidden = draw_left_hidden(jax.random.fold_in(streams_of[18], 71), 0)
    left_small = draw_left_small(jax.random.fold_in(streams_of[18], 71), 0)
    right_bases = draw_right_bases(jax.random.fold_in(streams_of[18], 71), 0)
    segment_number = draw_segment_number(jax.random.fold_in(streams_of[18], 71), 0)
    token_mask = draw_token_mask(jax.random.fold_in(streams_of[18], 71), 0)
    owners = draw_owners(jax.random.fold_in(streams_of[18], 71), 0)
    return {"inputs": inputs, "output_grad": output_grad, "input_project": input_project, "output_project": output_project, "expand_weight": expand_weight, "reduce_weight": reduce_weight, "first_gain": first_gain, "second_gain": second_gain, "biases": biases, "first_moment": first_moment, "second_moment": second_moment, "left_pairs": left_pairs, "left_hidden": left_hidden, "left_small": left_small, "right_bases": right_bases, "segment_number": segment_number, "token_mask": token_mask, "owners": owners}


@jax.custom_vjp
def low(v):
    return lax.optimization_barrier(v.astype(jnp.bfloat16)).astype(jnp.float32)

@jax.custom_vjp
def low_back(v):
    return v

def low_keep(v):
    return (low(v), None)

def low_pass(kept, grad):
    return (grad,)

def back_keep(v):
    return (v, None)

def back_low(kept, grad):
    return (low(grad),)
low.defvjp(low_keep, low_pass)
low_back.defvjp(back_keep, back_low)
EPS_NORM = 1e-12
CLIP_LIMIT = 64.0
BETA_ONE = 0.9
BETA_TWO = 0.99
ADAM_EPS = 1e-08
LEARN_RATE = 0.2
HIGHEST_PRECISION = lax.Precision.HIGHEST

def layer_norm(values, gain):
    centred = values - lax.optimization_barrier(jnp.mean(values, axis=-1, keepdims=True))
    spread = lax.optimization_barrier(jnp.mean(centred * centred, axis=-1, keepdims=True))
    return centred * lax.rsqrt(spread + EPS_NORM) * gain

def attend(block):
    query, keys, values, segment, valid = block
    scores = jnp.einsum('qhd,khd->hqk', query, keys, precision=HIGHEST_PRECISION) * HD ** (-0.5)
    scores = low_back(scores)
    places = jnp.arange(SEQ, dtype=jnp.int32)
    allowed = (segment[:, None] == segment[None, :]) & ((valid[None, :] == 1) | (places[:, None] == places[None, :]))
    scores = jnp.where(allowed[None], scores, -1e+30)
    weights = low(jax.nn.softmax(scores, axis=-1))
    return jnp.einsum('hqk,khd->qhd', weights, values, precision=HIGHEST_PRECISION)

def forward(inputs, biases, input_project, output_project, expand_weight, reduce_weight, first_gain, second_gain, segment_number, token_mask):
    tail_start = 2 * HEADS + FR
    query_bias = biases[:HEADS].reshape(D)
    value_bias = biases[HEADS:2 * HEADS].reshape(D)
    hidden_bias = biases[2 * HEADS:tail_start].reshape(FF)
    out_bias = biases[tail_start:tail_start + DR].reshape(D)
    first_shift = biases[tail_start + DR:tail_start + 2 * DR].reshape(D)
    ffn_bias = biases[tail_start + 2 * DR:tail_start + 3 * DR].reshape(D)
    second_shift = biases[tail_start + 3 * DR:tail_start + 4 * DR].reshape(D)
    query = low(low_back(jnp.dot(inputs, input_project[0], precision=HIGHEST_PRECISION)) + query_bias)
    keys = low(low_back(jnp.dot(inputs, input_project[1], precision=HIGHEST_PRECISION)))
    values = low(low_back(jnp.dot(inputs, input_project[2], precision=HIGHEST_PRECISION)) + value_bias)
    packed = TOKENS // SEQ

    def shaped(array):
        return array.reshape(packed, SEQ, HEADS, HD)
    context = lax.map(jax.checkpoint(attend), (shaped(query), shaped(keys), shaped(values), segment_number.reshape(packed, SEQ), token_mask.reshape(packed, SEQ)))
    context = low(low_back(context.reshape(TOKENS, D)))
    attention_out = low_back(jnp.dot(context, output_project, precision=HIGHEST_PRECISION))
    first_pre = inputs + attention_out + out_bias
    first_normed = layer_norm(first_pre, first_gain) + first_shift
    hidden_pre = low_back(jnp.dot(low(first_normed), expand_weight, precision=HIGHEST_PRECISION)) + hidden_bias
    hidden = low(jax.nn.gelu(hidden_pre, approximate=False))
    ffn_out = low_back(jnp.dot(hidden, reduce_weight, precision=HIGHEST_PRECISION))
    second_pre = first_normed + ffn_out + ffn_bias
    return layer_norm(second_pre, second_gain) + second_shift

def soap_update(grad_block, moment_one, moment_two, old_block, left_basis, right_basis):
    rotated = jnp.dot(jnp.dot(left_basis.T, grad_block, precision=HIGHEST_PRECISION), right_basis, precision=HIGHEST_PRECISION)
    new_one = BETA_ONE * moment_one + (1.0 - BETA_ONE) * rotated
    new_two = BETA_TWO * moment_two + (1.0 - BETA_TWO) * rotated * rotated
    direction = new_one / (1.0 - BETA_ONE ** STEP) / (jnp.sqrt(new_two / (1.0 - BETA_TWO ** STEP)) + ADAM_EPS)
    turned = jnp.dot(jnp.dot(left_basis, direction, precision=HIGHEST_PRECISION), right_basis.T, precision=HIGHEST_PRECISION)
    return (old_block - LEARN_RATE * turned, new_one, new_two)

def reference(inputs, output_grad, input_project, output_project, expand_weight, reduce_weight, first_gain, second_gain, biases, first_moment, second_moment, left_pairs, left_hidden, left_small, right_bases, segment_number, token_mask, owners):
    project_wide = input_project.astype(jnp.float32)
    output_wide = output_project.astype(jnp.float32)
    expand_wide = expand_weight.astype(jnp.float32)
    reduce_wide = reduce_weight.astype(jnp.float32)

    def closed(input_values, bias_values):
        return forward(input_values, bias_values, project_wide, output_wide, expand_wide, reduce_wide, first_gain, second_gain, segment_number, token_mask)
    layer_values, pullback = jax.vjp(closed, inputs.astype(jnp.float32), biases)
    input_values_grad, bias_raw = pullback(output_grad.astype(jnp.float32))
    clip_norm = jnp.sqrt(jnp.sum(bias_raw * bias_raw))
    factor = CLIP_LIMIT / jnp.maximum(clip_norm, CLIP_LIMIT)
    clipped = bias_raw * factor
    tail_start = 2 * HEADS + FR
    layout = [(0, 2 * HEADS, left_pairs), (2 * HEADS, FR, left_hidden)]
    layout = layout + [(tail_start + which * DR, DR, left_small[which]) for which in range(4)]
    new_parts, one_parts, two_parts, owner_parts = ([], [], [], [])
    for which in range(6):
        begin, amount, left_basis = layout[which]
        fresh, moment_one, moment_two = soap_update(clipped[begin:begin + amount], first_moment[begin:begin + amount], second_moment[begin:begin + amount], biases[begin:begin + amount], left_basis, right_bases[which])
        new_parts.append(fresh)
        one_parts.append(moment_one)
        two_parts.append(moment_two)
        owner_parts.append(jnp.full((amount,), owners[which], jnp.int32))
    fresh_all = jnp.concatenate(new_parts, axis=0)
    one_all = jnp.concatenate(one_parts, axis=0)
    two_all = jnp.concatenate(two_parts, axis=0)
    owner_rows = jnp.concatenate(owner_parts, axis=0)
    ranks = jnp.arange(DP_RANKS, dtype=jnp.int32)
    chosen = (owner_rows[None, :] == ranks[:, None])[:, :, None]

    def spread_out(matrix):
        return jnp.where(chosen, matrix[None], jnp.zeros_like(matrix)[None]).reshape(DP_RANKS * BROWS, HD)
    return (layer_values.astype(jnp.bfloat16), input_values_grad.astype(jnp.bfloat16), clipped, clip_norm.reshape(1), spread_out(fresh_all), fresh_all.astype(jnp.bfloat16), spread_out(one_all), spread_out(two_all))
```

```python
import jax
import jax.numpy as jnp
from jax import lax
from jax.sharding import PartitionSpec as P

D = 1024
HEADS = 16
HD = 64
SEQ = 512
STEP = 10
FR = 64
DR = 16
BROWS = 160


EPS_NORM = 1e-12
CLIP_LIMIT = 64.0
BETA_ONE = 0.9
BETA_TWO = 0.99
ADAM_EPS = 1e-08
LEARN_RATE = 0.2
HIGHEST_PRECISION = lax.Precision.HIGHEST


def layer_norm(values, gain):
    centred = values - jnp.mean(values, axis=-1, keepdims=True)
    spread = jnp.mean(centred * centred, axis=-1, keepdims=True)
    return centred * lax.rsqrt(spread + EPS_NORM) * gain


def normed_back(values, gain, upstream):

    def inner(array):
        return layer_norm(array, gain)

    result, pullback = jax.vjp(inner, values)
    return pullback(upstream)[0]


def gelu_exact(values):
    return jax.nn.gelu(values, approximate=False)


def gelu_back(values, upstream):
    result, pullback = jax.vjp(gelu_exact, values)
    return pullback(upstream)[0]


def masked_scores(query, keys, allowed, score_scale):
    scores = (
        jnp.einsum("sqhd,skhd->shqk", query, keys, preferred_element_type=jnp.float32) * score_scale
    )
    return jnp.where(allowed[:, None], scores, -1e30)


def soap_update(grad_block, moment_one, moment_two, old_block, left_basis, right_basis):
    rotated = jnp.dot(
        jnp.dot(left_basis.T, grad_block, precision=HIGHEST_PRECISION),
        right_basis,
        precision=HIGHEST_PRECISION,
    )
    new_one = BETA_ONE * moment_one + (1.0 - BETA_ONE) * rotated
    new_two = BETA_TWO * moment_two + (1.0 - BETA_TWO) * rotated * rotated
    direction = (
        new_one / (1.0 - BETA_ONE**STEP) / (jnp.sqrt(new_two / (1.0 - BETA_TWO**STEP)) + ADAM_EPS)
    )
    turned = jnp.dot(
        jnp.dot(left_basis, direction, precision=HIGHEST_PRECISION),
        right_basis.T,
        precision=HIGHEST_PRECISION,
    )
    return (old_block - LEARN_RATE * turned, new_one, new_two)


def on_device(
    inputs,
    output_grad,
    input_project,
    output_project,
    expand_weight,
    reduce_weight,
    first_gain,
    second_gain,
    biases,
    first_moment,
    second_moment,
    left_pairs,
    left_hidden,
    left_small,
    right_bases,
    segment_number,
    token_mask,
    owners,
):
    tensor_rank = lax.axis_index("tensor")
    local_width = output_project.shape[0]
    local_heads = local_width // HD
    local_hidden = expand_weight.shape[1]
    token_rows = segment_number.shape[0]
    sequences = token_rows // SEQ
    score_scale = HD ** (-0.5)
    tail_start = 2 * HEADS + FR
    hidden_rows = local_hidden // HD
    query_bias = lax.dynamic_slice_in_dim(
        biases, tensor_rank * local_heads, local_heads, 0
    ).reshape(local_width)
    value_bias = lax.dynamic_slice_in_dim(
        biases, HEADS + tensor_rank * local_heads, local_heads, 0
    ).reshape(local_width)
    out_bias = biases[tail_start : tail_start + DR].reshape(D)
    first_shift = biases[tail_start + DR : tail_start + 2 * DR].reshape(D)
    ffn_bias = biases[tail_start + 2 * DR : tail_start + 3 * DR].reshape(D)
    second_shift = biases[tail_start + 3 * DR : tail_start + 4 * DR].reshape(D)
    full_inputs = lax.all_gather(inputs, "tensor", axis=0, tiled=True)
    projected = jnp.einsum(
        "td,cde->cte", full_inputs, input_project, preferred_element_type=jnp.float32
    )
    query_low = (
        (projected[0] + query_bias).astype(jnp.bfloat16).reshape(sequences, SEQ, local_heads, HD)
    )
    keys_low = projected[1].astype(jnp.bfloat16).reshape(sequences, SEQ, local_heads, HD)
    values_low = (
        (projected[2] + value_bias).astype(jnp.bfloat16).reshape(sequences, SEQ, local_heads, HD)
    )
    segments = segment_number.reshape(sequences, SEQ)
    valid = token_mask.reshape(sequences, SEQ)
    places = jnp.arange(SEQ, dtype=jnp.int32)
    allowed = (segments[:, :, None] == segments[:, None, :]) & (
        (valid[:, None, :] == 1) | (places[:, None] == places[None, :])[None]
    )
    scores = masked_scores(query_low, keys_low, allowed, score_scale)
    row_peak = jnp.max(scores, axis=-1, keepdims=True)
    row_total = jnp.sum(jnp.exp(scores - row_peak), axis=-1, keepdims=True)
    log_total = row_peak + jnp.log(row_total)
    probs_low = jnp.exp(scores - log_total).astype(jnp.bfloat16)
    context = jnp.einsum(
        "shqk,skhd->sqhd", probs_low, values_low, preferred_element_type=jnp.float32
    )
    context_low = context.reshape(token_rows, local_width).astype(jnp.bfloat16)
    portion = context_low
    attention_share = lax.psum_scatter(
        jnp.dot(portion, output_project, preferred_element_type=jnp.float32),
        "tensor",
        scatter_dimension=0,
        tiled=True,
    )
    first_pre = inputs.astype(jnp.float32) + attention_share + out_bias
    first_normed = layer_norm(first_pre, first_gain) + first_shift
    normed_low = first_normed.astype(jnp.bfloat16)
    hidden_bias = lax.dynamic_slice_in_dim(
        biases, 2 * HEADS + tensor_rank * hidden_rows, hidden_rows, 0
    ).reshape(local_hidden)
    hidden_pre = (
        jnp.dot(
            lax.all_gather(normed_low, "tensor", axis=0, tiled=True),
            expand_weight,
            preferred_element_type=jnp.float32,
        )
        + hidden_bias
    )
    hidden_low = gelu_exact(hidden_pre).astype(jnp.bfloat16)
    portion = hidden_low
    ffn_share = lax.psum_scatter(
        jnp.dot(portion, reduce_weight, preferred_element_type=jnp.float32).astype(jnp.bfloat16),
        "tensor",
        scatter_dimension=0,
        tiled=True,
    ).astype(jnp.float32)
    second_pre = first_normed + ffn_share + ffn_bias
    layer_out = (layer_norm(second_pre, second_gain) + second_shift).astype(jnp.bfloat16)
    upstream = output_grad.astype(jnp.float32)
    second_grad = normed_back(second_pre, second_gain, upstream)
    down_low = second_grad.astype(jnp.bfloat16)
    hidden_grad = jnp.einsum(
        "td,fd->tf",
        lax.all_gather(down_low, "tensor", axis=0, tiled=True),
        reduce_weight,
        preferred_element_type=jnp.float32,
    )
    pre_grad = gelu_back(hidden_pre, hidden_grad)
    pre_low = pre_grad.astype(jnp.bfloat16)
    portion = pre_low
    normed_part = lax.psum_scatter(
        jnp.einsum("tf,df->td", portion, expand_weight, preferred_element_type=jnp.float32).astype(
            jnp.bfloat16
        ),
        "tensor",
        scatter_dimension=0,
        tiled=True,
    ).astype(jnp.float32)
    hidden_start = 2 * HEADS + tensor_rank * hidden_rows
    normed_grad = second_grad + normed_part
    first_grad = normed_back(first_pre, first_gain, normed_grad)
    attention_grad_low = first_grad.astype(jnp.bfloat16)
    context_grad = jnp.einsum(
        "td,ed->te",
        lax.all_gather(attention_grad_low, "tensor", axis=0, tiled=True),
        output_project,
        preferred_element_type=jnp.float32,
    )
    context_grad_low = context_grad.astype(jnp.bfloat16).reshape(sequences, SEQ, local_heads, HD)
    scores = masked_scores(query_low, keys_low, allowed, score_scale)
    probs = jnp.exp(scores - log_total)
    prob_grad = jnp.einsum(
        "sqhd,skhd->shqk", context_grad_low, values_low, preferred_element_type=jnp.float32
    )
    row_delta = jnp.sum(probs * prob_grad, axis=-1, keepdims=True)
    score_grad = (probs * (prob_grad - row_delta)).astype(jnp.bfloat16)
    query_grad = (
        jnp.einsum("shqk,skhd->sqhd", score_grad, keys_low, preferred_element_type=jnp.float32)
        * score_scale
    )
    key_grad = (
        jnp.einsum("shqk,sqhd->skhd", score_grad, query_low, preferred_element_type=jnp.float32)
        * score_scale
    )
    value_grad = jnp.einsum(
        "shqk,sqhd->skhd", probs_low, context_grad_low, preferred_element_type=jnp.float32
    )
    stacked_low = (
        jnp.stack([query_grad, key_grad, value_grad])
        .reshape(3, token_rows, local_width)
        .astype(jnp.bfloat16)
    )
    portion = stacked_low
    input_share = lax.psum_scatter(
        jnp.einsum(
            "cte,cde->td", portion, input_project, preferred_element_type=jnp.float32
        ).astype(jnp.bfloat16),
        "tensor",
        scatter_dimension=0,
        tiled=True,
    ).astype(jnp.float32)
    input_grad = (first_grad + input_share).astype(jnp.bfloat16)
    zero_index = jnp.int32(0)
    bias_term = jnp.zeros((BROWS, HD), jnp.float32)
    bias_term = lax.dynamic_update_slice(
        bias_term, jnp.sum(query_grad, axis=(0, 1)), (tensor_rank * local_heads, zero_index)
    )
    bias_term = lax.dynamic_update_slice(
        bias_term, jnp.sum(value_grad, axis=(0, 1)), (HEADS + tensor_rank * local_heads, zero_index)
    )
    bias_term = lax.dynamic_update_slice(
        bias_term, jnp.sum(pre_grad, axis=0).reshape(-1, HD), (hidden_start, zero_index)
    )
    tail_sums = jnp.concatenate(
        [
            jnp.sum(first_grad, axis=0),
            jnp.sum(normed_grad, axis=0),
            jnp.sum(second_grad, axis=0),
            jnp.sum(upstream, axis=0),
        ]
    ).reshape(4 * DR, HD)
    bias_term = lax.dynamic_update_slice(bias_term, tail_sums, (jnp.int32(tail_start), zero_index))
    bias_total = lax.psum(bias_term, ("dp", "tensor"))
    clip_norm = jnp.sqrt(jnp.sum(bias_total * bias_total))
    clipped = bias_total * (CLIP_LIMIT / jnp.maximum(clip_norm, CLIP_LIMIT))
    dp_rank = lax.axis_index("dp")
    layout = [(0, 2 * HEADS, left_pairs), (2 * HEADS, FR, left_hidden)]
    layout = layout + [(tail_start + which * DR, DR, left_small[which]) for which in range(4)]
    new_parts, one_parts, two_parts, owned_rows = ([], [], [], [])
    for which in range(6):
        begin, amount, left_basis = layout[which]
        fresh, moment_one, moment_two = soap_update(
            clipped[begin : begin + amount],
            first_moment[begin : begin + amount],
            second_moment[begin : begin + amount],
            biases[begin : begin + amount],
            left_basis,
            right_bases[which],
        )
        new_parts.append(fresh)
        one_parts.append(moment_one)
        two_parts.append(moment_two)
        owned_rows.append(jnp.full((amount, 1), owners[which] == dp_rank))
    new_all = jnp.concatenate(new_parts, axis=0)
    mine = jnp.concatenate(owned_rows, axis=0)
    new_owned = jnp.where(mine, new_all, 0.0)
    first_owned = jnp.where(mine, jnp.concatenate(one_parts, axis=0), 0.0)
    second_owned = jnp.where(mine, jnp.concatenate(two_parts, axis=0), 0.0)
    fresh_all = new_all.astype(jnp.bfloat16)
    return (
        layer_out,
        input_grad,
        clipped,
        clip_norm.reshape(1),
        new_owned,
        fresh_all,
        first_owned,
        second_owned,
    )


def solution(mesh):
    return jax.shard_map(
        on_device,
        mesh=mesh,
        in_specs=(
            P(("dp", "tensor"), None),
            P(("dp", "tensor"), None),
            P(None, None, "tensor"),
            P("tensor", None),
            P(None, "tensor"),
            P("tensor", None),
            P(),
            P(),
            P(),
            P(),
            P(),
            P(),
            P(),
            P(),
            P(),
            P("dp"),
            P("dp"),
            P(),
        ),
        out_specs=(
            P(("dp", "tensor"), None),
            P(("dp", "tensor"), None),
            P(),
            P(),
            P("dp", None),
            P(),
            P("dp", None),
            P("dp", None),
        ),
        check_vma=False,
    )
```

```python
from functools import partial

import jax
import jax.numpy as jnp
from jax import lax
from jax.experimental import pallas as pl
from jax.experimental.pallas import tpu as pltpu
from jax.sharding import PartitionSpec as P

D = 1024
HEADS = 16
HD = 64
PAIR = 2 * HD
SEQ = 512
STEP = 10
FR = 64
DR = 16
BROWS = 160
AT_QUERY, AT_VALUE, AT_HIDDEN = 0, D, 2 * D
AT_OUT = 2 * D + FR * HD
AT_FIRST, AT_FFN, AT_SECOND = AT_OUT + D, AT_OUT + 2 * D, AT_OUT + 3 * D
FLAT = BROWS * HD

EPS_NORM = 1e-12
CLIP_LIMIT = 64.0
BETA_ONE = 0.9
BETA_TWO = 0.99
ADAM_EPS = 1e-08
LEARN_RATE = 0.2
HIGHEST = lax.Precision.HIGHEST
MESH_ID = pl.DeviceIdType.MESH
BF16 = jnp.bfloat16
F32 = jnp.float32

SUBS = 4
UNIT = 256
TILE = 256


def nn(a, b):
    return jnp.dot(a, b, preferred_element_type=F32)


def nt(a, b):
    return lax.dot_general(a, b, (((1,), (1,)), ((), ())), preferred_element_type=F32)


def tn(a, b):
    return lax.dot_general(a, b, (((0,), (0,)), ((), ())), preferred_element_type=F32)


def flip(value, bit):
    return value + bit - 2 * bit * ((value // bit) % 2)


class Layout:
    def __init__(self, dp_size, ranks, tokens):
        self.dp_size, self.ranks, self.tokens = dp_size, ranks, tokens
        self.block = 1
        while tokens % (2 * self.block) == 0 and SEQ % (2 * self.block) == 0:
            self.block *= 2
        self.blocks = tokens // self.block
        self.units = SEQ // self.block
        self.width = D // ranks
        self.pairs = self.width // PAIR
        self.hidden = FR * HD // ranks
        rows = ranks * tokens // SEQ
        self.span = 1
        for row in range(rows):
            first = row * self.units // self.blocks
            last = (row * self.units + self.units - 1) // self.blocks
            self.span = max(self.span, last - first + 1)
        self.quads = ranks == 4 and dp_size % 4 == 0
        self.stages = [("tensor", 1 << b) for b in range(ranks.bit_length() - 1)]
        self.stages += [("dp", 1 << b) for b in range(dp_size.bit_length() - 1)]


def layer_kernel(
    lay,
    x,
    og,
    gain1,
    gain2,
    brow,
    seg,
    val,
    wqkv_in,
    wo_in,
    w1_in,
    w2_in,
    out,
    ig,
    bsum,
    wqkv,
    wo_b,
    w1_b,
    w2_b,
    xkv,
    qbuf,
    kbuf,
    vbuf,
    pbuf,
    linv,
    mask,
    ctx,
    cgrad,
    abuf,
    bbuf,
    cbuf,
    r1buf,
    low,
    hid,
    gp,
    back,
    dka,
    dva,
    arecv,
    sem_local,
    sem_own_s,
    sem_own_r,
    sem_y,
    sem_x,
    sem_z,
    sem_c,
    sem_w,
    sem_p,
    sem_hs,
    sem_hr,
    sem_gs,
    sem_gr,
    sem_as,
    sem_ar,
):
    T, S, B, NB, NU = lay.ranks, lay.tokens, lay.block, lay.blocks, lay.units
    W, PP, F = lay.width, lay.pairs, lay.hidden
    dp = lax.axis_index("dp")
    t = lax.axis_index("tensor")
    quads = lay.quads

    def rank(o):
        r = (t + o) % 2
        if T > 2:
            r = r + 2 * ((t // 2 + o // 2) % 2)
        if T > 4:
            r = r + 4 * ((t // 4 + o // 4) % 2)
        return r

    if quads:
        big = wo_b

        def wo(r):
            return big.at[r, pl.ds(0, W)]

        def w1(r):
            return big.at[r, pl.ds(W, D)]

        def w2(r):
            return big.at[r, pl.ds(W + D, F)]
    else:

        def wo(r):
            return wo_b.at[r]

        def w1(r):
            return w1_b.at[r]

        def w2(r):
            return w2_b.at[r]

    def pieces(r):
        return [wqkv.at[r], wo(r), w1(r), w2(r)]

    sources = [wqkv_in, wo_in, w1_in, w2_in]

    def peer(o):
        return (dp, rank(o))

    def remote(src, dst, send, recv, device):
        return pltpu.make_async_remote_copy(
            src_ref=src,
            dst_ref=dst,
            send_sem=send,
            recv_sem=recv,
            device_id=device,
            device_id_type=MESH_ID,
        )

    barrier = pltpu.get_barrier_semaphore()
    others = [peer(o) for o in range(1, T)]
    others += [(flip(dp, bit), t) for axis, bit in lay.stages if axis == "dp"]
    for device in others:
        pl.semaphore_signal(barrier, inc=1, device_id=device, device_id_type=MESH_ID)
    local = [
        pltpu.make_async_copy(src, dst, sem_local.at[i])
        for i, (src, dst) in enumerate(zip(sources, pieces(t)))
    ]
    for copy in local:
        copy.start()
    pl.semaphore_wait(barrier, len(others))

    row0 = (NB * t) // NU
    has_b = (NB * t + NB - 1) // NU != row0

    def place(j):
        u = NB * t + j
        row = u // NU
        return u, row, row - row0, u - row * NU

    def rows_at(w):
        return pl.ds(pl.multiple_of(w * B, B), B)

    def block_at(j):
        return pl.ds(j * B, B)

    for j in range(NB):
        u, row, slot, w = place(j)
        first = row * NU // NB
        last = (row * NU + NU - 1) // NB
        for o in range(lay.span):
            dest = first + o

            @pl.when((dest <= last) & (dest != t))
            def _():
                remote(
                    x.at[block_at(j)],
                    xkv.at[row - (NB * dest) // NU, rows_at(w)],
                    sem_hs.at[j * lay.span + o],
                    sem_hr.at[(row - (NB * dest) // NU) * NU + w],
                    (dp, dest),
                ).start()

    if quads:
        role = dp % 4
        relay = role == 3
        gy = role % 3
        gx = jnp.where(role == 1, 0, jnp.where(role == 3, 2, 1))
        gz = jnp.where(role == 2, 0, jnp.where(role == 3, 1, 2))
        far = rank(2)
        core, ynext = (dp, rank(1)), (dp, rank(2))
        xnext, znext = (flip(dp, 1), t), (flip(dp, 2), t)
        rounds = 4
        steps = rounds * SUBS
        part_a, part_b = D // SUBS, UNIT // SUBS

        def chunk(idx, g, fn):
            n = (idx // SUBS * 3 + g) * SUBS + idx % SUBS

            @pl.when((idx >= 0) & (idx < SUBS))
            def _():
                at = pl.ds(pl.multiple_of(idx * part_a, part_a), part_a)
                fn(lambda r: wqkv.at[r, g, at], n)

            @pl.when((idx >= SUBS) & (idx < steps))
            def _():
                row = ((idx // SUBS - 1) * 3 + g) * UNIT + (idx % SUBS) * part_b
                at = pl.ds(pl.multiple_of(row, part_b), part_b)
                fn(lambda r: big.at[r, at], n)

        def send_y(idx):
            def go(view, n):
                remote(view(t), view(t), sem_y.at[idx], sem_w.at[n], ynext).start()

            chunk(idx, gy, go)

        def to_core(view, n):
            remote(view(far), view(far), sem_c.at[n], sem_p.at[n], core).start()

        def arrived(view, n):
            remote(view(far), view(far), sem_c.at[n], sem_w.at[n], core).wait_recv()

        def to_x(view, n, idx):
            remote(view(far), view(far), sem_x.at[idx], sem_w.at[n], xnext).start()

        def to_z(view, n, idx):
            remote(view(far), view(far), sem_z.at[idx], sem_w.at[n], znext).start()

        def service(s, carry):
            def from_y(view, n):
                arrived(view, n)

                @pl.when(role != 3)
                def _():
                    to_x(view, n, s)
                    to_z(view, n, s)

                to_core(view, n)

            chunk(s, gy, from_y)
            send_y(s + SUBS)
            late = s - jnp.where(relay, 1, 2)

            def from_x(view, n):
                arrived(view, n)

                @pl.when(relay)
                def _():
                    to_z(view, n, late)

                to_core(view, n)

            def from_z(view, n):
                arrived(view, n)

                @pl.when(relay)
                def _():
                    to_x(view, n, late)

                to_core(view, n)

            chunk(late, gx, from_x)
            chunk(late, gz, from_z)
            return carry

        def services(low_step, high_step):
            lax.fori_loop(low_step, high_step, service, 0)

        def sent(idx, carry):
            def go(view, n):
                remote(view(t), view(t), sem_y.at[idx], sem_w.at[n], ynext).wait_send()
                remote(view(t), view(t), sem_x.at[idx], sem_w.at[n], xnext).wait_send()
                remote(view(t), view(t), sem_z.at[idx], sem_w.at[n], znext).wait_send()
                for g in range(3):
                    m = (idx // SUBS * 3 + g) * SUBS + idx % SUBS
                    remote(view(t), view(t), sem_c.at[m], sem_p.at[m], core).wait_send()

            chunk(idx, gy, go)
            return carry

        def from_partner(unit_low, unit_high):
            def go(n, carry):
                @pl.when(n < 3 * SUBS)
                def _():
                    view = wqkv.at[rank(3), 0, pl.ds(0, part_a)]
                    remote(view, view, sem_c.at[n], sem_p.at[n], core).wait_recv()

                @pl.when(n >= 3 * SUBS)
                def _():
                    view = big.at[rank(3), pl.ds(0, part_b)]
                    remote(view, view, sem_c.at[n], sem_p.at[n], core).wait_recv()

                return carry

            lax.fori_loop(unit_low * SUBS, unit_high * SUBS, go, 0)

        def own_copies(i):
            return remote(sources[i], pieces(t)[i], sem_own_s.at[i], sem_own_r.at[i], core)

        local[0].wait()
        lax.fori_loop(0, SUBS, lambda i, c: (send_y(i), c)[1], 0)
        for i in range(4):
            own_copies(i).start()
        for i in range(1, 4):
            local[i].wait()

        def have(i, o):
            if o == 1:
                remote(
                    sources[i], pieces(rank(1))[i], sem_own_s.at[i], sem_own_r.at[i], core
                ).wait_recv()

    else:

        def own_copies(i, o):
            n = i * T + o
            return remote(sources[i], pieces(t)[i], sem_own_s.at[n], sem_own_r.at[n], peer(o))

        for i in range(4):
            for o in range(1, T):
                own_copies(i, o).start()

        def services(low_step, high_step):
            pass

        def have(i, o):
            if o == 0:
                local[i].wait()
            else:
                n = i * T + o
                remote(
                    sources[i], pieces(rank(o))[i], sem_own_s.at[n], sem_own_r.at[n], peer(o)
                ).wait_recv()

    key_at = lax.broadcasted_iota(jnp.int32, (B, SEQ), 1)
    query_at = lax.broadcasted_iota(jnp.int32, (B, SEQ), 0)
    for j in range(NB):
        u, row, slot, w = place(j)
        numbers = seg[pl.ds(row, 1), :].astype(F32)
        keyed = jnp.where(val[pl.ds(row, 1), :] == 1, numbers, -1.0)
        same = key_at == query_at + w * B
        own = jnp.sum(jnp.where(same, numbers, 0.0), axis=1, keepdims=True)
        mask[j] = jnp.where((own == keyed) | same, 0.0, -1e30)
        xkv[slot, rows_at(w)] = x[block_at(j)]

    head_lane = lax.broadcasted_iota(jnp.int32, (B, PAIR), 1) < HD

    def split_heads(values):
        nought = jnp.zeros_like(values)
        return jnp.concatenate(
            [jnp.where(head_lane, values, nought), jnp.where(head_lane, nought, values)], axis=0
        )

    def join_heads(values):
        return jnp.where(head_lane, values[:B], values[B:])

    ones = jnp.ones((SEQ, PAIR), BF16)

    slot_first = jnp.where(has_b & (t % 4 == 2), 1, 0)

    def project_query(r):
        bias = brow[:, pl.ds(pl.multiple_of(AT_QUERY + r * W, PAIR), W)]
        query = ((nn(x[...], wqkv[r, 0]) + bias) * HD**-0.5).astype(BF16)
        for i in range(PP):
            qbuf[r * PP + i] = query[:, i * PAIR : (i + 1) * PAIR]

    def project_keys(r, first_time):
        bias = brow[:, pl.ds(pl.multiple_of(AT_VALUE + r * W, PAIR), W)]

        def body(turn, carry):
            slot = (slot_first + turn) % 2

            @pl.when((slot == 0) | has_b)
            def _():
                if first_time:
                    for w in range(NU):
                        owner = ((row0 + slot) * NU + w) // NB

                        @pl.when(owner != t)
                        def _():
                            remote(
                                x.at[block_at(0)],
                                xkv.at[slot, rows_at(w)],
                                sem_hs.at[0],
                                sem_hr.at[slot * NU + w],
                                (dp, owner),
                            ).wait_recv()

                rows = xkv[slot]
                keys = nn(rows, wqkv[r, 1]).astype(BF16)
                values = (nn(rows, wqkv[r, 2]) + bias).astype(BF16)
                for i in range(PP):
                    kbuf[r * PP + i, slot] = keys[:, i * PAIR : (i + 1) * PAIR]
                    vbuf[r * PP + i, slot] = values[:, i * PAIR : (i + 1) * PAIR]

            return carry

        lax.fori_loop(0, 2, body, 0)

    def attend(r, i):
        hp = r * PP + i
        for j in range(NB):
            u, row, slot, w = place(j)
            query = split_heads(qbuf[hp, block_at(j)])
            hide = mask[j]
            scores = nt(query, kbuf[hp, slot]) + jnp.concatenate([hide, hide], axis=0)
            peak = jnp.max(scores, axis=1, keepdims=True)
            probs = jnp.exp(scores - peak).astype(BF16)
            pbuf[hp, j] = probs
            mixed = nn(probs, jnp.concatenate([vbuf[hp, slot], ones], axis=1))
            inverse = 1.0 / join_heads(mixed[:, PAIR:])
            linv[hp, block_at(j)] = inverse
            ctx[r, block_at(j), pl.ds(i * PAIR, PAIR)] = (
                join_heads(mixed[:, :PAIR]) * inverse
            ).astype(BF16)

    def attention(o, first_time):
        r = rank(o)
        project_query(r)
        project_keys(r, first_time)
        for i in range(PP):
            attend(r, i)

    arrival = [(k + 1) * SUBS + 2 for k in range(4)]
    have(0, 0) if not quads else None
    attention(0, True)
    have(0, 1)
    services(0, 2)
    attention(1, False)
    if quads:
        services(2, arrival[0])
        attention(2, False)
        services(arrival[0], arrival[0] + 2)
        from_partner(0, 3)
        attention(3, False)
        services(arrival[0] + 2, arrival[1])
        have(1, 1)
        from_partner(3, 4)
    else:
        for o in range(2, T):
            have(0, o)
            attention(o, False)
        for o in range(T):
            have(1, o)

    for n in range(0, D, TILE):
        total = nn(ctx[0], wo(0)[:, n : n + TILE])
        for r in range(1, T):
            total = total + nn(ctx[r], wo(r)[:, n : n + TILE])
        at = pl.ds(n, TILE)
        abuf[:, at] = x[:, at].astype(F32) + total + brow[:, AT_OUT + n : AT_OUT + n + TILE]

    def row_mean(values):
        return jnp.mean(values, axis=1, keepdims=True)

    def row_tiles(body, carry):
        for j in range(NB):
            carry = body(block_at(j), carry)
        return carry

    def norm_first(at, carry):
        values = abuf[at]
        centred = values - row_mean(values)
        root = lax.rsqrt(row_mean(centred * centred) + EPS_NORM)
        normed = centred * root
        r1buf[at] = root
        abuf[at] = normed
        low[at] = (normed * gain1[...] + brow[:, AT_FIRST : AT_FIRST + D]).astype(BF16)
        return carry

    row_tiles(norm_first, 0)

    def expand(o):
        r = rank(o)
        for n in range(0, F, TILE):
            bias = brow[:, pl.ds(pl.multiple_of(AT_HIDDEN + r * F + n, PAIR), TILE)]
            pre = nn(low[...], w1(r)[:, n : n + TILE]) + bias
            cdf = 0.5 * (1.0 + lax.erf(pre * 0.5**0.5))
            density = jnp.exp(-0.5 * pre * pre) * 0.3989422804014327
            hid[r, :, pl.ds(n, TILE)] = (pre * cdf).astype(BF16)
            gp[r, :, pl.ds(n, TILE)] = (cdf + pre * density).astype(BF16)

    def reduce(o, start):
        r = rank(o)
        for n in range(0, D, TILE):
            at = pl.ds(n, TILE)
            part = nn(hid[r], w2(r)[:, n : n + TILE])
            bbuf[:, at] = part if start else bbuf[:, at] + part

    have(2, 0) if not quads else None
    expand(0)
    have(2, 1)
    expand(1)
    if quads:
        services(arrival[1], arrival[1] + 2)
        reduce(0, True)
        have(3, 1)
        reduce(1, False)
        services(arrival[1] + 2, arrival[2])
        expand(2)
        from_partner(4, 8)
        expand(3)
        services(arrival[2], arrival[3])
        reduce(2, False)
        from_partner(8, 12)
        reduce(3, False)
    else:
        for o in range(2, T):
            have(2, o)
            expand(o)
        for o in range(T):
            have(3, o)
            reduce(o, o == 0)

    nought_row = jnp.zeros((1, D), F32)

    def norm_second(at, carry):
        sum_up, sum_second = carry
        first_normed = abuf[at] * gain1[...] + brow[:, AT_FIRST : AT_FIRST + D]
        values = first_normed + bbuf[at] + brow[:, AT_FFN : AT_FFN + D]
        centred = values - row_mean(values)
        root = lax.rsqrt(row_mean(centred * centred) + EPS_NORM)
        normed = centred * root
        out[at] = (normed * gain2[...] + brow[:, AT_SECOND : AT_SECOND + D]).astype(BF16)
        upstream = og[at].astype(F32)
        weighted = upstream * gain2[...]
        grad = root * (weighted - row_mean(weighted) - normed * row_mean(weighted * normed))
        bbuf[at] = grad
        low[at] = grad.astype(BF16)
        return (
            sum_up + jnp.sum(upstream, axis=0, keepdims=True),
            sum_second + jnp.sum(grad, axis=0, keepdims=True),
        )

    sum_up, sum_second = row_tiles(norm_second, (nought_row, nought_row))
    bsum[:, AT_SECOND : AT_SECOND + D] = sum_up
    bsum[:, AT_FFN : AT_FFN + D] = sum_second

    def ffn_back(r, carry):
        for n in range(0, F, TILE):
            grad = nt(low[...], w2(r)[n : n + TILE, :]) * gp[r, :, pl.ds(n, TILE)].astype(F32)
            at = pl.ds(pl.multiple_of(AT_HIDDEN + r * F + n, PAIR), TILE)
            bsum[:, at] = jnp.sum(grad, axis=0, keepdims=True)
            hid[r, :, pl.ds(n, TILE)] = grad.astype(BF16)
        return carry

    lax.fori_loop(0, T, ffn_back, 0)
    for n in range(0, D, TILE):
        total = nt(hid[0], w1(0)[n : n + TILE, :])
        for r in range(1, T):
            total = total + nt(hid[r], w1(r)[n : n + TILE, :])
        cbuf[:, pl.ds(n, TILE)] = total

    def first_back(at, carry):
        sum_normed, sum_first = carry
        grad = bbuf[at] + cbuf[at]
        normed = abuf[at]
        weighted = grad * gain1[...]
        first = r1buf[at] * (
            weighted - row_mean(weighted) - normed * row_mean(weighted * normed)
        )
        bbuf[at] = first
        low[at] = first.astype(BF16)
        return (
            sum_normed + jnp.sum(grad, axis=0, keepdims=True),
            sum_first + jnp.sum(first, axis=0, keepdims=True),
        )

    sum_normed, sum_first = row_tiles(first_back, (nought_row, nought_row))
    bsum[:, AT_FIRST : AT_FIRST + D] = sum_normed
    bsum[:, AT_OUT : AT_OUT + D] = sum_first

    for r in range(T):
        cgrad[r] = nt(low[...], wo(r)[...]).astype(BF16)

    def attend_back(r, i):
        hp = r * PP + i
        dka[...] = jnp.zeros_like(dka)
        dva[...] = jnp.zeros_like(dva)
        query_sum = jnp.zeros((1, PAIR), F32)
        for j in range(NB):
            u, row, slot, w = place(j)
            lanes = pl.ds(i * PAIR, PAIR)
            scaled = cgrad[r, block_at(j), lanes].astype(F32) * linv[hp, block_at(j)]
            upstream = split_heads(scaled.astype(BF16))
            delta = jnp.sum(
                split_heads(scaled * ctx[r, block_at(j), lanes].astype(F32)), axis=1, keepdims=True
            )
            probs = pbuf[hp, j]
            query = split_heads(qbuf[hp, block_at(j)])
            score = (probs.astype(F32) * (nt(upstream, vbuf[hp, slot]) - delta)).astype(BF16)
            dva[slot] += tn(probs, upstream)
            dka[slot] += tn(score, query)
            grad = join_heads(nn(score, kbuf[hp, slot])) * HD**-0.5
            qbuf[hp, block_at(j)] = grad.astype(BF16)
            query_sum = query_sum + jnp.sum(grad, axis=0, keepdims=True)
        value_sum = jnp.zeros((1, PAIR), F32)
        for slot in range(2):
            kbuf[hp, slot] = dka[slot].astype(BF16)
            vbuf[hp, slot] = dva[slot].astype(BF16)
            value_sum = value_sum + jnp.sum(dva[slot], axis=0, keepdims=True)
        lanes = pl.multiple_of(r * W + i * PAIR, PAIR)
        bsum[:, pl.ds(AT_QUERY + lanes, PAIR)] = query_sum
        bsum[:, pl.ds(AT_VALUE + lanes, PAIR)] = value_sum

    def rank_back(r, carry):
        for i in range(PP):
            attend_back(r, i)
        return carry

    lax.fori_loop(0, T, rank_back, 0)

    def stage_copy(i):
        axis, bit = lay.stages[i]
        device = (dp, flip(t, bit)) if axis == "tensor" else (flip(dp, bit), t)
        return remote(bsum, arecv.at[i], sem_as.at[i], sem_ar.at[i], device)

    def stage_end(i):
        stage_copy(i).wait()
        bsum[...] = bsum[...] + arecv[i]

    stage_copy(0).start()

    def wide(buffer, r, *at):
        return jnp.concatenate([buffer[(r * PP + i, *at)] for i in range(PP)], axis=1)

    def shares(slot):
        def body(k, carry):
            at = pl.ds(pl.multiple_of(k * TILE, TILE), TILE)
            total = nt(wide(kbuf, 0, slot), wqkv[0, 1, at])
            total = total + nt(wide(vbuf, 0, slot), wqkv[0, 2, at])
            for r in range(1, T):
                total = total + nt(wide(kbuf, r, slot), wqkv[r, 1, at])
                total = total + nt(wide(vbuf, r, slot), wqkv[r, 2, at])
            xkv[slot, :, at] = total.astype(BF16)
            return carry

        lax.fori_loop(0, D // TILE, body, 0)

    def share_copy(slot, w):
        u = (row0 + slot) * NU + w
        owner = u // NB
        first = (row0 + slot) * NU // NB
        place_of = t - first - jnp.where(t > owner, 1, 0)
        number = (u - owner * NB) * (lay.span - 1) + place_of
        return remote(
            xkv.at[slot, rows_at(w)],
            back.at[number],
            sem_gs.at[slot * NU + w],
            sem_gr.at[number],
            (dp, owner),
        )

    def send_shares(turn, carry):
        slot = (1 - slot_first + turn) % 2

        @pl.when((slot == 0) | has_b)
        def _():
            shares(slot)
            for w in range(NU):
                owner = ((row0 + slot) * NU + w) // NB

                @pl.when(owner != t)
                def _():
                    share_copy(slot, w).start()

        return carry

    lax.fori_loop(0, 2, send_shares, 0)
    stage_end(0)
    if len(lay.stages) > 1:
        stage_copy(1).start()

    for n in range(0, D, TILE):
        total = nt(wide(qbuf, 0), wqkv[0, 0, pl.ds(n, TILE)])
        for r in range(1, T):
            total = total + nt(wide(qbuf, r), wqkv[r, 0, pl.ds(n, TILE)])
        at = pl.ds(n, TILE)
        bbuf[:, at] = bbuf[:, at] + total

    for i in range(1, len(lay.stages)):
        stage_end(i)
        if i + 1 < len(lay.stages):
            stage_copy(i + 1).start()

    for j in range(NB):
        u, row, slot, w = place(j)
        first = row * NU // NB
        last = (row * NU + NU - 1) // NB
        bbuf[block_at(j)] = bbuf[block_at(j)] + xkv[slot, rows_at(w)].astype(F32)
        for o in range(lay.span - 1):
            number = j * (lay.span - 1) + o

            @pl.when(first + o < last)
            def _():
                sender = first + o + jnp.where(first + o >= t, 1, 0)
                remote(
                    xkv.at[0, rows_at(0)],
                    back.at[number],
                    sem_gs.at[0],
                    sem_gr.at[number],
                    (dp, sender),
                ).wait_recv()
                bbuf[block_at(j)] = bbuf[block_at(j)] + back[number].astype(F32)

        ig[block_at(j)] = bbuf[block_at(j)].astype(BF16)

    for slot in range(2):
        for w in range(NU):
            owner = ((row0 + slot) * NU + w) // NB

            @pl.when((owner != t) & ((slot == 0) | has_b))
            def _():
                share_copy(slot, w).wait_send()

    for j in range(NB):
        u, row, slot, w = place(j)
        first = row * NU // NB
        last = (row * NU + NU - 1) // NB
        for o in range(lay.span):
            dest = first + o

            @pl.when((dest <= last) & (dest != t))
            def _():
                remote(
                    x.at[block_at(j)],
                    xkv.at[0, rows_at(0)],
                    sem_hs.at[j * lay.span + o],
                    sem_hr.at[0],
                    (dp, dest),
                ).wait_send()

    if quads:
        for i in range(4):
            own_copies(i).wait_send()
        lax.fori_loop(0, steps, sent, 0)
    else:
        for i in range(4):
            for o in range(1, T):
                own_copies(i, o).wait_send()


def layer_call(lay, *args):
    T, S = lay.ranks, lay.tokens
    hp = HEADS // 2
    vmem = pltpu.VMEM
    if lay.quads:
        wide = [
            vmem((T, lay.width + D + lay.hidden, D), BF16),
            vmem((16, PAIR), BF16),
            vmem((16, PAIR), BF16),
        ]
    else:
        wide = [
            vmem((T, lay.width, D), BF16),
            vmem((T, D, lay.hidden), BF16),
            vmem((T, lay.hidden, D), BF16),
        ]
    dma = pltpu.SemaphoreType.DMA
    steps = 4 * SUBS
    own = 4 if lay.quads else 4 * T
    stages = len(lay.stages)
    sharers = lay.blocks * max(lay.span - 1, 1)
    scratch = (
        [vmem((T, 3, D, lay.width), BF16)]
        + wide
        + [
            vmem((2, SEQ, D), BF16),
            vmem((hp, S, PAIR), BF16),
            vmem((hp, 2, SEQ, PAIR), BF16),
            vmem((hp, 2, SEQ, PAIR), BF16),
            vmem((hp, lay.blocks, 2 * lay.block, SEQ), BF16),
            vmem((hp, S, PAIR), F32),
            vmem((lay.blocks, lay.block, SEQ), F32),
            vmem((T, S, lay.width), BF16),
            vmem((T, S, lay.width), BF16),
            vmem((S, D), F32),
            vmem((S, D), F32),
            vmem((S, D), F32),
            vmem((S, 1), F32),
            vmem((S, D), BF16),
            vmem((T, S, lay.hidden), BF16),
            vmem((T, S, lay.hidden), BF16),
            vmem((sharers, lay.block, D), BF16),
            vmem((2, SEQ, PAIR), F32),
            vmem((2, SEQ, PAIR), F32),
            vmem((stages, 1, FLAT), F32),
            dma((4,)),
            dma((own,)),
            dma((own,)),
            dma((steps,)),
            dma((steps,)),
            dma((steps,)),
            dma((3 * steps,)),
            dma((3 * steps,)),
            dma((3 * steps,)),
            dma((lay.blocks * lay.span,)),
            dma((2 * lay.units,)),
            dma((2 * lay.units,)),
            dma((sharers,)),
            dma((stages,)),
            dma((stages,)),
        ]
    )
    in_vmem = pl.BlockSpec(memory_space=pltpu.VMEM)
    anywhere = pl.BlockSpec(memory_space=pl.ANY)
    return pl.pallas_call(
        partial(layer_kernel, lay),
        out_shape=(
            jax.ShapeDtypeStruct((S, D), BF16),
            jax.ShapeDtypeStruct((S, D), BF16),
            jax.ShapeDtypeStruct((1, FLAT), F32),
        ),
        in_specs=[in_vmem] * 7 + [anywhere] * 4,
        out_specs=(in_vmem,) * 3,
        scratch_shapes=scratch,
        compiler_params=pltpu.CompilerParams(
            collective_id=0, has_side_effects=True, vmem_limit_bytes=VMEM_BYTES
        ),
        name="layer",
    )(*args)


VMEM_BYTES = 63 * 2**20


def update_kernel(
    raw,
    biases,
    moment_one,
    moment_two,
    left_pairs,
    left_hidden,
    left_small,
    right_bases,
    owners,
    clipped_out,
    norm_out,
    new_out,
    copies_out,
    one_out,
    two_out,
):
    sums = raw[...]
    norm = jnp.sqrt(jnp.sum(sums * sums, keepdims=True))
    norm_out[...] = norm
    clipped = sums * (CLIP_LIMIT / jnp.maximum(norm, CLIP_LIMIT))
    clipped_out[...] = clipped
    dp = lax.axis_index("dp")
    tail = 2 * HEADS + FR
    layout = [(0, 2 * HEADS, left_pairs), (2 * HEADS, FR, left_hidden)]
    layout += [(tail + k * DR, DR, left_small.at[k]) for k in range(4)]
    for k, (begin, amount, left) in enumerate(layout):
        at = pl.ds(begin, amount)
        right = right_bases[k]
        half = lax.dot_general(
            left[...],
            clipped[begin : begin + amount],
            (((0,), (0,)), ((), ())),
            precision=HIGHEST,
            preferred_element_type=F32,
        )
        rotated = jnp.dot(half, right, precision=HIGHEST, preferred_element_type=F32)
        one = BETA_ONE * moment_one[at] + (1.0 - BETA_ONE) * rotated
        two = BETA_TWO * moment_two[at] + (1.0 - BETA_TWO) * rotated * rotated
        direction = (
            one / (1.0 - BETA_ONE**STEP) / (jnp.sqrt(two / (1.0 - BETA_TWO**STEP)) + ADAM_EPS)
        )
        half = jnp.dot(left[...], direction, precision=HIGHEST, preferred_element_type=F32)
        turned = lax.dot_general(
            half,
            right,
            (((1,), (1,)), ((), ())),
            precision=HIGHEST,
            preferred_element_type=F32,
        )
        new = biases[at] - LEARN_RATE * turned
        copies_out[at] = new.astype(BF16)
        mine = owners[k] == dp
        new_out[at] = jnp.where(mine, new, 0.0)
        one_out[at] = jnp.where(mine, one, 0.0)
        two_out[at] = jnp.where(mine, two, 0.0)


def update_call(*args):
    in_vmem = pl.BlockSpec(memory_space=pltpu.VMEM)
    block = jax.ShapeDtypeStruct((BROWS, HD), F32)
    return pl.pallas_call(
        update_kernel,
        out_shape=(
            block,
            jax.ShapeDtypeStruct((1, 1), F32),
            block,
            jax.ShapeDtypeStruct((BROWS, HD), BF16),
            block,
            block,
        ),
        in_specs=[in_vmem] * 8 + [pl.BlockSpec(memory_space=pltpu.SMEM)],
        out_specs=(in_vmem,) * 6,
        name="update",
    )(*args)


def on_device(
    dp_size,
    ranks,
    inputs,
    output_grad,
    input_project,
    output_project,
    expand_weight,
    reduce_weight,
    first_gain,
    second_gain,
    biases,
    first_moment,
    second_moment,
    left_pairs,
    left_hidden,
    left_small,
    right_bases,
    segment_number,
    token_mask,
    owners,
):
    lay = Layout(dp_size, ranks, inputs.shape[0])
    layer_out, input_grad, sums = layer_call(
        lay,
        inputs,
        output_grad,
        first_gain.reshape(1, D),
        second_gain.reshape(1, D),
        biases.reshape(1, FLAT),
        segment_number.reshape(-1, SEQ),
        token_mask.reshape(-1, SEQ),
        input_project,
        output_project,
        expand_weight,
        reduce_weight,
    )
    clipped, clip_norm, new_owned, copies, first_owned, second_owned = update_call(
        sums.reshape(BROWS, HD),
        biases,
        first_moment,
        second_moment,
        left_pairs,
        left_hidden,
        left_small,
        right_bases,
        owners,
    )
    return (
        layer_out,
        input_grad,
        clipped,
        clip_norm.reshape(1),
        new_owned,
        copies,
        first_owned,
        second_owned,
    )


def solution(mesh):
    return jax.shard_map(
        partial(on_device, mesh.shape["dp"], mesh.shape["tensor"]),
        mesh=mesh,
        in_specs=(
            P(("dp", "tensor"), None),
            P(("dp", "tensor"), None),
            P(None, None, "tensor"),
            P("tensor", None),
            P(None, "tensor"),
            P("tensor", None),
            P(),
            P(),
            P(),
            P(),
            P(),
            P(),
            P(),
            P(),
            P(),
            P("dp"),
            P("dp"),
            P(),
        ),
        out_specs=(
            P(("dp", "tensor"), None),
            P(("dp", "tensor"), None),
            P(),
            P(),
            P("dp", None),
            P(),
            P("dp", None),
            P("dp", None),
        ),
        check_vma=False,
    )
```

```python
from functools import partial

import jax
import jax.numpy as jnp
from jax import lax
from jax.experimental import pallas as pl
from jax.experimental.pallas import tpu as pltpu
from jax.sharding import PartitionSpec as P

D = 1024
HEADS = 16
HD = 64
PAIR = 2 * HD
SEQ = 512
STEP = 10
FR = 64
DR = 16
BROWS = 160
AT_QUERY, AT_VALUE, AT_HIDDEN = 0, D, 2 * D
AT_OUT = 2 * D + FR * HD
AT_FIRST, AT_FFN, AT_SECOND = AT_OUT + D, AT_OUT + 2 * D, AT_OUT + 3 * D
FLAT = BROWS * HD

EPS_NORM = 1e-12
CLIP_LIMIT = 64.0
BETA_ONE = 0.9
BETA_TWO = 0.99
ADAM_EPS = 1e-08
LEARN_RATE = 0.2
HIGHEST = lax.Precision.HIGHEST
MESH_ID = pl.DeviceIdType.MESH
BF16 = jnp.bfloat16
F32 = jnp.float32

SUBS = 4
RELAY_LAG, LAG = 2, 4
UNIT = 256
TILE = 256


def nn(a, b):
    return jnp.dot(a, b, preferred_element_type=F32)


def nt(a, b):
    return lax.dot_general(a, b, (((1,), (1,)), ((), ())), preferred_element_type=F32)


def tn(a, b):
    return lax.dot_general(a, b, (((0,), (0,)), ((), ())), preferred_element_type=F32)


def flip(value, bit):
    return value + bit - 2 * bit * ((value // bit) % 2)


class Layout:
    def __init__(self, dp_size, ranks, tokens):
        self.dp_size, self.ranks, self.tokens = dp_size, ranks, tokens
        self.block = 1
        while tokens % (2 * self.block) == 0 and SEQ % (2 * self.block) == 0:
            self.block *= 2
        self.blocks = tokens // self.block
        self.units = SEQ // self.block
        self.width = D // ranks
        self.pairs = self.width // PAIR
        self.hidden = FR * HD // ranks
        rows = ranks * tokens // SEQ
        self.span = 1
        for row in range(rows):
            first = row * self.units // self.blocks
            last = (row * self.units + self.units - 1) // self.blocks
            self.span = max(self.span, last - first + 1)
        self.quads = ranks == 4 and dp_size % 4 == 0


def layer_kernel(
    lay,
    x,
    og,
    gain1,
    gain2,
    biases_t,
    seg,
    val,
    wqkv_in,
    wo_in,
    w1_in,
    w2_in,
    out_hbm,
    ig_hbm,
    bsum,
    brow,
    out,
    ig,
    wqkv,
    wo_b,
    w1_b,
    w2_b,
    xkv,
    qbuf,
    kbuf,
    vbuf,
    pbuf,
    linv,
    mask,
    ctx,
    cgrad,
    abuf,
    bbuf,
    cbuf,
    r1buf,
    low,
    hid,
    gp,
    back,
    dka,
    dva,
    group_early,
    group_late,
    all_early,
    all_late,
    sem_local,
    sem_out,
    sem_own_s,
    sem_own_r,
    sem_y,
    sem_x,
    sem_z,
    sem_c,
    sem_w,
    sem_p,
    sem_hs,
    sem_hr,
    sem_gs,
    sem_gr,
    sem_as,
    sem_ar,
    sem_bs,
    sem_br,
):
    T, S, B, NB, NU = lay.ranks, lay.tokens, lay.block, lay.blocks, lay.units
    W, PP, F = lay.width, lay.pairs, lay.hidden
    dp = lax.axis_index("dp")
    t = lax.axis_index("tensor")
    quads = lay.quads

    def rank(o):
        r = (t + o) % 2
        if T > 2:
            r = r + 2 * ((t // 2 + o // 2) % 2)
        if T > 4:
            r = r + 4 * ((t // 4 + o // 4) % 2)
        return r

    if quads:
        big = wo_b

        def wo(r):
            return big.at[r, pl.ds(0, W)]

        def w1(r):
            return big.at[r, pl.ds(W, D)]

        def w2(r):
            return big.at[r, pl.ds(W + D, F)]
    else:

        def wo(r):
            return wo_b.at[r]

        def w1(r):
            return w1_b.at[r]

        def w2(r):
            return w2_b.at[r]

    def pieces(r):
        return [wqkv.at[r], wo(r), w1(r), w2(r)]

    sources = [wqkv_in, wo_in, w1_in, w2_in]

    def peer(o):
        return (dp, rank(o))

    def remote(src, dst, send, recv, device):
        return pltpu.make_async_remote_copy(
            src_ref=src,
            dst_ref=dst,
            send_sem=send,
            recv_sem=recv,
            device_id=device,
            device_id_type=MESH_ID,
        )

    barrier = pltpu.get_barrier_semaphore()
    others = [peer(o) for o in range(1, T)]
    others += [((dp + o) % lay.dp_size, t) for o in range(1, lay.dp_size)]
    for device in others:
        pl.semaphore_signal(barrier, inc=1, device_id=device, device_id_type=MESH_ID)
    local = [
        pltpu.make_async_copy(src, dst, sem_local.at[i])
        for i, (src, dst) in enumerate(zip(sources, pieces(t)))
    ]
    for copy in local:
        copy.start()

    row0 = (NB * t) // NU
    has_b = (NB * t + NB - 1) // NU != row0

    def place(j):
        u = NB * t + j
        row = u // NU
        return u, row, row - row0, u - row * NU

    def rows_at(w):
        return pl.ds(pl.multiple_of(w * B, B), B)

    def block_at(j):
        return pl.ds(j * B, B)

    key_at = lax.broadcasted_iota(jnp.int32, (B, SEQ), 1)
    query_at = lax.broadcasted_iota(jnp.int32, (B, SEQ), 0)
    for j in range(NB):
        u, row, slot, w = place(j)
        keys_here = pl.ds(pl.multiple_of(row * SEQ, SEQ), SEQ)
        numbers = seg[:, keys_here].astype(F32)
        keyed = jnp.where(val[:, keys_here] == 1, numbers, -1.0)
        same = key_at == query_at + w * B
        own = jnp.sum(jnp.where(same, numbers, 0.0), axis=1, keepdims=True)
        mask[j] = jnp.where((own == keyed) | same, 0.0, -1e30)
        xkv[slot, rows_at(w)] = x[block_at(j)]

    bias_rows = biases_t[...].T
    for i in range(BROWS):
        brow[:, i * HD : (i + 1) * HD] = bias_rows[i : i + 1]

    pl.semaphore_wait(barrier, len(others))

    def send_rows():
        for j in range(NB):
            u, row, slot, w = place(j)
            first = row * NU // NB
            last = (row * NU + NU - 1) // NB
            for o in range(lay.span):
                dest = first + o

                @pl.when((dest <= last) & (dest != t))
                def _():
                    remote(
                        x.at[block_at(j)],
                        xkv.at[row - (NB * dest) // NU, rows_at(w)],
                        sem_hs.at[j * lay.span + o],
                        sem_hr.at[(row - (NB * dest) // NU) * NU + w],
                        (dp, dest),
                    ).start()

    if quads:
        role = dp % 4
        relay = role == 3
        gy = role % 3
        gx = jnp.where(role == 1, 0, jnp.where(role == 3, 2, 1))
        gz = jnp.where(role == 2, 0, jnp.where(role == 3, 1, 2))
        far = rank(2)
        core, ynext = (dp, rank(1)), (dp, rank(2))
        xnext, znext = (flip(dp, 1), t), (flip(dp, 2), t)
        rounds = 4
        steps = rounds * SUBS
        part_a, part_b = D // SUBS, UNIT // SUBS

        def chunk(idx, g, fn):
            n = (idx // SUBS * 3 + g) * SUBS + idx % SUBS

            @pl.when((idx >= 0) & (idx < SUBS))
            def _():
                at = pl.ds(pl.multiple_of(idx * part_a, part_a), part_a)
                fn(lambda r: wqkv.at[r, g, at], n)

            @pl.when((idx >= SUBS) & (idx < steps))
            def _():
                row = ((idx // SUBS - 1) * 3 + g) * UNIT + (idx % SUBS) * part_b
                at = pl.ds(pl.multiple_of(row, part_b), part_b)
                fn(lambda r: big.at[r, at], n)

        def send_y(idx):
            def go(view, n):
                remote(view(t), view(t), sem_y.at[idx], sem_w.at[n], ynext).start()

            chunk(idx, gy, go)

        def to_core(view, n):
            remote(view(far), view(far), sem_c.at[n], sem_p.at[n], core).start()

        def arrived(view, n):
            remote(view(far), view(far), sem_c.at[n], sem_w.at[n], core).wait_recv()

        def to_x(view, n, idx):
            remote(view(far), view(far), sem_x.at[idx], sem_w.at[n], xnext).start()

        def to_z(view, n, idx):
            remote(view(far), view(far), sem_z.at[idx], sem_w.at[n], znext).start()

        def service(s, carry):
            def from_y(view, n):
                arrived(view, n)

                @pl.when(role != 3)
                def _():
                    to_x(view, n, s)
                    to_z(view, n, s)

                to_core(view, n)

            chunk(s, gy, from_y)
            send_y(s + SUBS)
            late = s - jnp.where(relay, RELAY_LAG, LAG)

            def from_x(view, n):
                arrived(view, n)

                @pl.when(relay)
                def _():
                    to_z(view, n, late)

                to_core(view, n)

            def from_z(view, n):
                arrived(view, n)

                @pl.when(relay)
                def _():
                    to_x(view, n, late)

                to_core(view, n)

            chunk(late, gx, from_x)
            chunk(late, gz, from_z)
            return carry

        def sent(idx, carry):
            def go(view, n):
                remote(view(t), view(t), sem_y.at[idx], sem_w.at[n], ynext).wait_send()
                remote(view(t), view(t), sem_x.at[idx], sem_w.at[n], xnext).wait_send()
                remote(view(t), view(t), sem_z.at[idx], sem_w.at[n], znext).wait_send()
                for g in range(3):
                    m = (idx // SUBS * 3 + g) * SUBS + idx % SUBS
                    remote(view(t), view(t), sem_c.at[m], sem_p.at[m], core).wait_send()

            chunk(idx, gy, go)
            return carry

        def from_partner(unit_low, unit_high):
            def go(n, carry):
                @pl.when(n < 3 * SUBS)
                def _():
                    view = wqkv.at[rank(3), 0, pl.ds(0, part_a)]
                    remote(view, view, sem_c.at[n], sem_p.at[n], core).wait_recv()

                @pl.when(n >= 3 * SUBS)
                def _():
                    view = big.at[rank(3), pl.ds(0, part_b)]
                    remote(view, view, sem_c.at[n], sem_p.at[n], core).wait_recv()

                return carry

            lax.fori_loop(unit_low * SUBS, unit_high * SUBS, go, 0)

        def own_copies(i):
            return remote(sources[i], pieces(t)[i], sem_own_s.at[i], sem_own_r.at[i], core)

        local[0].wait()
        lax.fori_loop(0, 2, lambda i, c: (send_y(i), c)[1], 0)
        send_rows()
        lax.fori_loop(2, SUBS, lambda i, c: (send_y(i), c)[1], 0)
        for i in range(4):
            own_copies(i).start()
        for i in range(1, 4):
            local[i].wait()

        first_unit = [0, 3, 4, 8, 12]

        def ready(i, o):
            @pl.when(o == 1)
            def _():
                remote(
                    sources[i], pieces(rank(1))[i], sem_own_s.at[i], sem_own_r.at[i], core
                ).wait_recv()

            @pl.when(o == 3)
            def _():
                from_partner(first_unit[i], first_unit[i + 1])

    else:

        def own_copies(i, o):
            n = i * T + o
            return remote(sources[i], pieces(t)[i], sem_own_s.at[n], sem_own_r.at[n], peer(o))

        send_rows()
        for i in range(4):
            for o in range(1, T):
                own_copies(i, o).start()

        def ready(i, o):
            @pl.when(o == 0)
            def _():
                local[i].wait()

            @pl.when(o != 0)
            def _():
                n = i * T + o
                remote(
                    sources[i], pieces(rank(o))[i], sem_own_s.at[n], sem_own_r.at[n], peer(o)
                ).wait_recv()

    head_lane = lax.broadcasted_iota(jnp.int32, (B, PAIR), 1) < HD

    def split_heads(values):
        nought = jnp.zeros_like(values)
        return jnp.concatenate(
            [jnp.where(head_lane, values, nought), jnp.where(head_lane, nought, values)], axis=0
        )

    def join_heads(values):
        return jnp.where(head_lane, values[:B], values[B:])

    ones = jnp.ones((SEQ, PAIR), BF16)

    slot_first = jnp.where(has_b & (t % 4 == 2), 1, 0)

    def project_query(r):
        bias = brow[:, pl.ds(pl.multiple_of(AT_QUERY + r * W, PAIR), W)]
        query = ((nn(x[...], wqkv[r, 0]) + bias) * HD**-0.5).astype(BF16)
        for i in range(PP):
            qbuf[r * PP + i] = query[:, i * PAIR : (i + 1) * PAIR]

    def project_keys(o, r):
        bias = brow[:, pl.ds(pl.multiple_of(AT_VALUE + r * W, PAIR), W)]

        def body(turn, carry):
            slot = (slot_first + turn) % 2

            @pl.when((slot == 0) | has_b)
            def _():
                for w in range(NU):
                    owner = ((row0 + slot) * NU + w) // NB

                    @pl.when((owner != t) & (o == 0))
                    def _():
                        remote(
                            x.at[block_at(0)],
                            xkv.at[slot, rows_at(w)],
                            sem_hs.at[0],
                            sem_hr.at[slot * NU + w],
                            (dp, owner),
                        ).wait_recv()

                rows = xkv[slot]
                keys = nn(rows, wqkv[r, 1]).astype(BF16)
                values = (nn(rows, wqkv[r, 2]) + bias).astype(BF16)
                for i in range(PP):
                    kbuf[r * PP + i, slot] = keys[:, i * PAIR : (i + 1) * PAIR]
                    vbuf[r * PP + i, slot] = values[:, i * PAIR : (i + 1) * PAIR]

            return carry

        lax.fori_loop(0, 2, body, 0)

    def attend(r, i):
        hp = r * PP + i
        for j in range(NB):
            u, row, slot, w = place(j)
            query = split_heads(qbuf[hp, block_at(j)])
            hide = mask[j]
            scores = nt(query, kbuf[hp, slot]) + jnp.concatenate([hide, hide], axis=0)
            peak = jnp.max(scores, axis=1, keepdims=True)
            probs = jnp.exp(scores - peak).astype(BF16)
            pbuf[hp, j] = probs
            mixed = nn(probs, jnp.concatenate([vbuf[hp, slot], ones], axis=1))
            inverse = 1.0 / join_heads(mixed[:, PAIR:])
            linv[hp, block_at(j)] = inverse
            ctx[r, block_at(j), pl.ds(i * PAIR, PAIR)] = (
                join_heads(mixed[:, :PAIR]) * inverse
            ).astype(BF16)

    def project(o):
        ready(0, o)
        r = rank(o)
        project_query(r)
        project_keys(o, r)

    def attend_rank(o):
        for i in range(PP):
            attend(rank(o), i)

    def row_mean(values):
        return jnp.mean(values, axis=1, keepdims=True)

    def row_tiles(body, carry):
        for j in range(NB):
            carry = body(block_at(j), carry)
        return carry

    def norm_first(at, carry):
        values = abuf[at]
        centred = values - row_mean(values)
        root = lax.rsqrt(row_mean(centred * centred) + EPS_NORM)
        normed = centred * root
        r1buf[at] = root
        abuf[at] = normed
        first_normed = normed * gain1[...] + brow[:, AT_FIRST : AT_FIRST + D]
        low[at] = first_normed.astype(BF16)
        bbuf[at] = first_normed + brow[:, AT_FFN : AT_FFN + D]
        return carry

    def finish_attention():
        for o in range(T):
            ready(1, o)
        for n in range(0, D, TILE):
            total = nn(ctx[0], wo(0)[:, n : n + TILE])
            for r in range(1, T):
                total = total + nn(ctx[r], wo(r)[:, n : n + TILE])
            at = pl.ds(n, TILE)
            abuf[:, at] = x[:, at].astype(F32) + total + brow[:, AT_OUT + n : AT_OUT + n + TILE]
        row_tiles(norm_first, 0)

    def expand(o):
        ready(2, o)
        r = rank(o)
        for n in range(0, F, TILE):
            bias = brow[:, pl.ds(pl.multiple_of(AT_HIDDEN + r * F + n, PAIR), TILE)]
            pre = nn(low[...], w1(r)[:, n : n + TILE]) + bias
            cdf = 0.5 * (1.0 + lax.erf(pre * 0.5**0.5))
            density = jnp.exp(-0.5 * pre * pre) * 0.3989422804014327
            hid[r, :, pl.ds(n, TILE)] = (pre * cdf).astype(BF16)
            gp[r, :, pl.ds(n, TILE)] = (cdf + pre * density).astype(BF16)

    def reduce(o):
        ready(3, o)
        r = rank(o)
        for n in range(0, D, TILE):
            at = pl.ds(n, TILE)
            bbuf[:, at] = bbuf[:, at] + nn(hid[r], w2(r)[:, n : n + TILE])

    if quads:
        whole = [(k + 1) * SUBS + LAG - 1 for k in range(rounds)]
        mid = SUBS // 2
        plan = [
            (project, [PLAN[0], PLAN[1], whole[0], whole[0] + 2]),
            (attend_rank, [PLAN[2], PLAN[3], whole[0] + 1, whole[0] + 3]),
            (expand, [whole[1] + 1, whole[1] + 2, whole[2], whole[2] + 1]),
            (reduce, [whole[1] + 3, whole[1] + 4, whole[3], whole[3]]),
        ]

        def step(s, carry):
            service(s, 0)

            @pl.when(s == whole[1])
            def _():
                finish_attention()

            for part, at_steps in plan:
                o = jnp.int32(-1)
                for k, at_step in enumerate(at_steps):
                    if at_step < whole[3]:
                        o = jnp.where(s == at_step, k, o)

                @pl.when(o >= 0)
                def _():
                    part(o)

            return carry

        lax.fori_loop(0, whole[3] + 1, step, 0)
        lax.fori_loop(2, T, lambda o, c: (reduce(o), c)[1], 0)
    else:

        def each_rank(part):
            lax.fori_loop(0, T, lambda o, c: (part(o), c)[1], 0)

        each_rank(project)
        each_rank(attend_rank)
        finish_attention()
        each_rank(expand)
        each_rank(reduce)

    nought_row = jnp.zeros((1, D), F32)

    def norm_second(at, carry):
        sum_up, sum_second = carry
        values = bbuf[at]
        centred = values - row_mean(values)
        root = lax.rsqrt(row_mean(centred * centred) + EPS_NORM)
        normed = centred * root
        out[at] = (normed * gain2[...] + brow[:, AT_SECOND : AT_SECOND + D]).astype(BF16)
        upstream = og[at].astype(F32)
        weighted = upstream * gain2[...]
        grad = root * (weighted - row_mean(weighted) - normed * row_mean(weighted * normed))
        bbuf[at] = grad
        low[at] = grad.astype(BF16)
        return (
            sum_up + jnp.sum(upstream, axis=0, keepdims=True),
            sum_second + jnp.sum(grad, axis=0, keepdims=True),
        )

    sum_up, sum_second = row_tiles(norm_second, (nought_row, nought_row))
    out_copy = pltpu.make_async_copy(out, out_hbm, sem_out.at[0])
    out_copy.start()
    bsum[:, AT_SECOND : AT_SECOND + D] = sum_up
    bsum[:, AT_FFN : AT_FFN + D] = sum_second

    def ffn_back(r, carry):
        for n in range(0, F, TILE):
            grad = nt(low[...], w2(r)[n : n + TILE, :]) * gp[r, :, pl.ds(n, TILE)].astype(F32)
            at = pl.ds(pl.multiple_of(AT_HIDDEN + r * F + n, PAIR), TILE)
            bsum[:, at] = jnp.sum(grad, axis=0, keepdims=True)
            hid[r, :, pl.ds(n, TILE)] = grad.astype(BF16)
        return carry

    lax.fori_loop(0, T, ffn_back, 0)
    for n in range(0, D, TILE):
        total = nt(hid[0], w1(0)[n : n + TILE, :])
        for r in range(1, T):
            total = total + nt(hid[r], w1(r)[n : n + TILE, :])
        cbuf[:, pl.ds(n, TILE)] = total

    def first_back(at, carry):
        sum_normed, sum_first = carry
        grad = bbuf[at] + cbuf[at]
        normed = abuf[at]
        weighted = grad * gain1[...]
        first = r1buf[at] * (
            weighted - row_mean(weighted) - normed * row_mean(weighted * normed)
        )
        bbuf[at] = first
        low[at] = first.astype(BF16)
        return (
            sum_normed + jnp.sum(grad, axis=0, keepdims=True),
            sum_first + jnp.sum(first, axis=0, keepdims=True),
        )

    sum_normed, sum_first = row_tiles(first_back, (nought_row, nought_row))
    bsum[:, AT_FIRST : AT_FIRST + D] = sum_normed
    bsum[:, AT_OUT : AT_OUT + D] = sum_first

    class Totals:
        def __init__(self, number, start, amount, group, everyone):
            self.number, self.at = number, pl.ds(start, amount)
            self.group, self.everyone = group, everyone

        def copies(self, buffer, sems, me, peers):
            send, recv = sems
            return [
                remote(
                    buffer.at[me],
                    buffer.at[me],
                    send.at[self.number, k],
                    recv.at[self.number, me],
                    device,
                )
                for k, device in enumerate(peers)
            ]

        def gather(self, buffer, sems, me, peers):
            for copy in self.copies(buffer, sems, me, peers):
                copy.wait_send()
            for k in range(buffer.shape[0]):

                @pl.when(k != me)
                def _():
                    remote(
                        buffer.at[k], buffer.at[k], sems[0].at[0, 0], sems[1].at[self.number, k], peers[0]
                    ).wait_recv()

            total = buffer[0]
            for k in range(1, buffer.shape[0]):
                total = total + buffer[k]
            return total

        def start(self):
            self.group[t] = bsum[:, self.at]
            for copy in self.copies(self.group, (sem_as, sem_ar), t, in_group):
                copy.start()

        def middle(self):
            self.everyone[dp] = self.gather(self.group, (sem_as, sem_ar), t, in_group)
            for copy in self.copies(self.everyone, (sem_bs, sem_br), dp, in_dp):
                copy.start()

        def finish(self):
            bsum[:, self.at] = self.gather(self.everyone, (sem_bs, sem_br), dp, in_dp)

    in_group = [peer(o) for o in range(1, T)]
    in_dp = [((dp + o) % lay.dp_size, t) for o in range(1, lay.dp_size)]
    early = Totals(0, AT_HIDDEN, FLAT - AT_HIDDEN, group_early, all_early)
    late = Totals(1, AT_QUERY, AT_HIDDEN, group_late, all_late)
    early.start()

    for r in range(T):
        cgrad[r] = nt(low[...], wo(r)[...]).astype(BF16)

    def attend_back(r, i):
        hp = r * PP + i
        dka[...] = jnp.zeros_like(dka)
        dva[...] = jnp.zeros_like(dva)
        query_sum = jnp.zeros((1, PAIR), F32)
        for j in range(NB):
            u, row, slot, w = place(j)
            lanes = pl.ds(i * PAIR, PAIR)
            scaled = cgrad[r, block_at(j), lanes].astype(F32) * linv[hp, block_at(j)]
            upstream = split_heads(scaled.astype(BF16))
            delta = jnp.sum(
                split_heads(scaled * ctx[r, block_at(j), lanes].astype(F32)), axis=1, keepdims=True
            )
            probs = pbuf[hp, j]
            query = split_heads(qbuf[hp, block_at(j)])
            score = (probs.astype(F32) * (nt(upstream, vbuf[hp, slot]) - delta)).astype(BF16)
            dva[slot] += tn(probs, upstream)
            dka[slot] += tn(score, query)
            grad = join_heads(nn(score, kbuf[hp, slot])) * HD**-0.5
            qbuf[hp, block_at(j)] = grad.astype(BF16)
            query_sum = query_sum + jnp.sum(grad, axis=0, keepdims=True)
        value_sum = jnp.zeros((1, PAIR), F32)
        for slot in range(2):
            kbuf[hp, slot] = dka[slot].astype(BF16)
            vbuf[hp, slot] = dva[slot].astype(BF16)
            value_sum = value_sum + jnp.sum(dva[slot], axis=0, keepdims=True)
        lanes = pl.multiple_of(r * W + i * PAIR, PAIR)
        bsum[:, pl.ds(AT_QUERY + lanes, PAIR)] = query_sum
        bsum[:, pl.ds(AT_VALUE + lanes, PAIR)] = value_sum

    def rank_back(r, carry):
        for i in range(PP):
            attend_back(r, i)

        @pl.when(r == T // 2 - 1)
        def _():
            early.middle()

        return carry

    lax.fori_loop(0, T, rank_back, 0)
    late.start()

    def wide(buffer, r, *at):
        return jnp.concatenate([buffer[(r * PP + i, *at)] for i in range(PP)], axis=1)

    def shares(slot):
        def body(k, carry):
            at = pl.ds(pl.multiple_of(k * TILE, TILE), TILE)
            total = nt(wide(kbuf, 0, slot), wqkv[0, 1, at])
            total = total + nt(wide(vbuf, 0, slot), wqkv[0, 2, at])
            for r in range(1, T):
                total = total + nt(wide(kbuf, r, slot), wqkv[r, 1, at])
                total = total + nt(wide(vbuf, r, slot), wqkv[r, 2, at])
            xkv[slot, :, at] = total.astype(BF16)
            return carry

        lax.fori_loop(0, D // TILE, body, 0)

    def share_copy(slot, w):
        u = (row0 + slot) * NU + w
        owner = u // NB
        first = (row0 + slot) * NU // NB
        place_of = t - first - jnp.where(t > owner, 1, 0)
        number = (u - owner * NB) * (lay.span - 1) + place_of
        return remote(
            xkv.at[slot, rows_at(w)],
            back.at[number],
            sem_gs.at[slot * NU + w],
            sem_gr.at[number],
            (dp, owner),
        )

    def send_shares(turn, carry):
        slot = (1 - slot_first + turn) % 2

        @pl.when((slot == 0) | has_b)
        def _():
            shares(slot)
            for w in range(NU):
                owner = ((row0 + slot) * NU + w) // NB

                @pl.when(owner != t)
                def _():
                    share_copy(slot, w).start()

        return carry

    lax.fori_loop(0, 2, send_shares, 0)
    late.middle()
    early.finish()

    for n in range(0, D, TILE):
        total = nt(wide(qbuf, 0), wqkv[0, 0, pl.ds(n, TILE)])
        for r in range(1, T):
            total = total + nt(wide(qbuf, r), wqkv[r, 0, pl.ds(n, TILE)])
        at = pl.ds(n, TILE)
        bbuf[:, at] = bbuf[:, at] + total

    for j in range(NB):
        u, row, slot, w = place(j)
        first = row * NU // NB
        last = (row * NU + NU - 1) // NB
        bbuf[block_at(j)] = bbuf[block_at(j)] + xkv[slot, rows_at(w)].astype(F32)
        for o in range(lay.span - 1):
            number = j * (lay.span - 1) + o

            @pl.when(first + o < last)
            def _():
                sender = first + o + jnp.where(first + o >= t, 1, 0)
                remote(
                    xkv.at[0, rows_at(0)],
                    back.at[number],
                    sem_gs.at[0],
                    sem_gr.at[number],
                    (dp, sender),
                ).wait_recv()
                bbuf[block_at(j)] = bbuf[block_at(j)] + back[number].astype(F32)

        ig[block_at(j)] = bbuf[block_at(j)].astype(BF16)

    ig_copy = pltpu.make_async_copy(ig, ig_hbm, sem_out.at[1])
    ig_copy.start()
    late.finish()

    out_copy.wait()
    ig_copy.wait()
    for slot in range(2):
        for w in range(NU):
            owner = ((row0 + slot) * NU + w) // NB

            @pl.when((owner != t) & ((slot == 0) | has_b))
            def _():
                share_copy(slot, w).wait_send()

    for j in range(NB):
        u, row, slot, w = place(j)
        first = row * NU // NB
        last = (row * NU + NU - 1) // NB
        for o in range(lay.span):
            dest = first + o

            @pl.when((dest <= last) & (dest != t))
            def _():
                remote(
                    x.at[block_at(j)],
                    xkv.at[0, rows_at(0)],
                    sem_hs.at[j * lay.span + o],
                    sem_hr.at[0],
                    (dp, dest),
                ).wait_send()

    if quads:
        for i in range(4):
            own_copies(i).wait_send()
        lax.fori_loop(0, steps, sent, 0)
    else:
        for i in range(4):
            for o in range(1, T):
                own_copies(i, o).wait_send()


def layer_call(lay, *args):
    T, S = lay.ranks, lay.tokens
    hp = HEADS // 2
    vmem = pltpu.VMEM
    if lay.quads:
        wide = [
            vmem((T, lay.width + D + lay.hidden, D), BF16),
            vmem((16, PAIR), BF16),
            vmem((16, PAIR), BF16),
        ]
    else:
        wide = [
            vmem((T, lay.width, D), BF16),
            vmem((T, D, lay.hidden), BF16),
            vmem((T, lay.hidden, D), BF16),
        ]
    dma = pltpu.SemaphoreType.DMA
    steps = 4 * SUBS
    own = 4 if lay.quads else 4 * T
    sharers = lay.blocks * max(lay.span - 1, 1)
    scratch = (
        [vmem((1, FLAT), F32), vmem((S, D), BF16), vmem((S, D), BF16)]
        + [vmem((T, 3, D, lay.width), BF16)]
        + wide
        + [
            vmem((2, SEQ, D), BF16),
            vmem((hp, S, PAIR), BF16),
            vmem((hp, 2, SEQ, PAIR), BF16),
            vmem((hp, 2, SEQ, PAIR), BF16),
            vmem((hp, lay.blocks, 2 * lay.block, SEQ), BF16),
            vmem((hp, S, PAIR), F32),
            vmem((lay.blocks, lay.block, SEQ), F32),
            vmem((T, S, lay.width), BF16),
            vmem((T, S, lay.width), BF16),
            vmem((S, D), F32),
            vmem((S, D), F32),
            vmem((S, D), F32),
            vmem((S, 1), F32),
            vmem((S, D), BF16),
            vmem((T, S, lay.hidden), BF16),
            vmem((T, S, lay.hidden), BF16),
            vmem((sharers, lay.block, D), BF16),
            vmem((2, SEQ, PAIR), F32),
            vmem((2, SEQ, PAIR), F32),
            vmem((T, 1, FLAT - AT_HIDDEN), F32),
            vmem((T, 1, AT_HIDDEN), F32),
            vmem((lay.dp_size, 1, FLAT - AT_HIDDEN), F32),
            vmem((lay.dp_size, 1, AT_HIDDEN), F32),
            dma((4,)),
            dma((2,)),
            dma((own,)),
            dma((own,)),
            dma((steps,)),
            dma((steps,)),
            dma((steps,)),
            dma((3 * steps,)),
            dma((3 * steps,)),
            dma((3 * steps,)),
            dma((lay.blocks * lay.span,)),
            dma((2 * lay.units,)),
            dma((2 * lay.units,)),
            dma((sharers,)),
            dma((2, T)),
            dma((2, T)),
            dma((2, lay.dp_size)),
            dma((2, lay.dp_size)),
        ]
    )
    in_vmem = pl.BlockSpec(memory_space=pltpu.VMEM)
    anywhere = pl.BlockSpec(memory_space=pl.ANY)
    return pl.pallas_call(
        partial(layer_kernel, lay),
        out_shape=(
            jax.ShapeDtypeStruct((S, D), BF16),
            jax.ShapeDtypeStruct((S, D), BF16),
            jax.ShapeDtypeStruct((1, FLAT), F32),
        ),
        in_specs=[in_vmem] * 7 + [anywhere] * 4,
        out_specs=(anywhere, anywhere, in_vmem),
        scratch_shapes=scratch,
        compiler_params=pltpu.CompilerParams(
            collective_id=0, has_side_effects=True, vmem_limit_bytes=VMEM_BYTES
        ),
        name="layer",
    )(*args)


VMEM_BYTES = 63 * 2**20
PLAN = [2, 5, 3, 6]


def update_kernel(
    raw,
    biases,
    moment_one,
    moment_two,
    left_pairs,
    left_hidden,
    left_small,
    right_bases,
    owners,
    out_in,
    ig_in,
    clipped_out,
    norm_out,
    new_out,
    copies_out,
    one_out,
    two_out,
    out_out,
    ig_out,
    rows,
    left,
    wide,
    sems,
):
    fetches = [
        pltpu.make_async_copy(src, wide.at[i], sems.at[i]) for i, src in enumerate((out_in, ig_in))
    ]
    stores = [
        pltpu.make_async_copy(wide.at[i], dst, sems.at[2 + i])
        for i, dst in enumerate((out_out, ig_out))
    ]
    for fetch in fetches:
        fetch.start()
    sums = raw[...]
    norm = jnp.sqrt(jnp.sum(sums * sums, keepdims=True))
    norm_out[...] = norm
    for i in range(BROWS):
        rows[i : i + 1] = sums[:, i * HD : (i + 1) * HD]
    clipped = rows[...].T * (CLIP_LIMIT / jnp.maximum(norm, CLIP_LIMIT))
    clipped_out[...] = clipped
    dp = lax.axis_index("dp")
    tail = 2 * HEADS + FR
    layout = [(0, 2 * HEADS, left_pairs), (2 * HEADS, FR, left_hidden)]
    layout += [(tail + k * DR, DR, left_small.at[k]) for k in range(4)]
    left[...] = jnp.zeros_like(left)
    for begin, amount, basis in layout:
        left[begin : begin + amount, begin : begin + amount] = basis[...]
    column = lax.broadcasted_iota(jnp.int32, (HD, BROWS), 1)

    def per_matrix(choose):
        result = choose(0)
        for k in range(1, len(layout)):
            result = jnp.where(column >= layout[k][0], choose(k), result)
        return result

    def product(a, b, over_a, over_b):
        return lax.dot_general(
            a,
            b,
            (((over_a,), (over_b,)), ((), ())),
            precision=HIGHEST,
            preferred_element_type=F32,
        )

    for fetch, store in zip(fetches, stores):
        fetch.wait()
        store.start()
    half = product(clipped, left[...], 1, 0)
    rotated = per_matrix(lambda k: product(right_bases[k], half, 0, 0))
    one = BETA_ONE * moment_one[...] + (1.0 - BETA_ONE) * rotated
    two = BETA_TWO * moment_two[...] + (1.0 - BETA_TWO) * rotated * rotated
    direction = (
        one / (1.0 - BETA_ONE**STEP) / (jnp.sqrt(two / (1.0 - BETA_TWO**STEP)) + ADAM_EPS)
    )
    half = per_matrix(lambda k: product(right_bases[k], direction, 1, 0))
    new = biases[...] - LEARN_RATE * product(half, left[...], 1, 1)
    copies_out[...] = new.astype(BF16)
    mine = per_matrix(lambda k: jnp.where(owners[k] == dp, 1.0, 0.0)) > 0.5
    new_out[...] = jnp.where(mine, new, 0.0)
    one_out[...] = jnp.where(mine, one, 0.0)
    two_out[...] = jnp.where(mine, two, 0.0)
    for store in stores:
        store.wait()


def update_call(tokens, *args):
    in_vmem = pl.BlockSpec(memory_space=pltpu.VMEM)
    anywhere = pl.BlockSpec(memory_space=pl.ANY)
    block = jax.ShapeDtypeStruct((HD, BROWS), F32)
    wide = jax.ShapeDtypeStruct((tokens, D), BF16)
    return pl.pallas_call(
        update_kernel,
        out_shape=(
            block,
            jax.ShapeDtypeStruct((1, 1), F32),
            block,
            jax.ShapeDtypeStruct((HD, BROWS), BF16),
            block,
            block,
            wide,
            wide,
        ),
        in_specs=[in_vmem] * 8 + [pl.BlockSpec(memory_space=pltpu.SMEM)] + [anywhere] * 2,
        out_specs=(in_vmem,) * 6 + (anywhere,) * 2,
        scratch_shapes=[
            pltpu.VMEM((BROWS, HD), F32),
            pltpu.VMEM((BROWS, BROWS), F32),
            pltpu.VMEM((2, tokens, D), BF16),
            pltpu.SemaphoreType.DMA((4,)),
        ],
        name="update",
    )(*args)


def on_device(
    dp_size,
    ranks,
    inputs,
    output_grad,
    input_project,
    output_project,
    expand_weight,
    reduce_weight,
    first_gain,
    second_gain,
    biases,
    first_moment,
    second_moment,
    left_pairs,
    left_hidden,
    left_small,
    right_bases,
    segment_number,
    token_mask,
    owners,
):
    lay = Layout(dp_size, ranks, inputs.shape[0])
    layer_out, input_grad, sums = layer_call(
        lay,
        inputs,
        output_grad,
        first_gain.reshape(1, D),
        second_gain.reshape(1, D),
        biases.T,
        segment_number.reshape(1, -1),
        token_mask.reshape(1, -1),
        input_project,
        output_project,
        expand_weight,
        reduce_weight,
    )
    clipped, clip_norm, new_owned, copies, first_owned, second_owned, layer_out, input_grad = (
        update_call(
            inputs.shape[0],
            sums,
            biases.T,
            first_moment.T,
            second_moment.T,
            left_pairs,
            left_hidden,
            left_small,
            right_bases,
            owners,
            layer_out,
            input_grad,
        )
    )
    return (
        layer_out,
        input_grad,
        clipped.T,
        clip_norm.reshape(1),
        new_owned.T,
        copies.T,
        first_owned.T,
        second_owned.T,
    )


def solution(mesh):
    return jax.shard_map(
        partial(on_device, mesh.shape["dp"], mesh.shape["tensor"]),
        mesh=mesh,
        in_specs=(
            P(("dp", "tensor"), None),
            P(("dp", "tensor"), None),
            P(None, None, "tensor"),
            P("tensor", None),
            P(None, "tensor"),
            P("tensor", None),
            P(),
            P(),
            P(),
            P(),
            P(),
            P(),
            P(),
            P(),
            P(),
            P("dp"),
            P("dp"),
            P(),
        ),
        out_specs=(
            P(("dp", "tensor"), None),
            P(("dp", "tensor"), None),
            P(),
            P(),
            P("dp", None),
            P(),
            P("dp", None),
            P("dp", None),
        ),
        check_vma=False,
    )
```

```python
from functools import partial

import jax
import jax.numpy as jnp
from jax import lax
from jax.experimental import pallas as pl
from jax.experimental.pallas import tpu as pltpu
from jax.sharding import PartitionSpec as P

D = 1024
HEADS = 16
HD = 64
PAIR = 2 * HD
SEQ = 512
STEP = 10
FR = 64
DR = 16
BROWS = 160
AT_QUERY, AT_VALUE, AT_HIDDEN = 0, D, 2 * D
AT_OUT = 2 * D + FR * HD
AT_FIRST, AT_FFN, AT_SECOND = AT_OUT + D, AT_OUT + 2 * D, AT_OUT + 3 * D
FLAT = BROWS * HD

EPS_NORM = 1e-12
CLIP_LIMIT = 64.0
BETA_ONE = 0.9
BETA_TWO = 0.99
ADAM_EPS = 1e-08
LEARN_RATE = 0.2
HIGHEST = lax.Precision.HIGHEST
MESH_ID = pl.DeviceIdType.MESH
BF16 = jnp.bfloat16
F32 = jnp.float32

SUBS = 4
LAST_SUBS = 4
RELAY_LAG, LAG = 2, 4
UNIT = 256
TILE = 256


def nn(a, b):
    return jnp.dot(a, b, preferred_element_type=F32)


def nt(a, b):
    return lax.dot_general(a, b, (((1,), (1,)), ((), ())), preferred_element_type=F32)


def tn(a, b):
    return lax.dot_general(a, b, (((0,), (0,)), ((), ())), preferred_element_type=F32)


def flip(value, bit):
    return value + bit - 2 * bit * ((value // bit) % 2)


class Layout:
    def __init__(self, dp_size, ranks, tokens):
        self.dp_size, self.ranks, self.tokens = dp_size, ranks, tokens
        self.block = 1
        while tokens % (2 * self.block) == 0 and SEQ % (2 * self.block) == 0:
            self.block *= 2
        self.blocks = tokens // self.block
        self.units = SEQ // self.block
        self.width = D // ranks
        self.pairs = self.width // PAIR
        self.hidden = FR * HD // ranks
        rows = ranks * tokens // SEQ
        self.span = 1
        for row in range(rows):
            first = row * self.units // self.blocks
            last = (row * self.units + self.units - 1) // self.blocks
            self.span = max(self.span, last - first + 1)
        self.quads = ranks == 4 and dp_size % 4 == 0


def layer_kernel(
    lay,
    x_hbm,
    og_hbm,
    gain1,
    gain2,
    biases_t,
    seg,
    val,
    wqkv_in,
    wo_in,
    w1_in,
    w2_in,
    out_hbm,
    ig_hbm,
    bsum,
    brow,
    x,
    og,
    out,
    ig,
    wqkv,
    wo_b,
    w1_b,
    w2_b,
    xkv,
    qbuf,
    kbuf,
    vbuf,
    pbuf,
    linv,
    mask,
    ctx,
    cgrad,
    abuf,
    bbuf,
    cbuf,
    r1buf,
    low,
    hid,
    gp,
    back,
    group_early,
    group_late,
    all_early,
    all_late,
    sem_local,
    sem_out,
    sem_own_s,
    sem_own_r,
    sem_y,
    sem_x,
    sem_z,
    sem_c,
    sem_w,
    sem_p,
    sem_hs,
    sem_hr,
    sem_gs,
    sem_gr,
    sem_as,
    sem_ar,
    sem_bs,
    sem_br,
    sem_up,
    sem_down,
):
    T, S, B, NB, NU = lay.ranks, lay.tokens, lay.block, lay.blocks, lay.units
    W, PP, F = lay.width, lay.pairs, lay.hidden
    dp = lax.axis_index("dp")
    t = lax.axis_index("tensor")
    quads = lay.quads

    def rank(o):
        r = (t + o) % 2
        if T > 2:
            r = r + 2 * ((t // 2 + o // 2) % 2)
        if T > 4:
            r = r + 4 * ((t // 4 + o // 4) % 2)
        return r

    if quads:
        big = wo_b

        def wo(r):
            return big.at[r, pl.ds(0, W)]

        def w1(r):
            return big.at[r, pl.ds(W, D)]

        def w2(r):
            return big.at[r, pl.ds(W + D, F)]
    else:

        def wo(r):
            return wo_b.at[r]

        def w1(r):
            return w1_b.at[r]

        def w2(r):
            return w2_b.at[r]

    def pieces(r):
        return [wqkv.at[r], wo(r), w1(r), w2(r)]

    sources = [wqkv_in, wo_in, w1_in, w2_in]

    def peer(o):
        return (dp, rank(o))

    def remote(src, dst, send, recv, device):
        return pltpu.make_async_remote_copy(
            src_ref=src,
            dst_ref=dst,
            send_sem=send,
            recv_sem=recv,
            device_id=device,
            device_id_type=MESH_ID,
        )

    barrier = pltpu.get_barrier_semaphore()
    others = [peer(o) for o in range(1, T)]
    heard = T - 1

    def greet(device):
        pl.semaphore_signal(barrier, inc=1, device_id=device, device_id_type=MESH_ID)

    if quads:
        others.append((flip(dp, 1), t))
        link, links = dp // 2, lay.dp_size // 2
        before, after = (dp - 2, t), (dp + 2, t)

        @pl.when(link > 0)
        def _():
            greet(before)

        @pl.when(link < links - 1)
        def _():
            greet(after)

        heard = heard + 1 + jnp.where(link > 0, 1, 0) + jnp.where(link < links - 1, 1, 0)
    else:
        others += [((dp + o) % lay.dp_size, t) for o in range(1, lay.dp_size)]
        heard = len(others)
    for device in others:
        greet(device)
    local = [
        pltpu.make_async_copy(src, dst, sem_local.at[i])
        for i, (src, dst) in enumerate(zip(sources, pieces(t)))
    ]
    x_copy = pltpu.make_async_copy(x_hbm, x, sem_out.at[3])
    x_copy.start()
    for copy in local:
        copy.start()
    og_copy = pltpu.make_async_copy(og_hbm, og, sem_out.at[2])
    og_copy.start()

    row0 = (NB * t) // NU
    has_b = (NB * t + NB - 1) // NU != row0

    def place(j):
        u = NB * t + j
        row = u // NU
        return u, row, row - row0, u - row * NU

    def rows_at(w):
        return pl.ds(pl.multiple_of(w * B, B), B)

    def block_at(j):
        return pl.ds(j * B, B)

    pl.semaphore_wait(barrier, heard)

    x_copy.wait()

    def send_rows():
        for j in range(NB):
            u, row, slot, w = place(j)
            first = row * NU // NB
            last = (row * NU + NU - 1) // NB
            for o in range(lay.span):
                dest = first + o

                @pl.when((dest <= last) & (dest != t))
                def _():
                    remote(
                        x.at[block_at(j)],
                        xkv.at[row - (NB * dest) // NU, rows_at(w)],
                        sem_hs.at[j * lay.span + o],
                        sem_hr.at[(row - (NB * dest) // NU) * NU + w],
                        (dp, dest),
                    ).start()

    if quads:
        role = dp % 4
        relay = role == 3
        gy = role % 3
        gx = jnp.where(role == 1, 0, jnp.where(role == 3, 2, 1))
        gz = jnp.where(role == 2, 0, jnp.where(role == 3, 1, 2))
        far = rank(2)
        core, ynext = (dp, rank(1)), (dp, rank(2))
        xnext, znext = (flip(dp, 1), t), (flip(dp, 2), t)
        rounds = 4
        tail_step = (rounds - 1) * SUBS
        steps = tail_step + LAST_SUBS
        part_a, part_b, part_c = D // SUBS, UNIT // SUBS, UNIT // LAST_SUBS

        def chunk(idx, g, fn):
            n = g * steps + idx

            @pl.when((idx >= 0) & (idx < SUBS))
            def _():
                at = pl.ds(pl.multiple_of(idx * part_a, part_a), part_a)
                fn(lambda r: wqkv.at[r, g, at], n)

            @pl.when((idx >= SUBS) & (idx < tail_step))
            def _():
                row = ((idx // SUBS - 1) * 3 + g) * UNIT + (idx % SUBS) * part_b
                at = pl.ds(pl.multiple_of(row, part_b), part_b)
                fn(lambda r: big.at[r, at], n)

            @pl.when((idx >= tail_step) & (idx < steps))
            def _():
                row = ((rounds - 2) * 3 + g) * UNIT + (idx - tail_step) * part_c
                at = pl.ds(pl.multiple_of(row, part_c), part_c)
                fn(lambda r: big.at[r, at], n)

        def send_y(idx):
            def go(view, n):
                remote(view(t), view(t), sem_y.at[idx], sem_w.at[n], ynext).start()

            chunk(idx, gy, go)

        def to_core(view, n):
            remote(view(far), view(far), sem_c.at[n], sem_p.at[n], core).start()

        def arrived(view, n):
            remote(view(far), view(far), sem_c.at[n], sem_w.at[n], core).wait_recv()

        def to_x(view, n, idx):
            remote(view(far), view(far), sem_x.at[idx], sem_w.at[n], xnext).start()

        def to_z(view, n, idx):
            remote(view(far), view(far), sem_z.at[idx], sem_w.at[n], znext).start()

        def service(s, carry):
            def from_y(view, n):
                arrived(view, n)

                @pl.when(role != 3)
                def _():
                    to_x(view, n, s)
                    to_z(view, n, s)

                to_core(view, n)

            chunk(s, gy, from_y)
            send_y(s + SUBS)
            late = s - jnp.where(relay, RELAY_LAG, LAG)

            def from_x(view, n):
                arrived(view, n)

                @pl.when(relay)
                def _():
                    to_z(view, n, late)

                to_core(view, n)

            def from_z(view, n):
                arrived(view, n)

                @pl.when(relay)
                def _():
                    to_x(view, n, late)

                to_core(view, n)

            chunk(late, gx, from_x)
            chunk(late, gz, from_z)
            return carry

        def sent(idx, carry):
            def go(view, n):
                remote(view(t), view(t), sem_y.at[idx], sem_w.at[n], ynext).wait_send()
                remote(view(t), view(t), sem_x.at[idx], sem_w.at[n], xnext).wait_send()
                remote(view(t), view(t), sem_z.at[idx], sem_w.at[n], znext).wait_send()
                for g in range(3):
                    m = g * steps + idx
                    remote(view(t), view(t), sem_c.at[m], sem_p.at[m], core).wait_send()

            chunk(idx, gy, go)
            return carry

        def from_partner(unit_low, unit_high):
            for unit in range(unit_low, unit_high):
                p, g = unit // 3, unit % 3
                low_step = p * SUBS
                if p == 0:
                    view = wqkv.at[rank(3), 0, pl.ds(0, part_a)]
                else:
                    view = big.at[rank(3), pl.ds(0, part_c if p == rounds - 1 else part_b)]

                def go(idx, carry):
                    n = g * steps + idx
                    remote(view, view, sem_c.at[n], sem_p.at[n], core).wait_recv()
                    return carry

                lax.fori_loop(low_step, steps if p == rounds - 1 else low_step + SUBS, go, 0)

        def own_copies(i):
            return remote(sources[i], pieces(t)[i], sem_own_s.at[i], sem_own_r.at[i], core)

        local[0].wait()
        lax.fori_loop(0, 2, lambda i, c: (send_y(i), c)[1], 0)
        send_rows()
        lax.fori_loop(2, SUBS, lambda i, c: (send_y(i), c)[1], 0)
        for i in range(4):
            own_copies(i).start()
        for i in range(1, 4):
            local[i].wait()

        first_unit = [0, 3, 4, 8, 12]

        def ready(i, o):
            @pl.when(o == 1)
            def _():
                remote(
                    sources[i], pieces(rank(1))[i], sem_own_s.at[i], sem_own_r.at[i], core
                ).wait_recv()

            @pl.when(o == 3)
            def _():
                from_partner(first_unit[i], first_unit[i + 1])

    else:

        def own_copies(i, o):
            n = i * T + o
            return remote(sources[i], pieces(t)[i], sem_own_s.at[n], sem_own_r.at[n], peer(o))

        send_rows()
        for i in range(4):
            for o in range(1, T):
                own_copies(i, o).start()

        def ready(i, o):
            @pl.when(o == 0)
            def _():
                local[i].wait()

            @pl.when(o != 0)
            def _():
                n = i * T + o
                remote(
                    sources[i], pieces(rank(o))[i], sem_own_s.at[n], sem_own_r.at[n], peer(o)
                ).wait_recv()

    key_at = lax.broadcasted_iota(jnp.int32, (B, SEQ), 1)
    query_at = lax.broadcasted_iota(jnp.int32, (B, SEQ), 0)
    for j in range(NB):
        u, row, slot, w = place(j)
        keys_here = pl.ds(pl.multiple_of(row * SEQ, SEQ), SEQ)
        numbers = seg[keys_here].reshape(1, SEQ).astype(F32)
        keyed = jnp.where(val[keys_here].reshape(1, SEQ) == 1, numbers, -1.0)
        same = key_at == query_at + w * B
        own = jnp.sum(jnp.where(same, numbers, 0.0), axis=1, keepdims=True)
        mask[j] = jnp.where((own == keyed) | same, 0.0, -1e30)
        xkv[slot, rows_at(w)] = x[block_at(j)]

    bias_rows = biases_t[...].T
    for i in range(BROWS):
        brow[:, i * HD : (i + 1) * HD] = bias_rows[i : i + 1]

    head_lane = lax.broadcasted_iota(jnp.int32, (B, PAIR), 1) < HD

    def split_heads(values):
        nought = jnp.zeros_like(values)
        return jnp.concatenate(
            [jnp.where(head_lane, values, nought), jnp.where(head_lane, nought, values)], axis=0
        )

    def join_heads(values):
        return jnp.where(head_lane, values[:B], values[B:])

    ones = jnp.ones((SEQ, PAIR), BF16)

    slot_first = jnp.where(has_b & (t % 4 == 2), 1, 0)

    def project_query(r):
        bias = brow[:, pl.ds(pl.multiple_of(AT_QUERY + r * W, PAIR), W)]
        query = ((nn(x[...], wqkv[r, 0]) + bias) * HD**-0.5).astype(BF16)
        for i in range(PP):
            qbuf[r * PP + i] = query[:, i * PAIR : (i + 1) * PAIR]

    def project_keys(o, r):
        bias = brow[:, pl.ds(pl.multiple_of(AT_VALUE + r * W, PAIR), W)]

        def body(turn, carry):
            slot = (slot_first + turn) % 2

            @pl.when((slot == 0) | has_b)
            def _():
                for w in range(NU):
                    owner = ((row0 + slot) * NU + w) // NB

                    @pl.when((owner != t) & (o == 0))
                    def _():
                        remote(
                            x.at[block_at(0)],
                            xkv.at[slot, rows_at(w)],
                            sem_hs.at[0],
                            sem_hr.at[slot * NU + w],
                            (dp, owner),
                        ).wait_recv()

                rows = xkv[slot]
                keys = nn(rows, wqkv[r, 1]).astype(BF16)
                values = (nn(rows, wqkv[r, 2]) + bias).astype(BF16)
                for i in range(PP):
                    kbuf[r * PP + i, slot] = keys[:, i * PAIR : (i + 1) * PAIR]
                    vbuf[r * PP + i, slot] = values[:, i * PAIR : (i + 1) * PAIR]

            return carry

        lax.fori_loop(0, 2, body, 0)

    def attend(r, i):
        hp = r * PP + i
        for j in range(NB):
            u, row, slot, w = place(j)
            query = split_heads(qbuf[hp, block_at(j)])
            hide = mask[j]
            scores = nt(query, kbuf[hp, slot]) + jnp.concatenate([hide, hide], axis=0)
            peak = jnp.max(scores, axis=1, keepdims=True)
            probs = jnp.exp(scores - peak).astype(BF16)
            pbuf[hp, j * 2 * B : (j + 1) * 2 * B] = probs
            mixed = nn(probs, jnp.concatenate([vbuf[hp, slot], ones], axis=1))
            inverse = 1.0 / join_heads(mixed[:, PAIR:])
            linv[hp, block_at(j)] = inverse
            ctx[r, block_at(j), pl.ds(i * PAIR, PAIR)] = (
                join_heads(mixed[:, :PAIR]) * inverse
            ).astype(BF16)

    def project(o):
        ready(0, o)
        r = rank(o)
        project_query(r)
        project_keys(o, r)

    def attend_rank(o):
        for i in range(PP):
            attend(rank(o), i)

    def row_mean(values):
        return jnp.mean(values, axis=1, keepdims=True)

    def row_tiles(body, carry):
        for j in range(NB):
            carry = body(block_at(j), carry)
        return carry

    def norm_first(at, carry):
        values = abuf[at]
        centred = values - row_mean(values)
        root = lax.rsqrt(row_mean(centred * centred) + EPS_NORM)
        normed = centred * root
        r1buf[at] = root
        abuf[at] = normed
        first_normed = normed * gain1[...] + brow[:, AT_FIRST : AT_FIRST + D]
        low[at] = first_normed.astype(BF16)
        bbuf[at] = first_normed + brow[:, AT_FFN : AT_FFN + D]
        return carry

    def finish_attention():
        for o in range(T):
            ready(1, o)
        for n in range(0, D, TILE):
            total = nn(ctx[0], wo(0)[:, n : n + TILE])
            for r in range(1, T):
                total = total + nn(ctx[r], wo(r)[:, n : n + TILE])
            at = pl.ds(n, TILE)
            abuf[:, at] = x[:, at].astype(F32) + total + brow[:, AT_OUT + n : AT_OUT + n + TILE]
        row_tiles(norm_first, 0)

    def expand(o):
        ready(2, o)
        r = rank(o)
        for n in range(0, F, TILE):
            bias = brow[:, pl.ds(pl.multiple_of(AT_HIDDEN + r * F + n, PAIR), TILE)]
            pre = nn(low[...], w1(r)[:, n : n + TILE]) + bias
            cdf = 0.5 * (1.0 + lax.erf(pre * 0.5**0.5))
            density = jnp.exp(-0.5 * pre * pre) * 0.3989422804014327
            hid[r, :, pl.ds(n, TILE)] = (pre * cdf).astype(BF16)
            gp[r, :, pl.ds(n, TILE)] = (cdf + pre * density).astype(BF16)

    def reduce(o):
        ready(3, o)
        r = rank(o)
        for n in range(0, D, TILE):
            at = pl.ds(n, TILE)
            bbuf[:, at] = bbuf[:, at] + nn(hid[r], w2(r)[:, n : n + TILE])

    if quads:
        whole = [(k + 1) * SUBS + LAG - 1 for k in range(rounds - 1)] + [steps + LAG - 1]
        plan = [
            (project, [PLAN[0], PLAN[1], whole[0], whole[0] + 2]),
            (attend_rank, [PLAN[2], PLAN[3], whole[0] + 1, whole[0] + 3]),
            (expand, [whole[1] + 1, whole[1] + 2, whole[2], whole[2] + 1]),
            (reduce, [whole[1] + 3, whole[1] + 4, whole[3], whole[3]]),
        ]

        def pass_on(place_in_chain, sem, to, s):
            @pl.when(s == 2 * place_in_chain)
            def _():
                @pl.when(place_in_chain > 0)
                def _():
                    pl.semaphore_wait(sem, 1)

                @pl.when(place_in_chain < links - 1)
                def _():
                    pl.semaphore_signal(sem, inc=1, device_id=to, device_id_type=MESH_ID)

        def step(s, carry):
            service(s, 0)
            pass_on(link, sem_up, after, s)
            pass_on(links - 1 - link, sem_down, before, s)

            @pl.when(s == whole[1])
            def _():
                finish_attention()

            for part, at_steps in plan:
                o = jnp.int32(-1)
                for k, at_step in enumerate(at_steps):
                    if at_step < whole[3]:
                        o = jnp.where(s == at_step, k, o)

                @pl.when(o >= 0)
                def _():
                    part(o)

            return carry

        lax.fori_loop(0, whole[3] + 1, step, 0)
        lax.fori_loop(2, T, lambda o, c: (reduce(o), c)[1], 0)
    else:

        def each_rank(part):
            lax.fori_loop(0, T, lambda o, c: (part(o), c)[1], 0)

        each_rank(project)
        each_rank(attend_rank)
        finish_attention()
        each_rank(expand)
        each_rank(reduce)

    nought_row = jnp.zeros((1, D), F32)
    og_copy.wait()

    def norm_second(at, carry):
        sum_up, sum_second = carry
        values = bbuf[at]
        centred = values - row_mean(values)
        root = lax.rsqrt(row_mean(centred * centred) + EPS_NORM)
        normed = centred * root
        out[at] = (normed * gain2[...] + brow[:, AT_SECOND : AT_SECOND + D]).astype(BF16)
        upstream = og[at].astype(F32)
        weighted = upstream * gain2[...]
        grad = root * (weighted - row_mean(weighted) - normed * row_mean(weighted * normed))
        bbuf[at] = grad
        low[at] = grad.astype(BF16)
        return (
            sum_up + jnp.sum(upstream, axis=0, keepdims=True),
            sum_second + jnp.sum(grad, axis=0, keepdims=True),
        )

    sum_up, sum_second = row_tiles(norm_second, (nought_row, nought_row))
    out_copy = pltpu.make_async_copy(out, out_hbm, sem_out.at[0])
    out_copy.start()
    bsum[:, AT_SECOND : AT_SECOND + D] = sum_up
    bsum[:, AT_FFN : AT_FFN + D] = sum_second

    def ffn_back(r, carry):
        for n in range(0, F, TILE):
            grad = nt(low[...], w2(r)[n : n + TILE, :]) * gp[r, :, pl.ds(n, TILE)].astype(F32)
            at = pl.ds(pl.multiple_of(AT_HIDDEN + r * F + n, PAIR), TILE)
            bsum[:, at] = jnp.sum(grad, axis=0, keepdims=True)
            hid[r, :, pl.ds(n, TILE)] = grad.astype(BF16)
        return carry

    lax.fori_loop(0, T, ffn_back, 0)
    for n in range(0, D, TILE):
        total = nt(hid[0], w1(0)[n : n + TILE, :])
        for r in range(1, T):
            total = total + nt(hid[r], w1(r)[n : n + TILE, :])
        cbuf[:, pl.ds(n, TILE)] = total

    def first_back(at, carry):
        sum_normed, sum_first = carry
        grad = bbuf[at] + cbuf[at]
        normed = abuf[at]
        weighted = grad * gain1[...]
        first = r1buf[at] * (
            weighted - row_mean(weighted) - normed * row_mean(weighted * normed)
        )
        bbuf[at] = first
        low[at] = first.astype(BF16)
        return (
            sum_normed + jnp.sum(grad, axis=0, keepdims=True),
            sum_first + jnp.sum(first, axis=0, keepdims=True),
        )

    sum_normed, sum_first = row_tiles(first_back, (nought_row, nought_row))
    bsum[:, AT_FIRST : AT_FIRST + D] = sum_normed
    bsum[:, AT_OUT : AT_OUT + D] = sum_first

    class Totals:
        def __init__(self, number, start, amount, group, everyone):
            self.number, self.at = number, pl.ds(start, amount)
            self.group, self.everyone = group, everyone

        def copies(self, buffer, sems, me, peers):
            send, recv = sems
            return [
                remote(
                    buffer.at[me],
                    buffer.at[me],
                    send.at[self.number, k],
                    recv.at[self.number, me],
                    device,
                )
                for k, device in enumerate(peers)
            ]

        def gather(self, buffer, sems, me, peers):
            for copy in self.copies(buffer, sems, me, peers):
                copy.wait_send()
            for k in range(buffer.shape[0]):

                @pl.when(k != me)
                def _():
                    remote(
                        buffer.at[k], buffer.at[k], sems[0].at[0, 0], sems[1].at[self.number, k], peers[0]
                    ).wait_recv()

            total = buffer[0]
            for k in range(1, buffer.shape[0]):
                total = total + buffer[k]
            return total

        def start(self):
            self.group[t] = bsum[:, self.at]
            for copy in self.copies(self.group, (sem_as, sem_ar), t, in_group):
                copy.start()

        def middle(self):
            self.everyone[dp] = self.gather(self.group, (sem_as, sem_ar), t, in_group)
            for copy in self.copies(self.everyone, (sem_bs, sem_br), dp, in_dp):
                copy.start()

        def finish(self):
            bsum[:, self.at] = self.gather(self.everyone, (sem_bs, sem_br), dp, in_dp)

    in_group = [peer(o) for o in range(1, T)]
    in_dp = [((dp + o) % lay.dp_size, t) for o in range(1, lay.dp_size)]
    early = Totals(0, AT_VALUE, FLAT - AT_VALUE, group_early, all_early)
    late = Totals(1, AT_QUERY, AT_VALUE, group_late, all_late)

    for r in range(T):
        grad = nt(low[...], wo(r)[...]).astype(BF16)
        cgrad[r] = grad
        bsum[:, AT_VALUE + r * W : AT_VALUE + (r + 1) * W] = jnp.sum(
            grad.astype(F32), axis=0, keepdims=True
        )
    early.start()

    lone = jnp.where(place(1)[1] != place(0)[1], 0, NB - 1)
    pair_at = jnp.where(lone == 0, 1, 0)
    slot_pair = (NB * t + pair_at) // NU - row0
    slot_lone = (NB * t + lone) // NU - row0
    slot_kept = jnp.where(has_b, slot_pair, 1)

    def attend_back(r, i, first_block, amount, slot):
        hp = r * PP + i
        lanes = pl.ds(i * PAIR, PAIR)
        queries, upstreams, deltas = [], [], []
        for k in range(amount):
            at = rows_at(first_block + k)
            scaled = cgrad[r, at, lanes].astype(F32) * linv[hp, at]
            upstreams.append(split_heads(scaled.astype(BF16)))
            deltas.append(split_heads(scaled * ctx[r, at, lanes].astype(F32)))
            queries.append(split_heads(qbuf[hp, at]))
        upstream, query = jnp.concatenate(upstreams), jnp.concatenate(queries)
        delta = jnp.sum(jnp.concatenate(deltas), axis=1, keepdims=True)
        probs = pbuf[hp, pl.ds(pl.multiple_of(first_block * 2 * B, 2 * B), amount * 2 * B)]
        score = (probs.astype(F32) * (nt(upstream, vbuf[hp, slot]) - delta)).astype(BF16)
        value_grad = nn(upstream.T, probs)
        key_grad = nn(query.T, score)
        joined = nn(score, kbuf[hp, slot]) * HD**-0.5
        total = jnp.zeros((1, PAIR), F32)
        for k in range(amount):
            grad = join_heads(joined[k * 2 * B : (k + 1) * 2 * B])
            qbuf[hp, rows_at(first_block + k)] = grad.astype(BF16)
            total = total + jnp.sum(grad, axis=0, keepdims=True)
        return key_grad.astype(BF16).T, value_grad.astype(BF16).T, total

    def rank_back_pair(r, carry):
        for i in range(PP):
            keys, values, total = attend_back(r, i, pair_at, 2, slot_pair)
            kbuf[r * PP + i, slot_kept] = keys
            vbuf[r * PP + i, slot_kept] = values
            bsum[:, pl.ds(pl.multiple_of(AT_QUERY + r * W + i * PAIR, PAIR), PAIR)] = total

        @pl.when(r == T // 2 - 1)
        def _():
            early.middle()

        return carry

    def rank_back_lone(r, carry):
        for i in range(PP):
            hp = r * PP + i
            keys, values, total = attend_back(r, i, lone, 1, slot_lone)
            at = pl.ds(pl.multiple_of(AT_QUERY + r * W + i * PAIR, PAIR), PAIR)
            bsum[:, at] = bsum[:, at] + total
            kept = [jnp.where(has_b, jnp.zeros_like(keys), buf[hp, 1]) for buf in (kbuf, vbuf)]
            kbuf[hp, slot_lone] = keys + kept[0]
            vbuf[hp, slot_lone] = values + kept[1]
        return carry

    def wide(buffer, r, *at):
        return jnp.concatenate([buffer[(r * PP + i, *at)] for i in range(PP)], axis=1)

    half = SEQ // 2

    def share_copy(slot, w, k):
        u = (row0 + slot) * NU + w
        owner = u // NB
        first = (row0 + slot) * NU // NB
        place_of = t - first - jnp.where(t > owner, 1, 0)
        number = (u - owner * NB) * (lay.span - 1) + place_of
        at = pl.ds(pl.multiple_of(k * TILE, TILE), TILE)
        return remote(
            xkv.at[slot, rows_at(w), at],
            back.at[number, :, at],
            sem_gs.at[slot * NU + w, k],
            sem_gr.at[number, k],
            (dp, owner),
        )

    def send_shares(slot, rows, first_unit, amount):
        def body(k, carry):
            at = pl.ds(pl.multiple_of(k * TILE, TILE), TILE)
            total = nt(wide(kbuf, 0, slot, rows), wqkv[0, 1, at])
            total = total + nt(wide(vbuf, 0, slot, rows), wqkv[0, 2, at])
            for r in range(1, T):
                total = total + nt(wide(kbuf, r, slot, rows), wqkv[r, 1, at])
                total = total + nt(wide(vbuf, r, slot, rows), wqkv[r, 2, at])
            xkv[slot, rows, at] = total.astype(BF16)
            for n in range(amount):
                w = first_unit + n
                owner = ((row0 + slot) * NU + w) // NB

                @pl.when(owner != t)
                def _():
                    share_copy(slot, w, k).start()

            return carry

        lax.fori_loop(0, D // TILE, body, 0)

    def send_half(slot, part):
        rows = pl.ds(pl.multiple_of(part * half, half), half)
        send_shares(slot, rows, part * (NU // 2), NU // 2)

    lax.fori_loop(0, T, rank_back_pair, 0)
    part_first = jnp.where(lone == 0, 1, 0)

    def turns(k, carry):
        @pl.when((k != 1) & has_b)
        def _():
            send_half(slot_pair, jnp.where(k == 0, part_first, 1 - part_first))

        @pl.when(k == 1)
        def _():
            lax.fori_loop(0, T, rank_back_lone, 0)
            late.start()

        return carry

    lax.fori_loop(0, 3, turns, 0)
    late.middle()
    send_shares(slot_lone, pl.ds(0, SEQ), 0, NU)

    for n in range(0, D, TILE):
        total = nt(wide(qbuf, 0), wqkv[0, 0, pl.ds(n, TILE)])
        for r in range(1, T):
            total = total + nt(wide(qbuf, r), wqkv[r, 0, pl.ds(n, TILE)])
        at = pl.ds(n, TILE)
        bbuf[:, at] = bbuf[:, at] + total

    for j in range(NB):
        u, row, slot, w = place(j)
        bbuf[block_at(j)] = bbuf[block_at(j)] + xkv[slot, rows_at(w)].astype(F32)
    early.finish()

    for j in range(NB):
        u, row, slot, w = place(j)
        first = row * NU // NB
        last = (row * NU + NU - 1) // NB
        for o in range(lay.span - 1):
            number = j * (lay.span - 1) + o

            @pl.when(first + o < last)
            def _():
                sender = first + o + jnp.where(first + o >= t, 1, 0)
                for k in range(D // TILE):
                    at = pl.ds(k * TILE, TILE)
                    remote(
                        xkv.at[0, rows_at(0), at],
                        back.at[number, :, at],
                        sem_gs.at[0, k],
                        sem_gr.at[number, k],
                        (dp, sender),
                    ).wait_recv()
                bbuf[block_at(j)] = bbuf[block_at(j)] + back[number].astype(F32)

        ig[block_at(j)] = bbuf[block_at(j)].astype(BF16)

    ig_copy = pltpu.make_async_copy(ig, ig_hbm, sem_out.at[1])
    ig_copy.start()
    late.finish()

    out_copy.wait()
    ig_copy.wait()
    for slot in range(2):
        for w in range(NU):
            owner = ((row0 + slot) * NU + w) // NB

            @pl.when((owner != t) & ((slot == 0) | has_b))
            def _():
                lax.fori_loop(0, D // TILE, lambda k, c: (share_copy(slot, w, k).wait_send(), c)[1], 0)

    for j in range(NB):
        u, row, slot, w = place(j)
        first = row * NU // NB
        last = (row * NU + NU - 1) // NB
        for o in range(lay.span):
            dest = first + o

            @pl.when((dest <= last) & (dest != t))
            def _():
                remote(
                    x.at[block_at(j)],
                    xkv.at[0, rows_at(0)],
                    sem_hs.at[j * lay.span + o],
                    sem_hr.at[0],
                    (dp, dest),
                ).wait_send()

    if quads:
        for i in range(4):
            own_copies(i).wait_send()
        lax.fori_loop(0, steps, sent, 0)
    else:
        for i in range(4):
            for o in range(1, T):
                own_copies(i, o).wait_send()


def layer_call(lay, *args):
    T, S = lay.ranks, lay.tokens
    hp = HEADS // 2
    vmem = pltpu.VMEM
    if lay.quads:
        wide = [
            vmem((T, lay.width + D + lay.hidden, D), BF16),
            vmem((16, PAIR), BF16),
            vmem((16, PAIR), BF16),
        ]
    else:
        wide = [
            vmem((T, lay.width, D), BF16),
            vmem((T, D, lay.hidden), BF16),
            vmem((T, lay.hidden, D), BF16),
        ]
    dma = pltpu.SemaphoreType.DMA
    steps = 3 * SUBS + LAST_SUBS
    own = 4 if lay.quads else 4 * T
    sharers = lay.blocks * max(lay.span - 1, 1)
    scratch = (
        [vmem((1, FLAT), F32)] + [vmem((S, D), BF16)] * 4
        + [vmem((T, 3, D, lay.width), BF16)]
        + wide
        + [
            vmem((2, SEQ, D), BF16),
            vmem((hp, S, PAIR), BF16),
            vmem((hp, 2, SEQ, PAIR), BF16),
            vmem((hp, 2, SEQ, PAIR), BF16),
            vmem((hp, lay.blocks * 2 * lay.block, SEQ), BF16),
            vmem((hp, S, PAIR), F32),
            vmem((lay.blocks, lay.block, SEQ), F32),
            vmem((T, S, lay.width), BF16),
            vmem((T, S, lay.width), BF16),
            vmem((S, D), F32),
            vmem((S, D), F32),
            vmem((S, D), F32),
            vmem((S, 1), F32),
            vmem((S, D), BF16),
            vmem((T, S, lay.hidden), BF16),
            vmem((T, S, lay.hidden), BF16),
            vmem((sharers, lay.block, D), BF16),
            vmem((T, 1, FLAT - AT_VALUE), F32),
            vmem((T, 1, AT_VALUE), F32),
            vmem((lay.dp_size, 1, FLAT - AT_VALUE), F32),
            vmem((lay.dp_size, 1, AT_VALUE), F32),
            dma((4,)),
            dma((4,)),
            dma((own,)),
            dma((own,)),
            dma((steps,)),
            dma((steps,)),
            dma((steps,)),
            dma((3 * steps,)),
            dma((3 * steps,)),
            dma((3 * steps,)),
            dma((lay.blocks * lay.span,)),
            dma((2 * lay.units,)),
            dma((2 * lay.units, D // TILE)),
            dma((sharers, D // TILE)),
            dma((2, T)),
            dma((2, T)),
            dma((2, lay.dp_size)),
            dma((2, lay.dp_size)),
            pltpu.SemaphoreType.REGULAR,
            pltpu.SemaphoreType.REGULAR,
        ]
    )
    in_vmem = pl.BlockSpec(memory_space=pltpu.VMEM)
    anywhere = pl.BlockSpec(memory_space=pl.ANY)
    return pl.pallas_call(
        partial(layer_kernel, lay),
        out_shape=(
            jax.ShapeDtypeStruct((S, D), BF16),
            jax.ShapeDtypeStruct((S, D), BF16),
            jax.ShapeDtypeStruct((1, FLAT), F32),
        ),
        in_specs=[anywhere] * 2 + [in_vmem] * 5 + [anywhere] * 4,
        out_specs=(anywhere, anywhere, in_vmem),
        scratch_shapes=scratch,
        compiler_params=pltpu.CompilerParams(
            collective_id=0, has_side_effects=True, vmem_limit_bytes=VMEM_BYTES
        ),
        name="layer",
    )(*args)


VMEM_BYTES = 63 * 2**20
PLAN = [2, 5, 3, 6]


def update_kernel(
    raw,
    biases,
    moment_one,
    moment_two,
    left_pairs,
    left_hidden,
    left_small,
    right_bases,
    owners,
    out_in,
    ig_in,
    clipped_out,
    norm_out,
    new_out,
    copies_out,
    one_out,
    two_out,
    out_out,
    ig_out,
    rows,
    left,
    wide,
    sems,
):
    fetches = [
        pltpu.make_async_copy(src, wide.at[i], sems.at[i]) for i, src in enumerate((out_in, ig_in))
    ]
    stores = [
        pltpu.make_async_copy(wide.at[i], dst, sems.at[2 + i])
        for i, dst in enumerate((out_out, ig_out))
    ]
    for fetch in fetches:
        fetch.start()
    sums = raw[...]
    norm = jnp.sqrt(jnp.sum(sums * sums, keepdims=True))
    norm_out[...] = norm
    for i in range(BROWS):
        rows[i : i + 1] = sums[:, i * HD : (i + 1) * HD]
    clipped = rows[...].T * (CLIP_LIMIT / jnp.maximum(norm, CLIP_LIMIT))
    clipped_out[...] = clipped
    dp = lax.axis_index("dp")
    tail = 2 * HEADS + FR
    layout = [(0, 2 * HEADS, left_pairs), (2 * HEADS, FR, left_hidden)]
    layout += [(tail + k * DR, DR, left_small.at[k]) for k in range(4)]
    left[...] = jnp.zeros_like(left)
    for begin, amount, basis in layout:
        left[begin : begin + amount, begin : begin + amount] = basis[...]
    for fetch, store in zip(fetches, stores):
        fetch.wait()
        store.start()
    column = lax.broadcasted_iota(jnp.int32, (HD, BROWS), 1)

    def per_matrix(choose):
        result = choose(0)
        for k in range(1, len(layout)):
            result = jnp.where(column >= layout[k][0], choose(k), result)
        return result

    def product(a, b, over_a, over_b):
        return lax.dot_general(
            a,
            b,
            (((over_a,), (over_b,)), ((), ())),
            precision=HIGHEST,
            preferred_element_type=F32,
        )

    half = product(clipped, left[...], 1, 0)
    rotated = per_matrix(lambda k: product(right_bases[k], half, 0, 0))
    one = BETA_ONE * moment_one[...] + (1.0 - BETA_ONE) * rotated
    two = BETA_TWO * moment_two[...] + (1.0 - BETA_TWO) * rotated * rotated
    direction = (
        one / (1.0 - BETA_ONE**STEP) / (jnp.sqrt(two / (1.0 - BETA_TWO**STEP)) + ADAM_EPS)
    )
    half = per_matrix(lambda k: product(right_bases[k], direction, 1, 0))
    new = biases[...] - LEARN_RATE * product(half, left[...], 1, 1)
    copies_out[...] = new.astype(BF16)
    mine = per_matrix(lambda k: jnp.where(owners[k] == dp, 1.0, 0.0)) > 0.5
    new_out[...] = jnp.where(mine, new, 0.0)
    one_out[...] = jnp.where(mine, one, 0.0)
    two_out[...] = jnp.where(mine, two, 0.0)
    for store in stores:
        store.wait()


def update_call(tokens, *args):
    in_vmem = pl.BlockSpec(memory_space=pltpu.VMEM)
    anywhere = pl.BlockSpec(memory_space=pl.ANY)
    block = jax.ShapeDtypeStruct((HD, BROWS), F32)
    wide = jax.ShapeDtypeStruct((tokens, D), BF16)
    return pl.pallas_call(
        update_kernel,
        out_shape=(
            block,
            jax.ShapeDtypeStruct((1, 1), F32),
            block,
            jax.ShapeDtypeStruct((HD, BROWS), BF16),
            block,
            block,
            wide,
            wide,
        ),
        in_specs=[in_vmem] * 8 + [pl.BlockSpec(memory_space=pltpu.SMEM)] + [anywhere] * 2,
        out_specs=(in_vmem,) * 6 + (anywhere,) * 2,
        scratch_shapes=[
            pltpu.VMEM((BROWS, HD), F32),
            pltpu.VMEM((BROWS, BROWS), F32),
            pltpu.VMEM((2, tokens, D), BF16),
            pltpu.SemaphoreType.DMA((4,)),
        ],
        name="update",
    )(*args)


def on_device(
    dp_size,
    ranks,
    inputs,
    output_grad,
    input_project,
    output_project,
    expand_weight,
    reduce_weight,
    first_gain,
    second_gain,
    biases,
    first_moment,
    second_moment,
    left_pairs,
    left_hidden,
    left_small,
    right_bases,
    segment_number,
    token_mask,
    owners,
):
    lay = Layout(dp_size, ranks, inputs.shape[0])
    layer_out, input_grad, sums = layer_call(
        lay,
        inputs,
        output_grad,
        first_gain.reshape(1, D),
        second_gain.reshape(1, D),
        biases.T,
        segment_number,
        token_mask,
        input_project,
        output_project,
        expand_weight,
        reduce_weight,
    )
    clipped, clip_norm, new_owned, copies, first_owned, second_owned, layer_out, input_grad = (
        update_call(
            inputs.shape[0],
            sums,
            biases.T,
            first_moment.T,
            second_moment.T,
            left_pairs,
            left_hidden,
            left_small,
            right_bases,
            owners,
            layer_out,
            input_grad,
        )
    )
    return (
        layer_out,
        input_grad,
        clipped.T,
        clip_norm.reshape(1),
        new_owned.T,
        copies.T,
        first_owned.T,
        second_owned.T,
    )


def solution(mesh):
    return jax.shard_map(
        partial(on_device, mesh.shape["dp"], mesh.shape["tensor"]),
        mesh=mesh,
        in_specs=(
            P(("dp", "tensor"), None),
            P(("dp", "tensor"), None),
            P(None, None, "tensor"),
            P("tensor", None),
            P(None, "tensor"),
            P("tensor", None),
            P(),
            P(),
            P(),
            P(),
            P(),
            P(),
            P(),
            P(),
            P(),
            P("dp"),
            P("dp"),
            P(),
        ),
        out_specs=(
            P(("dp", "tensor"), None),
            P(("dp", "tensor"), None),
            P(),
            P(),
            P("dp", None),
            P(),
            P("dp", None),
            P("dp", None),
        ),
        check_vma=False,
    )
```

```python
from functools import partial

import jax
import jax.numpy as jnp
from jax import lax
from jax.experimental import pallas as pl
from jax.experimental.pallas import tpu as pltpu
from jax.sharding import PartitionSpec as P

D = 1024
HEADS = 16
HD = 64
PAIR = 2 * HD
SEQ = 512
STEP = 10
FR = 64
DR = 16
BROWS = 160
AT_QUERY, AT_VALUE, AT_HIDDEN = 0, D, 2 * D
AT_OUT = 2 * D + FR * HD
AT_FIRST, AT_FFN, AT_SECOND = AT_OUT + D, AT_OUT + 2 * D, AT_OUT + 3 * D
FLAT = BROWS * HD

EPS_NORM = 1e-12
CLIP_LIMIT = 64.0
BETA_ONE = 0.9
BETA_TWO = 0.99
ADAM_EPS = 1e-08
LEARN_RATE = 0.2
HIGHEST = lax.Precision.HIGHEST
MESH_ID = pl.DeviceIdType.MESH
BF16 = jnp.bfloat16
F32 = jnp.float32

SUBS = 4
LAST_SUBS = 4
DIRECT = 2
RELAY_LAG, LAG = 2, 4
UNIT = 256
TILE = 256


def nn(a, b):
    return jnp.dot(a, b, preferred_element_type=F32)


def nt(a, b):
    return lax.dot_general(a, b, (((1,), (1,)), ((), ())), preferred_element_type=F32)


def tn(a, b):
    return lax.dot_general(a, b, (((0,), (0,)), ((), ())), preferred_element_type=F32)


def flip(value, bit):
    return value + bit - 2 * bit * ((value // bit) % 2)


class Layout:
    def __init__(self, dp_size, ranks, tokens):
        self.dp_size, self.ranks, self.tokens = dp_size, ranks, tokens
        self.block = 1
        while tokens % (2 * self.block) == 0 and SEQ % (2 * self.block) == 0:
            self.block *= 2
        self.blocks = tokens // self.block
        self.units = SEQ // self.block
        self.width = D // ranks
        self.pairs = self.width // PAIR
        self.hidden = FR * HD // ranks
        rows = ranks * tokens // SEQ
        self.span = 1
        for row in range(rows):
            first = row * self.units // self.blocks
            last = (row * self.units + self.units - 1) // self.blocks
            self.span = max(self.span, last - first + 1)
        self.quads = ranks == 4 and dp_size % 4 == 0


def layer_kernel(
    lay,
    x_hbm,
    og_hbm,
    gain1_hbm,
    gain2_hbm,
    biases_hbm,
    seg_hbm,
    val_hbm,
    wqkv_in,
    wo_in,
    w1_in,
    w2_in,
    out_hbm,
    ig_hbm,
    bsum,
    brow,
    x,
    og,
    out,
    ig,
    gain1,
    gain2,
    biases_t,
    seg,
    val,
    wqkv,
    wo_b,
    w1_b,
    w2_b,
    xkv,
    qbuf,
    kbuf,
    vbuf,
    pbuf,
    linv,
    mask,
    ctx,
    cgrad,
    abuf,
    bbuf,
    cbuf,
    r1buf,
    low,
    hid,
    gp,
    back,
    group_early,
    group_late,
    all_early,
    all_late,
    sem_local,
    sem_out,
    sem_own_s,
    sem_own_r,
    sem_y,
    sem_x,
    sem_z,
    sem_c,
    sem_w,
    sem_p,
    sem_hs,
    sem_hr,
    sem_gs,
    sem_gr,
    sem_as,
    sem_ar,
    sem_bs,
    sem_br,
    sem_up,
    sem_down,
):
    T, S, B, NB, NU = lay.ranks, lay.tokens, lay.block, lay.blocks, lay.units
    W, PP, F = lay.width, lay.pairs, lay.hidden
    dp = lax.axis_index("dp")
    t = lax.axis_index("tensor")
    quads = lay.quads

    def rank(o):
        r = (t + o) % 2
        if T > 2:
            r = r + 2 * ((t // 2 + o // 2) % 2)
        if T > 4:
            r = r + 4 * ((t // 4 + o // 4) % 2)
        return r

    if quads:
        big = wo_b

        def wo(r):
            return big.at[r, pl.ds(0, W)]

        def w1(r):
            return big.at[r, pl.ds(W, D)]

        def w2(r):
            return big.at[r, pl.ds(W + D, F)]
    else:

        def wo(r):
            return wo_b.at[r]

        def w1(r):
            return w1_b.at[r]

        def w2(r):
            return w2_b.at[r]

    def pieces(r):
        return [wqkv.at[r], wo(r), w1(r), w2(r)]

    sources = [wqkv_in, wo_in, w1_in, w2_in]

    def peer(o):
        return (dp, rank(o))

    def remote(src, dst, send, recv, device):
        return pltpu.make_async_remote_copy(
            src_ref=src,
            dst_ref=dst,
            send_sem=send,
            recv_sem=recv,
            device_id=device,
            device_id_type=MESH_ID,
        )

    barrier = pltpu.get_barrier_semaphore()
    others = [peer(o) for o in range(1, T)]
    heard = T - 1

    def greet(device):
        pl.semaphore_signal(barrier, inc=1, device_id=device, device_id_type=MESH_ID)

    if quads:
        others.append((flip(dp, 1), t))
        link, links = dp // 2, lay.dp_size // 2
        before, after = (dp - 2, t), (dp + 2, t)

        @pl.when(link > 0)
        def _():
            greet(before)

        @pl.when(link < links - 1)
        def _():
            greet(after)

        heard = heard + 1 + jnp.where(link > 0, 1, 0) + jnp.where(link < links - 1, 1, 0)
    else:
        others += [((dp + o) % lay.dp_size, t) for o in range(1, lay.dp_size)]
        heard = len(others)
    for device in others:
        greet(device)
    local = [
        pltpu.make_async_copy(src, dst, sem_local.at[i])
        for i, (src, dst) in enumerate(zip(sources, pieces(t)))
    ]
    x_copy = pltpu.make_async_copy(x_hbm, x, sem_out.at[3])
    x_copy.start()
    for copy in local:
        copy.start()
    og_copy = pltpu.make_async_copy(og_hbm, og, sem_out.at[2])
    og_copy.start()
    small = [
        pltpu.make_async_copy(src, dst, sem_out.at[4 + i])
        for i, (src, dst) in enumerate(
            [
                (biases_hbm, biases_t),
                (seg_hbm, seg),
                (val_hbm, val),
                (gain1_hbm, gain1),
                (gain2_hbm, gain2),
            ]
        )
    ]
    for copy in small:
        copy.start()

    row0 = (NB * t) // NU
    has_b = (NB * t + NB - 1) // NU != row0

    def place(j):
        u = NB * t + j
        row = u // NU
        return u, row, row - row0, u - row * NU

    def rows_at(w):
        return pl.ds(pl.multiple_of(w * B, B), B)

    def block_at(j):
        return pl.ds(j * B, B)

    pl.semaphore_wait(barrier, heard)

    x_copy.wait()

    def send_rows():
        for j in range(NB):
            u, row, slot, w = place(j)
            first = row * NU // NB
            last = (row * NU + NU - 1) // NB
            for o in range(lay.span):
                dest = first + o

                @pl.when((dest <= last) & (dest != t))
                def _():
                    remote(
                        x.at[block_at(j)],
                        xkv.at[row - (NB * dest) // NU, rows_at(w)],
                        sem_hs.at[j * lay.span + o],
                        sem_hr.at[(row - (NB * dest) // NU) * NU + w],
                        (dp, dest),
                    ).start()

    if quads:
        role = dp % 4
        relay = role == 3
        gy = role % 3
        gx = jnp.where(role == 1, 0, jnp.where(role == 3, 2, 1))
        gz = jnp.where(role == 2, 0, jnp.where(role == 3, 1, 2))
        far = rank(2)
        core, ynext = (dp, rank(1)), (dp, rank(2))
        xnext, znext = (flip(dp, 1), t), (flip(dp, 2), t)
        rounds = 4
        tail_step = (rounds - 1) * SUBS
        steps = tail_step + LAST_SUBS
        part_a, part_b, part_c = D // SUBS, UNIT // SUBS, UNIT // LAST_SUBS

        def chunk(idx, g, fn):
            n = g * steps + idx

            @pl.when((idx >= 0) & (idx < SUBS))
            def _():
                at = pl.ds(pl.multiple_of(idx * part_a, part_a), part_a)
                fn(lambda r: wqkv.at[r, g, at], n)

            @pl.when((idx >= SUBS) & (idx < tail_step))
            def _():
                row = ((idx // SUBS - 1) * 3 + g) * UNIT + (idx % SUBS) * part_b
                at = pl.ds(pl.multiple_of(row, part_b), part_b)
                fn(lambda r: big.at[r, at], n)

            @pl.when((idx >= tail_step) & (idx < steps))
            def _():
                row = ((rounds - 2) * 3 + g) * UNIT + (idx - tail_step) * part_c
                at = pl.ds(pl.multiple_of(row, part_c), part_c)
                fn(lambda r: big.at[r, at], n)

        relayed = steps - DIRECT
        g_direct = jnp.where(role == 1, 2, 1)
        is_served = (role == 1) | (role == 2)

        def send_y(idx):
            def go(view, n):
                remote(view(t), view(t), sem_y.at[idx], sem_w.at[n], ynext).start()

            chunk(idx, gy, go)

            def go_direct(view, n):
                remote(
                    view(t), view(t), sem_y.at[idx + DIRECT], sem_w.at[n], ynext
                ).start()

            @pl.when((idx >= relayed) & is_served)
            def _():
                chunk(idx, g_direct, go_direct)

        def to_core(view, n):
            remote(view(far), view(far), sem_c.at[n], sem_p.at[n], core).start()

        def arrived(view, n):
            remote(view(far), view(far), sem_c.at[n], sem_w.at[n], core).wait_recv()

        def to_x(view, n, idx):
            remote(view(far), view(far), sem_x.at[idx], sem_w.at[n], xnext).start()

        def to_z(view, n, idx):
            remote(view(far), view(far), sem_z.at[idx], sem_w.at[n], znext).start()

        def service(s, carry):
            def from_y(view, n):
                arrived(view, n)

                @pl.when(role != 3)
                def _():
                    to_x(view, n, s)
                    to_z(view, n, s)

                to_core(view, n)

            chunk(s, gy, from_y)
            send_y(s + SUBS)
            late = s - jnp.where(relay, RELAY_LAG, LAG)

            def from_x(view, n):
                arrived(view, n)

                @pl.when(relay & (late < relayed))
                def _():
                    to_z(view, n, late)

                to_core(view, n)

            def from_z(view, n):
                arrived(view, n)

                @pl.when(relay & (late < relayed))
                def _():
                    to_x(view, n, late)

                to_core(view, n)

            chunk(late, gx, from_x)
            chunk(late, gz, from_z)
            return carry

        def sent(idx, carry):
            def go(view, n):
                remote(view(t), view(t), sem_y.at[idx], sem_w.at[n], ynext).wait_send()

                @pl.when((role != 3) | (idx < relayed))
                def _():
                    remote(view(t), view(t), sem_x.at[idx], sem_w.at[n], xnext).wait_send()
                    remote(view(t), view(t), sem_z.at[idx], sem_w.at[n], znext).wait_send()

                @pl.when((idx >= relayed) & is_served)
                def _():
                    remote(
                        view(t), view(t), sem_y.at[idx + DIRECT], sem_w.at[n], ynext
                    ).wait_send()

                for g in range(3):
                    m = g * steps + idx
                    remote(view(t), view(t), sem_c.at[m], sem_p.at[m], core).wait_send()

            chunk(idx, gy, go)
            return carry

        def from_partner(units):
            for unit in units:
                p, g = unit // 3, unit % 3
                if p == 0:
                    view = wqkv.at[rank(3), 0, pl.ds(0, part_a)]
                else:
                    view = big.at[rank(3), pl.ds(0, part_c if p == rounds - 1 else part_b)]

                def go(idx, carry):
                    n = g * steps + idx
                    remote(view, view, sem_c.at[n], sem_p.at[n], core).wait_recv()
                    return carry

                if p == rounds - 1:
                    lax.fori_loop(tail_step, steps, go, 0)
                else:
                    lax.fori_loop(p * SUBS, (p + 1) * SUBS, go, 0)

        def own_copies(i):
            return remote(sources[i], pieces(t)[i], sem_own_s.at[i], sem_own_r.at[i], core)

        local[0].wait()
        lax.fori_loop(0, 2, lambda i, c: (send_y(i), c)[1], 0)
        send_rows()
        lax.fori_loop(2, SUBS, lambda i, c: (send_y(i), c)[1], 0)
        for i in range(4):
            own_copies(i).start()
        for i in range(1, 4):
            local[i].wait()

        first_unit = [0, 3, 4, 8, 12]

        def ready(i, o):
            @pl.when(o == 1)
            def _():
                remote(
                    sources[i], pieces(rank(1))[i], sem_own_s.at[i], sem_own_r.at[i], core
                ).wait_recv()

            @pl.when(o == 3)
            def _():
                from_partner(range(first_unit[i], first_unit[i + 1]))

    else:

        def own_copies(i, o):
            n = i * T + o
            return remote(sources[i], pieces(t)[i], sem_own_s.at[n], sem_own_r.at[n], peer(o))

        send_rows()
        for i in range(4):
            for o in range(1, T):
                own_copies(i, o).start()

        def ready(i, o):
            @pl.when(o == 0)
            def _():
                local[i].wait()

            @pl.when(o != 0)
            def _():
                n = i * T + o
                remote(
                    sources[i], pieces(rank(o))[i], sem_own_s.at[n], sem_own_r.at[n], peer(o)
                ).wait_recv()

    for copy in small:
        copy.wait()
    key_at = lax.broadcasted_iota(jnp.int32, (B, SEQ), 1)
    query_at = lax.broadcasted_iota(jnp.int32, (B, SEQ), 0)
    for j in range(NB):
        u, row, slot, w = place(j)
        keys_here = pl.ds(pl.multiple_of(row * SEQ, SEQ), SEQ)
        numbers = seg[keys_here].reshape(1, SEQ).astype(F32)
        keyed = jnp.where(val[keys_here].reshape(1, SEQ) == 1, numbers, -1.0)
        same = key_at == query_at + w * B
        own = jnp.sum(jnp.where(same, numbers, 0.0), axis=1, keepdims=True)
        mask[j] = jnp.where((own == keyed) | same, 0.0, -1e30)
        xkv[slot, rows_at(w)] = x[block_at(j)]

    bias_rows = biases_t[...].T
    for i in range(BROWS):
        brow[:, i * HD : (i + 1) * HD] = bias_rows[i : i + 1]

    head_lane = lax.broadcasted_iota(jnp.int32, (B, PAIR), 1) < HD

    def split_heads(values):
        nought = jnp.zeros_like(values)
        return jnp.concatenate(
            [jnp.where(head_lane, values, nought), jnp.where(head_lane, nought, values)], axis=0
        )

    def join_heads(values):
        return jnp.where(head_lane, values[:B], values[B:])

    ones = jnp.ones((SEQ, PAIR), BF16)

    slot_first = jnp.where(has_b & (t % 4 == 2), 1, 0)

    def project_query(r):
        bias = brow[:, pl.ds(pl.multiple_of(AT_QUERY + r * W, PAIR), W)]
        query = ((nn(x[...], wqkv[r, 0]) + bias) * HD**-0.5).astype(BF16)
        for i in range(PP):
            qbuf[r * PP + i] = query[:, i * PAIR : (i + 1) * PAIR]

    def project_keys(o, r):
        bias = brow[:, pl.ds(pl.multiple_of(AT_VALUE + r * W, PAIR), W)]

        def body(turn, carry):
            slot = (slot_first + turn) % 2

            @pl.when((slot == 0) | has_b)
            def _():
                for w in range(NU):
                    owner = ((row0 + slot) * NU + w) // NB

                    @pl.when((owner != t) & (o == 0))
                    def _():
                        remote(
                            x.at[block_at(0)],
                            xkv.at[slot, rows_at(w)],
                            sem_hs.at[0],
                            sem_hr.at[slot * NU + w],
                            (dp, owner),
                        ).wait_recv()

                rows = xkv[slot]
                keys = nn(rows, wqkv[r, 1]).astype(BF16)
                values = (nn(rows, wqkv[r, 2]) + bias).astype(BF16)
                for i in range(PP):
                    kbuf[r * PP + i, slot] = keys[:, i * PAIR : (i + 1) * PAIR]
                    vbuf[r * PP + i, slot] = values[:, i * PAIR : (i + 1) * PAIR]

            return carry

        lax.fori_loop(0, 2, body, 0)

    def attend(r, i):
        hp = r * PP + i
        for j in range(NB):
            u, row, slot, w = place(j)
            query = split_heads(qbuf[hp, block_at(j)])
            hide = mask[j]
            scores = nt(query, kbuf[hp, slot]) + jnp.concatenate([hide, hide], axis=0)
            peak = jnp.max(scores, axis=1, keepdims=True)
            probs = jnp.exp(scores - peak).astype(BF16)
            pbuf[hp, j * 2 * B : (j + 1) * 2 * B] = probs
            mixed = nn(probs, jnp.concatenate([vbuf[hp, slot], ones], axis=1))
            inverse = 1.0 / join_heads(mixed[:, PAIR:])
            linv[hp, block_at(j)] = inverse
            ctx[r, block_at(j), pl.ds(i * PAIR, PAIR)] = (
                join_heads(mixed[:, :PAIR]) * inverse
            ).astype(BF16)

    def project(o):
        ready(0, o)
        r = rank(o)
        project_query(r)
        project_keys(o, r)

    def attend_rank(o):
        for i in range(PP):
            attend(rank(o), i)

    def row_mean(values):
        return jnp.mean(values, axis=1, keepdims=True)

    def row_tiles(body, carry):
        for j in range(NB):
            carry = body(block_at(j), carry)
        return carry

    def norm_first(at, carry):
        values = abuf[at]
        centred = values - row_mean(values)
        root = lax.rsqrt(row_mean(centred * centred) + EPS_NORM)
        normed = centred * root
        r1buf[at] = root
        abuf[at] = normed
        first_normed = normed * gain1[...] + brow[:, AT_FIRST : AT_FIRST + D]
        low[at] = first_normed.astype(BF16)
        bbuf[at] = first_normed + brow[:, AT_FFN : AT_FFN + D]
        return carry

    def finish_attention():
        for o in range(T):
            ready(1, o)
        for n in range(0, D, TILE):
            total = nn(ctx[0], wo(0)[:, n : n + TILE])
            for r in range(1, T):
                total = total + nn(ctx[r], wo(r)[:, n : n + TILE])
            at = pl.ds(n, TILE)
            abuf[:, at] = x[:, at].astype(F32) + total + brow[:, AT_OUT + n : AT_OUT + n + TILE]
        row_tiles(norm_first, 0)

    def expand(o):
        ready(2, o)
        r = rank(o)
        for n in range(0, F, TILE):
            bias = brow[:, pl.ds(pl.multiple_of(AT_HIDDEN + r * F + n, PAIR), TILE)]
            pre = nn(low[...], w1(r)[:, n : n + TILE]) + bias
            cdf = 0.5 * (1.0 + lax.erf(pre * 0.5**0.5))
            density = jnp.exp(-0.5 * pre * pre) * 0.3989422804014327
            hid[r, :, pl.ds(n, TILE)] = (pre * cdf).astype(BF16)
            gp[r, :, pl.ds(n, TILE)] = (cdf + pre * density).astype(BF16)

    def reduce(o):
        ready(3, o)
        r = rank(o)
        for n in range(0, D, TILE):
            at = pl.ds(n, TILE)
            bbuf[:, at] = bbuf[:, at] + nn(hid[r], w2(r)[:, n : n + TILE])

    if quads:
        whole = [(k + 1) * SUBS + LAG - 1 for k in range(rounds - 1)] + [steps + LAG - 1]
        plan = [
            (project, [PLAN[0], PLAN[1], whole[0], whole[0] + 2]),
            (attend_rank, [PLAN[2], PLAN[3], whole[0] + 1, whole[0] + 3]),
            (expand, [whole[1] + 1, whole[1] + 2, whole[2], whole[2] + 1]),
            (reduce, [whole[1] + 3, whole[1] + 4]),
        ]

        def pass_on(place_in_chain, sem, to, s):
            @pl.when(s == 2 * place_in_chain)
            def _():
                @pl.when(place_in_chain > 0)
                def _():
                    pl.semaphore_wait(sem, 1)

                @pl.when(place_in_chain < links - 1)
                def _():
                    pl.semaphore_signal(sem, inc=1, device_id=to, device_id_type=MESH_ID)

        def step(s, carry):
            service(s, 0)
            pass_on(link, sem_up, after, s)
            pass_on(links - 1 - link, sem_down, before, s)

            @pl.when(s == whole[1])
            def _():
                finish_attention()

            for part, at_steps in plan:
                o = jnp.int32(-1)
                for k, at_step in enumerate(at_steps):
                    if at_step < whole[3]:
                        o = jnp.where(s == at_step, k, o)

                @pl.when(o >= 0)
                def _():
                    part(o)

            return carry

        lax.fori_loop(0, whole[3] + 1, step, 0)
        lax.fori_loop(2, T, lambda o, c: (reduce(o), c)[1], 0)
    else:

        def each_rank(part):
            lax.fori_loop(0, T, lambda o, c: (part(o), c)[1], 0)

        each_rank(project)
        each_rank(attend_rank)
        finish_attention()
        each_rank(expand)
        each_rank(reduce)

    nought_row = jnp.zeros((1, D), F32)
    og_copy.wait()

    def norm_second(at, carry):
        sum_up, sum_second = carry
        values = bbuf[at]
        centred = values - row_mean(values)
        root = lax.rsqrt(row_mean(centred * centred) + EPS_NORM)
        normed = centred * root
        out[at] = (normed * gain2[...] + brow[:, AT_SECOND : AT_SECOND + D]).astype(BF16)
        upstream = og[at].astype(F32)
        weighted = upstream * gain2[...]
        grad = root * (weighted - row_mean(weighted) - normed * row_mean(weighted * normed))
        bbuf[at] = grad
        low[at] = grad.astype(BF16)
        return (
            sum_up + jnp.sum(upstream, axis=0, keepdims=True),
            sum_second + jnp.sum(grad, axis=0, keepdims=True),
        )

    sum_up, sum_second = row_tiles(norm_second, (nought_row, nought_row))
    out_copy = pltpu.make_async_copy(out, out_hbm, sem_out.at[0])
    out_copy.start()
    bsum[:, AT_SECOND : AT_SECOND + D] = sum_up
    bsum[:, AT_FFN : AT_FFN + D] = sum_second

    def ffn_back(r, carry):
        for n in range(0, F, TILE):
            grad = nt(low[...], w2(r)[n : n + TILE, :]) * gp[r, :, pl.ds(n, TILE)].astype(F32)
            at = pl.ds(pl.multiple_of(AT_HIDDEN + r * F + n, PAIR), TILE)
            bsum[:, at] = jnp.sum(grad, axis=0, keepdims=True)
            hid[r, :, pl.ds(n, TILE)] = grad.astype(BF16)
        return carry

    lax.fori_loop(0, T, ffn_back, 0)
    for n in range(0, D, TILE):
        total = nt(hid[0], w1(0)[n : n + TILE, :])
        for r in range(1, T):
            total = total + nt(hid[r], w1(r)[n : n + TILE, :])
        cbuf[:, pl.ds(n, TILE)] = total

    def first_back(at, carry):
        sum_normed, sum_first = carry
        grad = bbuf[at] + cbuf[at]
        normed = abuf[at]
        weighted = grad * gain1[...]
        first = r1buf[at] * (
            weighted - row_mean(weighted) - normed * row_mean(weighted * normed)
        )
        bbuf[at] = first
        low[at] = first.astype(BF16)
        return (
            sum_normed + jnp.sum(grad, axis=0, keepdims=True),
            sum_first + jnp.sum(first, axis=0, keepdims=True),
        )

    sum_normed, sum_first = row_tiles(first_back, (nought_row, nought_row))
    bsum[:, AT_FIRST : AT_FIRST + D] = sum_normed
    bsum[:, AT_OUT : AT_OUT + D] = sum_first

    class Totals:
        def __init__(self, number, start, amount, group, everyone):
            self.number, self.at = number, pl.ds(start, amount)
            self.group, self.everyone = group, everyone

        def copies(self, buffer, sems, me, peers):
            send, recv = sems
            return [
                remote(
                    buffer.at[me],
                    buffer.at[me],
                    send.at[self.number, k],
                    recv.at[self.number, me],
                    device,
                )
                for k, device in enumerate(peers)
            ]

        def gather(self, buffer, sems, me, peers):
            for copy in self.copies(buffer, sems, me, peers):
                copy.wait_send()
            for k in range(buffer.shape[0]):

                @pl.when(k != me)
                def _():
                    remote(
                        buffer.at[k], buffer.at[k], sems[0].at[0, 0], sems[1].at[self.number, k], peers[0]
                    ).wait_recv()

            total = buffer[0]
            for k in range(1, buffer.shape[0]):
                total = total + buffer[k]
            return total

        def start(self):
            self.group[t] = bsum[:, self.at]
            for copy in self.copies(self.group, (sem_as, sem_ar), t, in_group):
                copy.start()

        def middle(self):
            self.everyone[dp] = self.gather(self.group, (sem_as, sem_ar), t, in_group)
            for copy in self.copies(self.everyone, (sem_bs, sem_br), dp, in_dp):
                copy.start()

        def finish(self):
            bsum[:, self.at] = self.gather(self.everyone, (sem_bs, sem_br), dp, in_dp)

    in_group = [peer(o) for o in range(1, T)]
    in_dp = [((dp + o) % lay.dp_size, t) for o in range(1, lay.dp_size)]
    early = Totals(0, AT_VALUE, FLAT - AT_VALUE, group_early, all_early)
    late = Totals(1, AT_QUERY, AT_VALUE, group_late, all_late)

    for r in range(T):
        grad = nt(low[...], wo(r)[...]).astype(BF16)
        cgrad[r] = grad
        bsum[:, AT_VALUE + r * W : AT_VALUE + (r + 1) * W] = jnp.sum(
            grad.astype(F32), axis=0, keepdims=True
        )
    early.start()

    lone = jnp.where(place(1)[1] != place(0)[1], 0, NB - 1)
    pair_at = jnp.where(lone == 0, 1, 0)
    slot_pair = (NB * t + pair_at) // NU - row0
    slot_lone = (NB * t + lone) // NU - row0
    slot_kept = jnp.where(has_b, slot_pair, 1)

    def attend_back(r, i, first_block, amount, slot):
        hp = r * PP + i
        lanes = pl.ds(i * PAIR, PAIR)
        queries, upstreams, deltas = [], [], []
        for k in range(amount):
            at = rows_at(first_block + k)
            scaled = cgrad[r, at, lanes].astype(F32) * linv[hp, at]
            upstreams.append(split_heads(scaled.astype(BF16)))
            deltas.append(split_heads(scaled * ctx[r, at, lanes].astype(F32)))
            queries.append(split_heads(qbuf[hp, at]))
        upstream, query = jnp.concatenate(upstreams), jnp.concatenate(queries)
        delta = jnp.sum(jnp.concatenate(deltas), axis=1, keepdims=True)
        probs = pbuf[hp, pl.ds(pl.multiple_of(first_block * 2 * B, 2 * B), amount * 2 * B)]
        score = (probs.astype(F32) * (nt(upstream, vbuf[hp, slot]) - delta)).astype(BF16)
        value_grad = nn(upstream.T, probs)
        key_grad = nn(query.T, score)
        joined = nn(score, kbuf[hp, slot]) * HD**-0.5
        total = jnp.zeros((1, PAIR), F32)
        for k in range(amount):
            grad = join_heads(joined[k * 2 * B : (k + 1) * 2 * B])
            qbuf[hp, rows_at(first_block + k)] = grad.astype(BF16)
            total = total + jnp.sum(grad, axis=0, keepdims=True)
        return key_grad.astype(BF16).T, value_grad.astype(BF16).T, total

    def rank_back_pair(r, carry):
        for i in range(PP):
            keys, values, total = attend_back(r, i, pair_at, 2, slot_pair)
            kbuf[r * PP + i, slot_kept] = keys
            vbuf[r * PP + i, slot_kept] = values
            bsum[:, pl.ds(pl.multiple_of(AT_QUERY + r * W + i * PAIR, PAIR), PAIR)] = total

        @pl.when(r == T // 2 - 1)
        def _():
            early.middle()

        return carry

    def rank_back_lone(r, carry):
        for i in range(PP):
            hp = r * PP + i
            keys, values, total = attend_back(r, i, lone, 1, slot_lone)
            at = pl.ds(pl.multiple_of(AT_QUERY + r * W + i * PAIR, PAIR), PAIR)
            bsum[:, at] = bsum[:, at] + total
            kept = [jnp.where(has_b, jnp.zeros_like(keys), buf[hp, 1]) for buf in (kbuf, vbuf)]
            kbuf[hp, slot_lone] = keys + kept[0]
            vbuf[hp, slot_lone] = values + kept[1]
        return carry

    def wide(buffer, r, *at):
        return jnp.concatenate([buffer[(r * PP + i, *at)] for i in range(PP)], axis=1)

    half = SEQ // 2

    def share_copy(slot, w, k):
        u = (row0 + slot) * NU + w
        owner = u // NB
        first = (row0 + slot) * NU // NB
        place_of = t - first - jnp.where(t > owner, 1, 0)
        number = (u - owner * NB) * (lay.span - 1) + place_of
        at = pl.ds(pl.multiple_of(k * TILE, TILE), TILE)
        return remote(
            xkv.at[slot, rows_at(w), at],
            back.at[number, :, at],
            sem_gs.at[slot * NU + w, k],
            sem_gr.at[number, k],
            (dp, owner),
        )

    def send_shares(slot, rows, first_unit, amount):
        def body(k, carry):
            at = pl.ds(pl.multiple_of(k * TILE, TILE), TILE)
            total = nt(wide(kbuf, 0, slot, rows), wqkv[0, 1, at])
            total = total + nt(wide(vbuf, 0, slot, rows), wqkv[0, 2, at])
            for r in range(1, T):
                total = total + nt(wide(kbuf, r, slot, rows), wqkv[r, 1, at])
                total = total + nt(wide(vbuf, r, slot, rows), wqkv[r, 2, at])
            xkv[slot, rows, at] = total.astype(BF16)
            for n in range(amount):
                w = first_unit + n
                owner = ((row0 + slot) * NU + w) // NB

                @pl.when(owner != t)
                def _():
                    share_copy(slot, w, k).start()

            return carry

        lax.fori_loop(0, D // TILE, body, 0)

    def send_half(slot, part):
        rows = pl.ds(pl.multiple_of(part * half, half), half)
        send_shares(slot, rows, part * (NU // 2), NU // 2)

    lax.fori_loop(0, T, rank_back_pair, 0)
    part_first = jnp.where(lone == 0, 1, 0)

    lax.fori_loop(0, T, rank_back_lone, 0)
    late.start()

    def halves(k, carry):
        @pl.when(has_b)
        def _():
            send_half(slot_pair, (part_first + k) % 2)

        return carry

    lax.fori_loop(0, 2, halves, 0)
    late.middle()
    send_shares(slot_lone, pl.ds(0, SEQ), 0, NU)

    for n in range(0, D, TILE):
        total = nt(wide(qbuf, 0), wqkv[0, 0, pl.ds(n, TILE)])
        for r in range(1, T):
            total = total + nt(wide(qbuf, r), wqkv[r, 0, pl.ds(n, TILE)])
        at = pl.ds(n, TILE)
        bbuf[:, at] = bbuf[:, at] + total

    for j in range(NB):
        u, row, slot, w = place(j)
        bbuf[block_at(j)] = bbuf[block_at(j)] + xkv[slot, rows_at(w)].astype(F32)
    early.finish()

    for j in range(NB):
        u, row, slot, w = place(j)
        first = row * NU // NB
        last = (row * NU + NU - 1) // NB
        for o in range(lay.span):
            dest = first + o

            @pl.when((dest <= last) & (dest != t))
            def _():
                remote(
                    x.at[block_at(j)],
                    xkv.at[0, rows_at(0)],
                    sem_hs.at[j * lay.span + o],
                    sem_hr.at[0],
                    (dp, dest),
                ).wait_send()

    if quads:
        for i in range(4):
            own_copies(i).wait_send()
        lax.fori_loop(0, steps, sent, 0)
    else:
        for i in range(4):
            for o in range(1, T):
                own_copies(i, o).wait_send()

    for j in range(NB):
        u, row, slot, w = place(j)
        first = row * NU // NB
        last = (row * NU + NU - 1) // NB
        for o in range(lay.span - 1):
            number = j * (lay.span - 1) + o

            @pl.when(first + o < last)
            def _():
                sender = first + o + jnp.where(first + o >= t, 1, 0)
                for k in range(D // TILE):
                    at = pl.ds(k * TILE, TILE)
                    remote(
                        xkv.at[0, rows_at(0), at],
                        back.at[number, :, at],
                        sem_gs.at[0, k],
                        sem_gr.at[number, k],
                        (dp, sender),
                    ).wait_recv()
                bbuf[block_at(j)] = bbuf[block_at(j)] + back[number].astype(F32)

        ig[block_at(j)] = bbuf[block_at(j)].astype(BF16)

    ig_copy = pltpu.make_async_copy(ig, ig_hbm, sem_out.at[1])
    ig_copy.start()
    late.finish()

    out_copy.wait()
    ig_copy.wait()
    for slot in range(2):
        for w in range(NU):
            owner = ((row0 + slot) * NU + w) // NB

            @pl.when((owner != t) & ((slot == 0) | has_b))
            def _():
                lax.fori_loop(0, D // TILE, lambda k, c: (share_copy(slot, w, k).wait_send(), c)[1], 0)


def layer_call(lay, *args):
    T, S = lay.ranks, lay.tokens
    hp = HEADS // 2
    vmem = pltpu.VMEM
    if lay.quads:
        wide = [
            vmem((T, lay.width + D + lay.hidden, D), BF16),
            vmem((16, PAIR), BF16),
            vmem((16, PAIR), BF16),
        ]
    else:
        wide = [
            vmem((T, lay.width, D), BF16),
            vmem((T, D, lay.hidden), BF16),
            vmem((T, lay.hidden, D), BF16),
        ]
    dma = pltpu.SemaphoreType.DMA
    steps = 3 * SUBS + LAST_SUBS
    own = 4 if lay.quads else 4 * T
    sharers = lay.blocks * max(lay.span - 1, 1)
    scratch = (
        [vmem((1, FLAT), F32)]
        + [vmem((S, D), BF16)] * 4
        + [vmem((1, D), F32)] * 2
        + [vmem((HD, BROWS), F32)]
        + [vmem((T * S,), jnp.int32)] * 2
        + [vmem((T, 3, D, lay.width), BF16)]
        + wide
        + [
            vmem((2, SEQ, D), BF16),
            vmem((hp, S, PAIR), BF16),
            vmem((hp, 2, SEQ, PAIR), BF16),
            vmem((hp, 2, SEQ, PAIR), BF16),
            vmem((hp, lay.blocks * 2 * lay.block, SEQ), BF16),
            vmem((hp, S, PAIR), F32),
            vmem((lay.blocks, lay.block, SEQ), F32),
            vmem((T, S, lay.width), BF16),
            vmem((T, S, lay.width), BF16),
            vmem((S, D), F32),
            vmem((S, D), F32),
            vmem((S, D), F32),
            vmem((S, 1), F32),
            vmem((S, D), BF16),
            vmem((T, S, lay.hidden), BF16),
            vmem((T, S, lay.hidden), BF16),
            vmem((sharers, lay.block, D), BF16),
            vmem((T, 1, FLAT - AT_VALUE), F32),
            vmem((T, 1, AT_VALUE), F32),
            vmem((lay.dp_size, 1, FLAT - AT_VALUE), F32),
            vmem((lay.dp_size, 1, AT_VALUE), F32),
            dma((4,)),
            dma((9,)),
            dma((own,)),
            dma((own,)),
            dma((steps + DIRECT,)),
            dma((steps,)),
            dma((steps,)),
            dma((3 * steps,)),
            dma((3 * steps,)),
            dma((3 * steps,)),
            dma((lay.blocks * lay.span,)),
            dma((2 * lay.units,)),
            dma((2 * lay.units, D // TILE)),
            dma((sharers, D // TILE)),
            dma((2, T)),
            dma((2, T)),
            dma((2, lay.dp_size)),
            dma((2, lay.dp_size)),
            pltpu.SemaphoreType.REGULAR,
            pltpu.SemaphoreType.REGULAR,
        ]
    )
    in_vmem = pl.BlockSpec(memory_space=pltpu.VMEM)
    anywhere = pl.BlockSpec(memory_space=pl.ANY)
    return pl.pallas_call(
        partial(layer_kernel, lay),
        out_shape=(
            jax.ShapeDtypeStruct((S, D), BF16),
            jax.ShapeDtypeStruct((S, D), BF16),
            jax.ShapeDtypeStruct((1, FLAT), F32),
        ),
        in_specs=[anywhere] * 11,
        out_specs=(anywhere, anywhere, in_vmem),
        scratch_shapes=scratch,
        compiler_params=pltpu.CompilerParams(
            collective_id=0, has_side_effects=True, vmem_limit_bytes=VMEM_BYTES
        ),
        name="layer",
    )(*args)


VMEM_BYTES = 63 * 2**20
PLAN = [2, 5, 3, 6]
PARTS = 4


def update_kernel(
    raw,
    biases,
    moment_one,
    moment_two,
    left_pairs,
    left_hidden,
    left_small,
    right_bases,
    owners,
    out_in,
    ig_in,
    clipped_out,
    norm_out,
    new_out,
    copies_out,
    one_out,
    two_out,
    out_out,
    ig_out,
    rows,
    left,
    wide,
    sems,
):
    amount = out_in.shape[0] // PARTS
    parts = [pl.ds(k * amount, amount) for k in range(PARTS)]
    fetches = [
        pltpu.make_async_copy(src.at[at], wide.at[i, at], sems.at[0, i, k])
        for i, src in enumerate((out_in, ig_in))
        for k, at in enumerate(parts)
    ]
    stores = [
        pltpu.make_async_copy(wide.at[i, at], dst.at[at], sems.at[1, i, k])
        for i, dst in enumerate((out_out, ig_out))
        for k, at in enumerate(parts)
    ]
    for fetch in fetches:
        fetch.start()
    sums = raw[...]
    norm = jnp.sqrt(jnp.sum(sums * sums, keepdims=True))
    norm_out[...] = norm
    for i in range(BROWS):
        rows[i : i + 1] = sums[:, i * HD : (i + 1) * HD]
    clipped = rows[...].T * (CLIP_LIMIT / jnp.maximum(norm, CLIP_LIMIT))
    clipped_out[...] = clipped
    dp = lax.axis_index("dp")
    tail = 2 * HEADS + FR
    layout = [(0, 2 * HEADS, left_pairs), (2 * HEADS, FR, left_hidden)]
    layout += [(tail + k * DR, DR, left_small.at[k]) for k in range(4)]
    left[...] = jnp.zeros_like(left)
    for begin, amount, basis in layout:
        left[begin : begin + amount, begin : begin + amount] = basis[...]
    for fetch, store in zip(fetches, stores):
        fetch.wait()
        store.start()
    column = lax.broadcasted_iota(jnp.int32, (HD, BROWS), 1)

    def per_matrix(choose):
        result = choose(0)
        for k in range(1, len(layout)):
            result = jnp.where(column >= layout[k][0], choose(k), result)
        return result

    def product(a, b, over_a, over_b):
        return lax.dot_general(
            a,
            b,
            (((over_a,), (over_b,)), ((), ())),
            precision=HIGHEST,
            preferred_element_type=F32,
        )

    half = product(clipped, left[...], 1, 0)
    rotated = per_matrix(lambda k: product(right_bases[k], half, 0, 0))
    one = BETA_ONE * moment_one[...] + (1.0 - BETA_ONE) * rotated
    two = BETA_TWO * moment_two[...] + (1.0 - BETA_TWO) * rotated * rotated
    direction = (
        one / (1.0 - BETA_ONE**STEP) / (jnp.sqrt(two / (1.0 - BETA_TWO**STEP)) + ADAM_EPS)
    )
    half = per_matrix(lambda k: product(right_bases[k], direction, 1, 0))
    new = biases[...] - LEARN_RATE * product(half, left[...], 1, 1)
    copies_out[...] = new.astype(BF16)
    mine = per_matrix(lambda k: jnp.where(owners[k] == dp, 1.0, 0.0)) > 0.5
    new_out[...] = jnp.where(mine, new, 0.0)
    one_out[...] = jnp.where(mine, one, 0.0)
    two_out[...] = jnp.where(mine, two, 0.0)
    for store in stores:
        store.wait()


def update_call(tokens, *args):
    in_vmem = pl.BlockSpec(memory_space=pltpu.VMEM)
    anywhere = pl.BlockSpec(memory_space=pl.ANY)
    block = jax.ShapeDtypeStruct((HD, BROWS), F32)
    wide = jax.ShapeDtypeStruct((tokens, D), BF16)
    return pl.pallas_call(
        update_kernel,
        out_shape=(
            block,
            jax.ShapeDtypeStruct((1, 1), F32),
            block,
            jax.ShapeDtypeStruct((HD, BROWS), BF16),
            block,
            block,
            wide,
            wide,
        ),
        in_specs=[in_vmem] * 8 + [pl.BlockSpec(memory_space=pltpu.SMEM)] + [anywhere] * 2,
        out_specs=(in_vmem,) * 6 + (anywhere,) * 2,
        scratch_shapes=[
            pltpu.VMEM((BROWS, HD), F32),
            pltpu.VMEM((BROWS, BROWS), F32),
            pltpu.VMEM((2, tokens, D), BF16),
            pltpu.SemaphoreType.DMA((2, 2, PARTS)),
        ],
        name="update",
    )(*args)


def on_device(
    dp_size,
    ranks,
    inputs,
    output_grad,
    input_project,
    output_project,
    expand_weight,
    reduce_weight,
    first_gain,
    second_gain,
    biases,
    first_moment,
    second_moment,
    left_pairs,
    left_hidden,
    left_small,
    right_bases,
    segment_number,
    token_mask,
    owners,
):
    lay = Layout(dp_size, ranks, inputs.shape[0])
    layer_out, input_grad, sums = layer_call(
        lay,
        inputs,
        output_grad,
        first_gain.reshape(1, D),
        second_gain.reshape(1, D),
        biases.T,
        segment_number,
        token_mask,
        input_project,
        output_project,
        expand_weight,
        reduce_weight,
    )
    clipped, clip_norm, new_owned, copies, first_owned, second_owned, layer_out, input_grad = (
        update_call(
            inputs.shape[0],
            sums,
            biases.T,
            first_moment.T,
            second_moment.T,
            left_pairs,
            left_hidden,
            left_small,
            right_bases,
            owners,
            layer_out,
            input_grad,
        )
    )
    return (
        layer_out,
        input_grad,
        clipped.T,
        clip_norm.reshape(1),
        new_owned.T,
        copies.T,
        first_owned.T,
        second_owned.T,
    )


def solution(mesh):
    return jax.shard_map(
        partial(on_device, mesh.shape["dp"], mesh.shape["tensor"]),
        mesh=mesh,
        in_specs=(
            P(("dp", "tensor"), None),
            P(("dp", "tensor"), None),
            P(None, None, "tensor"),
            P("tensor", None),
            P(None, "tensor"),
            P("tensor", None),
            P(),
            P(),
            P(),
            P(),
            P(),
            P(),
            P(),
            P(),
            P(),
            P("dp"),
            P("dp"),
            P(),
        ),
        out_specs=(
            P(("dp", "tensor"), None),
            P(("dp", "tensor"), None),
            P(),
            P(),
            P("dp", None),
            P(),
            P("dp", None),
            P("dp", None),
        ),
        check_vma=False,
    )
```

```python
from functools import partial

import jax
import jax.numpy as jnp
from jax import lax
from jax.experimental import pallas as pl
from jax.experimental.pallas import tpu as pltpu
from jax.sharding import PartitionSpec as P

D = 1024
HEADS = 16
HD = 64
PAIR = 2 * HD
SEQ = 512
STEP = 10
FR = 64
DR = 16
BROWS = 160
AT_QUERY, AT_VALUE, AT_HIDDEN = 0, D, 2 * D
AT_OUT = 2 * D + FR * HD
AT_FIRST, AT_FFN, AT_SECOND = AT_OUT + D, AT_OUT + 2 * D, AT_OUT + 3 * D
FLAT = BROWS * HD

EPS_NORM = 1e-12
CLIP_LIMIT = 64.0
BETA_ONE = 0.9
BETA_TWO = 0.99
ADAM_EPS = 1e-08
LEARN_RATE = 0.2
HIGHEST = lax.Precision.HIGHEST
MESH_ID = pl.DeviceIdType.MESH
BF16 = jnp.bfloat16
F32 = jnp.float32

SUBS = 4
LAST_SUBS = 4
DIRECT = 2
RELAY_LAG, LAG = 2, 4
UNIT = 256
TILE = 256


def nn(a, b):
    return jnp.dot(a, b, preferred_element_type=F32)


def nt(a, b):
    return lax.dot_general(a, b, (((1,), (1,)), ((), ())), preferred_element_type=F32)


def tn(a, b):
    return lax.dot_general(a, b, (((0,), (0,)), ((), ())), preferred_element_type=F32)


def flip(value, bit):
    return value + bit - 2 * bit * ((value // bit) % 2)


class Layout:
    def __init__(self, dp_size, ranks, tokens):
        self.dp_size, self.ranks, self.tokens = dp_size, ranks, tokens
        self.block = 1
        while tokens % (2 * self.block) == 0 and SEQ % (2 * self.block) == 0:
            self.block *= 2
        self.blocks = tokens // self.block
        self.units = SEQ // self.block
        self.width = D // ranks
        self.pairs = self.width // PAIR
        self.hidden = FR * HD // ranks
        rows = ranks * tokens // SEQ
        self.span = 1
        for row in range(rows):
            first = row * self.units // self.blocks
            last = (row * self.units + self.units - 1) // self.blocks
            self.span = max(self.span, last - first + 1)
        self.quads = ranks == 4 and dp_size % 4 == 0


def layer_kernel(
    lay,
    x_hbm,
    og_hbm,
    gain1_hbm,
    gain2_hbm,
    biases_hbm,
    seg_hbm,
    val_hbm,
    wqkv_in,
    wo_in,
    w1_in,
    w2_in,
    out_hbm,
    ig_hbm,
    bsum,
    brow,
    x,
    og,
    out,
    ig,
    gain1,
    gain2,
    biases_t,
    seg,
    val,
    wqkv,
    wo_b,
    w1_b,
    w2_b,
    xkv,
    qbuf,
    kbuf,
    vbuf,
    pbuf,
    linv,
    mask,
    ctx,
    cgrad,
    abuf,
    bbuf,
    cbuf,
    r1buf,
    low,
    hid,
    gp,
    back,
    group_early,
    group_late,
    all_early,
    all_late,
    sem_local,
    sem_out,
    sem_own_s,
    sem_own_r,
    sem_y,
    sem_x,
    sem_z,
    sem_c,
    sem_w,
    sem_p,
    sem_hs,
    sem_hr,
    sem_gs,
    sem_gr,
    sem_as,
    sem_ar,
    sem_bs,
    sem_br,
    sem_up,
    sem_down,
):
    T, S, B, NB, NU = lay.ranks, lay.tokens, lay.block, lay.blocks, lay.units
    W, PP, F = lay.width, lay.pairs, lay.hidden
    dp = lax.axis_index("dp")
    t = lax.axis_index("tensor")
    quads = lay.quads

    def rank(o):
        r = (t + o) % 2
        if T > 2:
            r = r + 2 * ((t // 2 + o // 2) % 2)
        if T > 4:
            r = r + 4 * ((t // 4 + o // 4) % 2)
        return r

    if quads:
        big = wo_b

        def wo(r):
            return big.at[r, pl.ds(0, W)]

        def w1(r):
            return big.at[r, pl.ds(W, D)]

        def w2(r):
            return big.at[r, pl.ds(W + D, F)]
    else:

        def wo(r):
            return wo_b.at[r]

        def w1(r):
            return w1_b.at[r]

        def w2(r):
            return w2_b.at[r]

    def pieces(r):
        return [wqkv.at[r], wo(r), w1(r), w2(r)]

    sources = [wqkv_in, wo_in, w1_in, w2_in]

    def peer(o):
        return (dp, rank(o))

    def remote(src, dst, send, recv, device):
        return pltpu.make_async_remote_copy(
            src_ref=src,
            dst_ref=dst,
            send_sem=send,
            recv_sem=recv,
            device_id=device,
            device_id_type=MESH_ID,
        )

    barrier = pltpu.get_barrier_semaphore()
    others = [peer(o) for o in range(1, T)]
    heard = T - 1

    def greet(device):
        pl.semaphore_signal(barrier, inc=1, device_id=device, device_id_type=MESH_ID)

    if quads:
        others.append((flip(dp, 1), t))
        link, links = dp // 2, lay.dp_size // 2
        before, after = (dp - 2, t), (dp + 2, t)

        @pl.when(link > 0)
        def _():
            greet(before)

        @pl.when(link < links - 1)
        def _():
            greet(after)

        heard = heard + 1 + jnp.where(link > 0, 1, 0) + jnp.where(link < links - 1, 1, 0)
    else:
        others += [((dp + o) % lay.dp_size, t) for o in range(1, lay.dp_size)]
        heard = len(others)
    for device in others:
        greet(device)
    local = [
        pltpu.make_async_copy(src, dst, sem_local.at[i])
        for i, (src, dst) in enumerate(zip(sources, pieces(t)))
    ]
    x_copy = pltpu.make_async_copy(x_hbm, x, sem_out.at[3])
    x_copy.start()
    for copy in local:
        copy.start()
    og_copy = pltpu.make_async_copy(og_hbm, og, sem_out.at[2])
    og_copy.start()
    small = [
        pltpu.make_async_copy(src, dst, sem_out.at[4 + i])
        for i, (src, dst) in enumerate(
            [
                (biases_hbm, biases_t),
                (seg_hbm, seg),
                (val_hbm, val),
                (gain1_hbm, gain1),
                (gain2_hbm, gain2),
            ]
        )
    ]
    for copy in small:
        copy.start()

    row0 = (NB * t) // NU
    has_b = (NB * t + NB - 1) // NU != row0

    def place(j):
        u = NB * t + j
        row = u // NU
        return u, row, row - row0, u - row * NU

    def rows_at(w):
        return pl.ds(pl.multiple_of(w * B, B), B)

    def block_at(j):
        return pl.ds(j * B, B)

    pl.semaphore_wait(barrier, heard)

    x_copy.wait()

    def send_rows():
        for j in range(NB):
            u, row, slot, w = place(j)
            first = row * NU // NB
            last = (row * NU + NU - 1) // NB
            for o in range(lay.span):
                dest = first + o

                @pl.when((dest <= last) & (dest != t))
                def _():
                    remote(
                        x.at[block_at(j)],
                        xkv.at[row - (NB * dest) // NU, rows_at(w)],
                        sem_hs.at[j * lay.span + o],
                        sem_hr.at[(row - (NB * dest) // NU) * NU + w],
                        (dp, dest),
                    ).start()

    if quads:
        role = dp % 4
        relay = role == 3
        gy = role % 3
        gx = jnp.where(role == 1, 0, jnp.where(role == 3, 2, 1))
        gz = jnp.where(role == 2, 0, jnp.where(role == 3, 1, 2))
        far = rank(2)
        core, ynext = (dp, rank(1)), (dp, rank(2))
        xnext, znext = (flip(dp, 1), t), (flip(dp, 2), t)
        rounds = 4
        tail_step = (rounds - 1) * SUBS
        steps = tail_step + LAST_SUBS
        part_a, part_b, part_c = D // SUBS, UNIT // SUBS, UNIT // LAST_SUBS

        def chunk(idx, g, fn):
            n = g * steps + idx

            @pl.when((idx >= 0) & (idx < SUBS))
            def _():
                at = pl.ds(pl.multiple_of(idx * part_a, part_a), part_a)
                fn(lambda r: wqkv.at[r, g, at], n)

            @pl.when((idx >= SUBS) & (idx < tail_step))
            def _():
                row = ((idx // SUBS - 1) * 3 + g) * UNIT + (idx % SUBS) * part_b
                at = pl.ds(pl.multiple_of(row, part_b), part_b)
                fn(lambda r: big.at[r, at], n)

            @pl.when((idx >= tail_step) & (idx < steps))
            def _():
                row = ((rounds - 2) * 3 + g) * UNIT + (idx - tail_step) * part_c
                at = pl.ds(pl.multiple_of(row, part_c), part_c)
                fn(lambda r: big.at[r, at], n)

        relayed = steps - DIRECT
        g_direct = jnp.where(role == 1, 2, 1)
        is_served = (role == 1) | (role == 2)

        def send_y(idx):
            def go(view, n):
                remote(view(t), view(t), sem_y.at[idx], sem_w.at[n], ynext).start()

            chunk(idx, gy, go)

            def go_direct(view, n):
                remote(
                    view(t), view(t), sem_y.at[idx + DIRECT], sem_w.at[n], ynext
                ).start()

            @pl.when((idx >= relayed) & is_served)
            def _():
                chunk(idx, g_direct, go_direct)

        def to_core(view, n):
            remote(view(far), view(far), sem_c.at[n], sem_p.at[n], core).start()

        def arrived(view, n):
            remote(view(far), view(far), sem_c.at[n], sem_w.at[n], core).wait_recv()

        def to_x(view, n, idx):
            remote(view(far), view(far), sem_x.at[idx], sem_w.at[n], xnext).start()

        def to_z(view, n, idx):
            remote(view(far), view(far), sem_z.at[idx], sem_w.at[n], znext).start()

        def service(s, carry):
            def from_y(view, n):
                arrived(view, n)

                @pl.when(role != 3)
                def _():
                    to_x(view, n, s)
                    to_z(view, n, s)

                to_core(view, n)

            chunk(s, gy, from_y)
            send_y(s + SUBS)
            late = s - jnp.where(relay, RELAY_LAG, LAG)

            def from_x(view, n):
                arrived(view, n)

                @pl.when(relay & (late < relayed))
                def _():
                    to_z(view, n, late)

                to_core(view, n)

            def from_z(view, n):
                arrived(view, n)

                @pl.when(relay & (late < relayed))
                def _():
                    to_x(view, n, late)

                to_core(view, n)

            chunk(late, gx, from_x)
            chunk(late, gz, from_z)
            return carry

        def sent(idx, carry):
            def go(view, n):
                remote(view(t), view(t), sem_y.at[idx], sem_w.at[n], ynext).wait_send()

                @pl.when((role != 3) | (idx < relayed))
                def _():
                    remote(view(t), view(t), sem_x.at[idx], sem_w.at[n], xnext).wait_send()
                    remote(view(t), view(t), sem_z.at[idx], sem_w.at[n], znext).wait_send()

                @pl.when((idx >= relayed) & is_served)
                def _():
                    remote(
                        view(t), view(t), sem_y.at[idx + DIRECT], sem_w.at[n], ynext
                    ).wait_send()

                for g in range(3):
                    m = g * steps + idx
                    remote(view(t), view(t), sem_c.at[m], sem_p.at[m], core).wait_send()

            chunk(idx, gy, go)
            return carry

        def from_partner(units):
            for unit in units:
                p, g = unit // 3, unit % 3
                if p == 0:
                    view = wqkv.at[rank(3), 0, pl.ds(0, part_a)]
                else:
                    view = big.at[rank(3), pl.ds(0, part_c if p == rounds - 1 else part_b)]

                def go(idx, carry):
                    n = g * steps + idx
                    remote(view, view, sem_c.at[n], sem_p.at[n], core).wait_recv()
                    return carry

                if p == rounds - 1:
                    lax.fori_loop(tail_step, steps, go, 0)
                else:
                    lax.fori_loop(p * SUBS, (p + 1) * SUBS, go, 0)

        def own_copies(i):
            return remote(sources[i], pieces(t)[i], sem_own_s.at[i], sem_own_r.at[i], core)

        local[0].wait()
        lax.fori_loop(0, 2, lambda i, c: (send_y(i), c)[1], 0)
        send_rows()
        lax.fori_loop(2, SUBS, lambda i, c: (send_y(i), c)[1], 0)
        for i in range(4):
            own_copies(i).start()
        for i in range(1, 4):
            local[i].wait()

        first_unit = [0, 3, 4, 8, 12]

        def ready(i, o):
            @pl.when(o == 1)
            def _():
                remote(
                    sources[i], pieces(rank(1))[i], sem_own_s.at[i], sem_own_r.at[i], core
                ).wait_recv()

            @pl.when(o == 3)
            def _():
                from_partner(range(first_unit[i], first_unit[i + 1]))

    else:

        def own_copies(i, o):
            n = i * T + o
            return remote(sources[i], pieces(t)[i], sem_own_s.at[n], sem_own_r.at[n], peer(o))

        send_rows()
        for i in range(4):
            for o in range(1, T):
                own_copies(i, o).start()

        def ready(i, o):
            @pl.when(o == 0)
            def _():
                local[i].wait()

            @pl.when(o != 0)
            def _():
                n = i * T + o
                remote(
                    sources[i], pieces(rank(o))[i], sem_own_s.at[n], sem_own_r.at[n], peer(o)
                ).wait_recv()

    for copy in small:
        copy.wait()
    key_at = lax.broadcasted_iota(jnp.int32, (B, SEQ), 1)
    query_at = lax.broadcasted_iota(jnp.int32, (B, SEQ), 0)
    for j in range(NB):
        u, row, slot, w = place(j)
        keys_here = pl.ds(pl.multiple_of(row * SEQ, SEQ), SEQ)
        numbers = seg[keys_here].reshape(1, SEQ).astype(F32)
        keyed = jnp.where(val[keys_here].reshape(1, SEQ) == 1, numbers, -1.0)
        same = key_at == query_at + w * B
        own = jnp.sum(jnp.where(same, numbers, 0.0), axis=1, keepdims=True)
        mask[j] = jnp.where((own == keyed) | same, 0.0, -1e30)
        xkv[slot, rows_at(w)] = x[block_at(j)]

    bias_rows = biases_t[...].T
    for i in range(BROWS):
        brow[:, i * HD : (i + 1) * HD] = bias_rows[i : i + 1]

    head_lane = lax.broadcasted_iota(jnp.int32, (B, PAIR), 1) < HD

    def split_heads(values):
        nought = jnp.zeros_like(values)
        return jnp.concatenate(
            [jnp.where(head_lane, values, nought), jnp.where(head_lane, nought, values)], axis=0
        )

    def join_heads(values):
        return jnp.where(head_lane, values[:B], values[B:])

    ones = jnp.ones((SEQ, PAIR), BF16)

    slot_first = jnp.where(has_b & (t % 4 == 2), 1, 0)

    def project_query(r):
        bias = brow[:, pl.ds(pl.multiple_of(AT_QUERY + r * W, PAIR), W)]
        query = ((nn(x[...], wqkv[r, 0]) + bias) * HD**-0.5).astype(BF16)
        for i in range(PP):
            qbuf[r * PP + i] = query[:, i * PAIR : (i + 1) * PAIR]

    def project_keys(o, r):
        bias = brow[:, pl.ds(pl.multiple_of(AT_VALUE + r * W, PAIR), W)]

        def body(turn, carry):
            slot = (slot_first + turn) % 2

            @pl.when((slot == 0) | has_b)
            def _():
                for w in range(NU):
                    owner = ((row0 + slot) * NU + w) // NB

                    @pl.when((owner != t) & (o == 0))
                    def _():
                        remote(
                            x.at[block_at(0)],
                            xkv.at[slot, rows_at(w)],
                            sem_hs.at[0],
                            sem_hr.at[slot * NU + w],
                            (dp, owner),
                        ).wait_recv()

                rows = xkv[slot]
                keys = nn(rows, wqkv[r, 1]).astype(BF16)
                values = (nn(rows, wqkv[r, 2]) + bias).astype(BF16)
                for i in range(PP):
                    kbuf[r * PP + i, slot] = keys[:, i * PAIR : (i + 1) * PAIR]
                    vbuf[r * PP + i, slot] = values[:, i * PAIR : (i + 1) * PAIR]

            return carry

        lax.fori_loop(0, 2, body, 0)

    def attend(r, i):
        hp = r * PP + i
        for j in range(NB):
            u, row, slot, w = place(j)
            query = split_heads(qbuf[hp, block_at(j)])
            hide = mask[j]
            scores = nt(query, kbuf[hp, slot]) + jnp.concatenate([hide, hide], axis=0)
            peak = jnp.max(scores, axis=1, keepdims=True)
            probs = jnp.exp(scores - peak).astype(BF16)
            pbuf[hp, j * 2 * B : (j + 1) * 2 * B] = probs
            mixed = nn(probs, jnp.concatenate([vbuf[hp, slot], ones], axis=1))
            inverse = 1.0 / join_heads(mixed[:, PAIR:])
            linv[hp, block_at(j)] = inverse
            ctx[r, block_at(j), pl.ds(i * PAIR, PAIR)] = (
                join_heads(mixed[:, :PAIR]) * inverse
            ).astype(BF16)

    def project(o):
        ready(0, o)
        r = rank(o)
        project_query(r)
        project_keys(o, r)

    def attend_rank(o):
        for i in range(PP):
            attend(rank(o), i)

    def row_mean(values):
        return jnp.mean(values, axis=1, keepdims=True)

    def row_tiles(body, carry):
        for j in range(NB):
            carry = body(block_at(j), carry)
        return carry

    def norm_first(at, carry):
        values = abuf[at]
        centred = values - row_mean(values)
        root = lax.rsqrt(row_mean(centred * centred) + EPS_NORM)
        normed = centred * root
        r1buf[at] = root
        abuf[at] = normed
        first_normed = normed * gain1[...] + brow[:, AT_FIRST : AT_FIRST + D]
        low[at] = first_normed.astype(BF16)
        bbuf[at] = first_normed + brow[:, AT_FFN : AT_FFN + D]
        return carry

    def finish_attention():
        for o in range(T):
            ready(1, o)
        for n in range(0, D, TILE):
            total = nn(ctx[0], wo(0)[:, n : n + TILE])
            for r in range(1, T):
                total = total + nn(ctx[r], wo(r)[:, n : n + TILE])
            at = pl.ds(n, TILE)
            abuf[:, at] = x[:, at].astype(F32) + total + brow[:, AT_OUT + n : AT_OUT + n + TILE]
        row_tiles(norm_first, 0)

    def expand(o):
        ready(2, o)
        r = rank(o)
        for n in range(0, F, TILE):
            bias = brow[:, pl.ds(pl.multiple_of(AT_HIDDEN + r * F + n, PAIR), TILE)]
            pre = nn(low[...], w1(r)[:, n : n + TILE]) + bias
            cdf = 0.5 * (1.0 + lax.erf(pre * 0.5**0.5))
            density = jnp.exp(-0.5 * pre * pre) * 0.3989422804014327
            hid[r, :, pl.ds(n, TILE)] = (pre * cdf).astype(BF16)
            gp[r, :, pl.ds(n, TILE)] = (cdf + pre * density).astype(BF16)

    def reduce(o):
        ready(3, o)
        r = rank(o)
        for n in range(0, D, TILE):
            at = pl.ds(n, TILE)
            bbuf[:, at] = bbuf[:, at] + nn(hid[r], w2(r)[:, n : n + TILE])

    if quads:
        whole = [(k + 1) * SUBS + LAG - 1 for k in range(rounds - 1)] + [steps + LAG - 1]
        plan = [
            (project, [PLAN[0], PLAN[1], whole[0], whole[0] + 2]),
            (attend_rank, [PLAN[2], PLAN[3], whole[0] + 1, whole[0] + 3]),
            (expand, [whole[1] + 1, whole[1] + 2, whole[2], whole[2] + 1]),
            (reduce, [whole[1] + 3, whole[1] + 4]),
        ]

        def pass_on(place_in_chain, sem, to, s):
            @pl.when(s == 2 * place_in_chain)
            def _():
                @pl.when(place_in_chain > 0)
                def _():
                    pl.semaphore_wait(sem, 1)

                @pl.when(place_in_chain < links - 1)
                def _():
                    pl.semaphore_signal(sem, inc=1, device_id=to, device_id_type=MESH_ID)

        def step(s, carry):
            service(s, 0)
            pass_on(link, sem_up, after, s)
            pass_on(links - 1 - link, sem_down, before, s)

            @pl.when(s == whole[1])
            def _():
                finish_attention()

            for part, at_steps in plan:
                o = jnp.int32(-1)
                for k, at_step in enumerate(at_steps):
                    if at_step < whole[3]:
                        o = jnp.where(s == at_step, k, o)

                @pl.when(o >= 0)
                def _():
                    part(o)

            return carry

        lax.fori_loop(0, whole[3] + 1, step, 0)
        lax.fori_loop(2, T, lambda o, c: (reduce(o), c)[1], 0)
    else:

        def each_rank(part):
            lax.fori_loop(0, T, lambda o, c: (part(o), c)[1], 0)

        each_rank(project)
        each_rank(attend_rank)
        finish_attention()
        each_rank(expand)
        each_rank(reduce)

    nought_row = jnp.zeros((1, D), F32)
    og_copy.wait()

    def norm_second(at, carry):
        sum_up, sum_second = carry
        values = bbuf[at]
        centred = values - row_mean(values)
        root = lax.rsqrt(row_mean(centred * centred) + EPS_NORM)
        normed = centred * root
        out[at] = (normed * gain2[...] + brow[:, AT_SECOND : AT_SECOND + D]).astype(BF16)
        upstream = og[at].astype(F32)
        weighted = upstream * gain2[...]
        grad = root * (weighted - row_mean(weighted) - normed * row_mean(weighted * normed))
        bbuf[at] = grad
        low[at] = grad.astype(BF16)
        return (
            sum_up + jnp.sum(upstream, axis=0, keepdims=True),
            sum_second + jnp.sum(grad, axis=0, keepdims=True),
        )

    sum_up, sum_second = row_tiles(norm_second, (nought_row, nought_row))
    out_copy = pltpu.make_async_copy(out, out_hbm, sem_out.at[0])
    out_copy.start()
    bsum[:, AT_SECOND : AT_SECOND + D] = sum_up
    bsum[:, AT_FFN : AT_FFN + D] = sum_second

    def ffn_back(r, carry):
        for n in range(0, F, TILE):
            grad = nt(low[...], w2(r)[n : n + TILE, :]) * gp[r, :, pl.ds(n, TILE)].astype(F32)
            at = pl.ds(pl.multiple_of(AT_HIDDEN + r * F + n, PAIR), TILE)
            bsum[:, at] = jnp.sum(grad, axis=0, keepdims=True)
            hid[r, :, pl.ds(n, TILE)] = grad.astype(BF16)
        return carry

    lax.fori_loop(0, T, ffn_back, 0, unroll=2)
    for n in range(0, D, TILE):
        total = nt(hid[0], w1(0)[n : n + TILE, :])
        for r in range(1, T):
            total = total + nt(hid[r], w1(r)[n : n + TILE, :])
        cbuf[:, pl.ds(n, TILE)] = total

    def first_back(at, carry):
        sum_normed, sum_first = carry
        grad = bbuf[at] + cbuf[at]
        normed = abuf[at]
        weighted = grad * gain1[...]
        first = r1buf[at] * (
            weighted - row_mean(weighted) - normed * row_mean(weighted * normed)
        )
        bbuf[at] = first
        low[at] = first.astype(BF16)
        return (
            sum_normed + jnp.sum(grad, axis=0, keepdims=True),
            sum_first + jnp.sum(first, axis=0, keepdims=True),
        )

    sum_normed, sum_first = row_tiles(first_back, (nought_row, nought_row))
    bsum[:, AT_FIRST : AT_FIRST + D] = sum_normed
    bsum[:, AT_OUT : AT_OUT + D] = sum_first

    class Totals:
        def __init__(self, number, start, amount, group, everyone):
            self.number, self.at = number, pl.ds(start, amount)
            self.group, self.everyone = group, everyone

        def copies(self, buffer, sems, me, peers):
            send, recv = sems
            return [
                remote(
                    buffer.at[me],
                    buffer.at[me],
                    send.at[self.number, k],
                    recv.at[self.number, me],
                    device,
                )
                for k, device in enumerate(peers)
            ]

        def gather(self, buffer, sems, me, peers):
            for copy in self.copies(buffer, sems, me, peers):
                copy.wait_send()
            for k in range(buffer.shape[0]):

                @pl.when(k != me)
                def _():
                    remote(
                        buffer.at[k], buffer.at[k], sems[0].at[0, 0], sems[1].at[self.number, k], peers[0]
                    ).wait_recv()

            total = buffer[0]
            for k in range(1, buffer.shape[0]):
                total = total + buffer[k]
            return total

        def start(self):
            self.group[t] = bsum[:, self.at]
            for copy in self.copies(self.group, (sem_as, sem_ar), t, in_group):
                copy.start()

        def middle(self):
            self.everyone[dp] = self.gather(self.group, (sem_as, sem_ar), t, in_group)
            for copy in self.copies(self.everyone, (sem_bs, sem_br), dp, in_dp):
                copy.start()

        def finish(self):
            bsum[:, self.at] = self.gather(self.everyone, (sem_bs, sem_br), dp, in_dp)

    in_group = [peer(o) for o in range(1, T)]
    in_dp = [((dp + o) % lay.dp_size, t) for o in range(1, lay.dp_size)]
    early = Totals(0, AT_VALUE, FLAT - AT_VALUE, group_early, all_early)
    late = Totals(1, AT_QUERY, AT_VALUE, group_late, all_late)

    for r in range(T):
        grad = nt(low[...], wo(r)[...]).astype(BF16)
        cgrad[r] = grad
        bsum[:, AT_VALUE + r * W : AT_VALUE + (r + 1) * W] = jnp.sum(
            grad.astype(F32), axis=0, keepdims=True
        )
    early.start()

    lone = jnp.where(place(1)[1] != place(0)[1], 0, NB - 1)
    pair_at = jnp.where(lone == 0, 1, 0)
    slot_pair = (NB * t + pair_at) // NU - row0
    slot_lone = (NB * t + lone) // NU - row0
    slot_kept = jnp.where(has_b, slot_pair, 1)

    def attend_back(r, i, first_block, amount, slot):
        hp = r * PP + i
        lanes = pl.ds(i * PAIR, PAIR)
        queries, upstreams, deltas = [], [], []
        for k in range(amount):
            at = rows_at(first_block + k)
            scaled = cgrad[r, at, lanes].astype(F32) * linv[hp, at]
            upstreams.append(split_heads(scaled.astype(BF16)))
            deltas.append(split_heads(scaled * ctx[r, at, lanes].astype(F32)))
            queries.append(split_heads(qbuf[hp, at]))
        upstream, query = jnp.concatenate(upstreams), jnp.concatenate(queries)
        delta = jnp.sum(jnp.concatenate(deltas), axis=1, keepdims=True)
        probs = pbuf[hp, pl.ds(pl.multiple_of(first_block * 2 * B, 2 * B), amount * 2 * B)]
        score = (probs.astype(F32) * (nt(upstream, vbuf[hp, slot]) - delta)).astype(BF16)
        value_grad = nn(upstream.T, probs)
        key_grad = nn(query.T, score)
        joined = nn(score, kbuf[hp, slot]) * HD**-0.5
        total = jnp.zeros((1, PAIR), F32)
        for k in range(amount):
            grad = join_heads(joined[k * 2 * B : (k + 1) * 2 * B])
            qbuf[hp, rows_at(first_block + k)] = grad.astype(BF16)
            total = total + jnp.sum(grad, axis=0, keepdims=True)
        return key_grad.astype(BF16).T, value_grad.astype(BF16).T, total

    def rank_back_pair(r, carry):
        for i in range(PP):
            keys, values, total = attend_back(r, i, pair_at, 2, slot_pair)
            kbuf[r * PP + i, slot_kept] = keys
            vbuf[r * PP + i, slot_kept] = values
            bsum[:, pl.ds(pl.multiple_of(AT_QUERY + r * W + i * PAIR, PAIR), PAIR)] = total

        @pl.when(r == T // 2 - 1)
        def _():
            early.middle()

        return carry

    def rank_back_lone(r, carry):
        for i in range(PP):
            hp = r * PP + i
            keys, values, total = attend_back(r, i, lone, 1, slot_lone)
            at = pl.ds(pl.multiple_of(AT_QUERY + r * W + i * PAIR, PAIR), PAIR)
            bsum[:, at] = bsum[:, at] + total
            kept = [jnp.where(has_b, jnp.zeros_like(keys), buf[hp, 1]) for buf in (kbuf, vbuf)]
            kbuf[hp, slot_lone] = keys + kept[0]
            vbuf[hp, slot_lone] = values + kept[1]
        return carry

    def wide(buffer, r, *at):
        return jnp.concatenate([buffer[(r * PP + i, *at)] for i in range(PP)], axis=1)

    half = SEQ // 2

    def share_copy(slot, w, k):
        u = (row0 + slot) * NU + w
        owner = u // NB
        first = (row0 + slot) * NU // NB
        place_of = t - first - jnp.where(t > owner, 1, 0)
        number = (u - owner * NB) * (lay.span - 1) + place_of
        at = pl.ds(pl.multiple_of(k * TILE, TILE), TILE)
        return remote(
            xkv.at[slot, rows_at(w), at],
            back.at[number, :, at],
            sem_gs.at[slot * NU + w, k],
            sem_gr.at[number, k],
            (dp, owner),
        )

    def send_shares(slot, rows, first_unit, amount):
        def body(k, carry):
            at = pl.ds(pl.multiple_of(k * TILE, TILE), TILE)
            total = nt(wide(kbuf, 0, slot, rows), wqkv[0, 1, at])
            total = total + nt(wide(vbuf, 0, slot, rows), wqkv[0, 2, at])
            for r in range(1, T):
                total = total + nt(wide(kbuf, r, slot, rows), wqkv[r, 1, at])
                total = total + nt(wide(vbuf, r, slot, rows), wqkv[r, 2, at])
            xkv[slot, rows, at] = total.astype(BF16)
            for n in range(amount):
                w = first_unit + n
                owner = ((row0 + slot) * NU + w) // NB

                @pl.when(owner != t)
                def _():
                    share_copy(slot, w, k).start()

            return carry

        lax.fori_loop(0, D // TILE, body, 0)

    def send_half(slot, part):
        rows = pl.ds(pl.multiple_of(part * half, half), half)
        send_shares(slot, rows, part * (NU // 2), NU // 2)

    lax.fori_loop(0, T, rank_back_pair, 0)
    part_first = jnp.where(lone == 0, 1, 0)

    lax.fori_loop(0, T, rank_back_lone, 0, unroll=2)
    late.start()

    def halves(k, carry):
        @pl.when(has_b)
        def _():
            send_half(slot_pair, (part_first + k) % 2)

        return carry

    lax.fori_loop(0, 2, halves, 0)
    late.middle()
    send_shares(slot_lone, pl.ds(0, SEQ), 0, NU)

    for n in range(0, D, TILE):
        total = nt(wide(qbuf, 0), wqkv[0, 0, pl.ds(n, TILE)])
        for r in range(1, T):
            total = total + nt(wide(qbuf, r), wqkv[r, 0, pl.ds(n, TILE)])
        at = pl.ds(n, TILE)
        bbuf[:, at] = bbuf[:, at] + total

    for j in range(NB):
        u, row, slot, w = place(j)
        bbuf[block_at(j)] = bbuf[block_at(j)] + xkv[slot, rows_at(w)].astype(F32)
    early.finish()

    for j in range(NB):
        u, row, slot, w = place(j)
        first = row * NU // NB
        last = (row * NU + NU - 1) // NB
        for o in range(lay.span):
            dest = first + o

            @pl.when((dest <= last) & (dest != t))
            def _():
                remote(
                    x.at[block_at(j)],
                    xkv.at[0, rows_at(0)],
                    sem_hs.at[j * lay.span + o],
                    sem_hr.at[0],
                    (dp, dest),
                ).wait_send()

    if quads:
        for i in range(4):
            own_copies(i).wait_send()
        lax.fori_loop(0, steps, sent, 0)
    else:
        for i in range(4):
            for o in range(1, T):
                own_copies(i, o).wait_send()

    for j in range(NB):
        u, row, slot, w = place(j)
        first = row * NU // NB
        last = (row * NU + NU - 1) // NB
        for o in range(lay.span - 1):
            number = j * (lay.span - 1) + o

            @pl.when(first + o < last)
            def _():
                sender = first + o + jnp.where(first + o >= t, 1, 0)
                for k in range(D // TILE):
                    at = pl.ds(k * TILE, TILE)
                    remote(
                        xkv.at[0, rows_at(0), at],
                        back.at[number, :, at],
                        sem_gs.at[0, k],
                        sem_gr.at[number, k],
                        (dp, sender),
                    ).wait_recv()
                bbuf[block_at(j)] = bbuf[block_at(j)] + back[number].astype(F32)

        ig[block_at(j)] = bbuf[block_at(j)].astype(BF16)

    ig_copy = pltpu.make_async_copy(ig, ig_hbm, sem_out.at[1])
    ig_copy.start()
    late.finish()

    out_copy.wait()
    ig_copy.wait()
    for slot in range(2):
        for w in range(NU):
            owner = ((row0 + slot) * NU + w) // NB

            @pl.when((owner != t) & ((slot == 0) | has_b))
            def _():
                lax.fori_loop(0, D // TILE, lambda k, c: (share_copy(slot, w, k).wait_send(), c)[1], 0)


def layer_call(lay, *args):
    T, S = lay.ranks, lay.tokens
    hp = HEADS // 2
    vmem = pltpu.VMEM
    if lay.quads:
        wide = [
            vmem((T, lay.width + D + lay.hidden, D), BF16),
            vmem((16, PAIR), BF16),
            vmem((16, PAIR), BF16),
        ]
    else:
        wide = [
            vmem((T, lay.width, D), BF16),
            vmem((T, D, lay.hidden), BF16),
            vmem((T, lay.hidden, D), BF16),
        ]
    dma = pltpu.SemaphoreType.DMA
    steps = 3 * SUBS + LAST_SUBS
    own = 4 if lay.quads else 4 * T
    sharers = lay.blocks * max(lay.span - 1, 1)
    scratch = (
        [vmem((1, FLAT), F32)]
        + [vmem((S, D), BF16)] * 4
        + [vmem((1, D), F32)] * 2
        + [vmem((HD, BROWS), F32)]
        + [vmem((T * S,), jnp.int32)] * 2
        + [vmem((T, 3, D, lay.width), BF16)]
        + wide
        + [
            vmem((2, SEQ, D), BF16),
            vmem((hp, S, PAIR), BF16),
            vmem((hp, 2, SEQ, PAIR), BF16),
            vmem((hp, 2, SEQ, PAIR), BF16),
            vmem((hp, lay.blocks * 2 * lay.block, SEQ), BF16),
            vmem((hp, S, PAIR), F32),
            vmem((lay.blocks, lay.block, SEQ), F32),
            vmem((T, S, lay.width), BF16),
            vmem((T, S, lay.width), BF16),
            vmem((S, D), F32),
            vmem((S, D), F32),
            vmem((S, D), F32),
            vmem((S, 1), F32),
            vmem((S, D), BF16),
            vmem((T, S, lay.hidden), BF16),
            vmem((T, S, lay.hidden), BF16),
            vmem((sharers, lay.block, D), BF16),
            vmem((T, 1, FLAT - AT_VALUE), F32),
            vmem((T, 1, AT_VALUE), F32),
            vmem((lay.dp_size, 1, FLAT - AT_VALUE), F32),
            vmem((lay.dp_size, 1, AT_VALUE), F32),
            dma((4,)),
            dma((9,)),
            dma((own,)),
            dma((own,)),
            dma((steps + DIRECT,)),
            dma((steps,)),
            dma((steps,)),
            dma((3 * steps,)),
            dma((3 * steps,)),
            dma((3 * steps,)),
            dma((lay.blocks * lay.span,)),
            dma((2 * lay.units,)),
            dma((2 * lay.units, D // TILE)),
            dma((sharers, D // TILE)),
            dma((2, T)),
            dma((2, T)),
            dma((2, lay.dp_size)),
            dma((2, lay.dp_size)),
            pltpu.SemaphoreType.REGULAR,
            pltpu.SemaphoreType.REGULAR,
        ]
    )
    in_vmem = pl.BlockSpec(memory_space=pltpu.VMEM)
    anywhere = pl.BlockSpec(memory_space=pl.ANY)
    return pl.pallas_call(
        partial(layer_kernel, lay),
        out_shape=(
            jax.ShapeDtypeStruct((S, D), BF16),
            jax.ShapeDtypeStruct((S, D), BF16),
            jax.ShapeDtypeStruct((1, FLAT), F32),
        ),
        in_specs=[anywhere] * 11,
        out_specs=(anywhere, anywhere, in_vmem),
        scratch_shapes=scratch,
        compiler_params=pltpu.CompilerParams(
            collective_id=0, has_side_effects=True, vmem_limit_bytes=VMEM_BYTES
        ),
        name="layer",
    )(*args)


VMEM_BYTES = 63 * 2**20
PLAN = [2, 5, 3, 6]
PARTS = 4


def update_kernel(
    raw,
    biases,
    moment_one,
    moment_two,
    left_pairs,
    left_hidden,
    left_small,
    right_bases,
    owners,
    out_in,
    ig_in,
    clipped_out,
    norm_out,
    new_out,
    copies_out,
    one_out,
    two_out,
    out_out,
    ig_out,
    rows,
    left,
    wide,
    sems,
):
    amount = out_in.shape[0] // PARTS
    parts = [pl.ds(k * amount, amount) for k in range(PARTS)]
    fetches = [
        pltpu.make_async_copy(src.at[at], wide.at[i, at], sems.at[0, i, k])
        for i, src in enumerate((out_in, ig_in))
        for k, at in enumerate(parts)
    ]
    stores = [
        pltpu.make_async_copy(wide.at[i, at], dst.at[at], sems.at[1, i, k])
        for i, dst in enumerate((out_out, ig_out))
        for k, at in enumerate(parts)
    ]
    for fetch in fetches:
        fetch.start()
    sums = raw[...]
    norm = jnp.sqrt(jnp.sum(sums * sums, keepdims=True))
    norm_out[...] = norm
    for i in range(BROWS):
        rows[i : i + 1] = sums[:, i * HD : (i + 1) * HD]
    clipped = rows[...].T * (CLIP_LIMIT / jnp.maximum(norm, CLIP_LIMIT))
    clipped_out[...] = clipped
    dp = lax.axis_index("dp")
    tail = 2 * HEADS + FR
    layout = [(0, 2 * HEADS, left_pairs), (2 * HEADS, FR, left_hidden)]
    layout += [(tail + k * DR, DR, left_small.at[k]) for k in range(4)]
    left[...] = jnp.zeros_like(left)
    for begin, amount, basis in layout:
        left[begin : begin + amount, begin : begin + amount] = basis[...]
    for fetch, store in zip(fetches, stores):
        fetch.wait()
        store.start()
    column = lax.broadcasted_iota(jnp.int32, (HD, BROWS), 1)

    def per_matrix(choose):
        result = choose(0)
        for k in range(1, len(layout)):
            result = jnp.where(column >= layout[k][0], choose(k), result)
        return result

    def product(a, b, over_a, over_b):
        return lax.dot_general(
            a,
            b,
            (((over_a,), (over_b,)), ((), ())),
            precision=HIGHEST,
            preferred_element_type=F32,
        )

    half = product(clipped, left[...], 1, 0)
    rotated = per_matrix(lambda k: product(right_bases[k], half, 0, 0))
    one = BETA_ONE * moment_one[...] + (1.0 - BETA_ONE) * rotated
    two = BETA_TWO * moment_two[...] + (1.0 - BETA_TWO) * rotated * rotated
    direction = (
        one / (1.0 - BETA_ONE**STEP) / (jnp.sqrt(two / (1.0 - BETA_TWO**STEP)) + ADAM_EPS)
    )
    half = per_matrix(lambda k: product(right_bases[k], direction, 1, 0))
    new = biases[...] - LEARN_RATE * product(half, left[...], 1, 1)
    copies_out[...] = new.astype(BF16)
    mine = per_matrix(lambda k: jnp.where(owners[k] == dp, 1.0, 0.0)) > 0.5
    new_out[...] = jnp.where(mine, new, 0.0)
    one_out[...] = jnp.where(mine, one, 0.0)
    two_out[...] = jnp.where(mine, two, 0.0)
    for store in stores:
        store.wait()


def update_call(tokens, *args):
    in_vmem = pl.BlockSpec(memory_space=pltpu.VMEM)
    anywhere = pl.BlockSpec(memory_space=pl.ANY)
    block = jax.ShapeDtypeStruct((HD, BROWS), F32)
    wide = jax.ShapeDtypeStruct((tokens, D), BF16)
    return pl.pallas_call(
        update_kernel,
        out_shape=(
            block,
            jax.ShapeDtypeStruct((1, 1), F32),
            block,
            jax.ShapeDtypeStruct((HD, BROWS), BF16),
            block,
            block,
            wide,
            wide,
        ),
        in_specs=[in_vmem] * 8 + [pl.BlockSpec(memory_space=pltpu.SMEM)] + [anywhere] * 2,
        out_specs=(in_vmem,) * 6 + (anywhere,) * 2,
        scratch_shapes=[
            pltpu.VMEM((BROWS, HD), F32),
            pltpu.VMEM((BROWS, BROWS), F32),
            pltpu.VMEM((2, tokens, D), BF16),
            pltpu.SemaphoreType.DMA((2, 2, PARTS)),
        ],
        name="update",
    )(*args)


def on_device(
    dp_size,
    ranks,
    inputs,
    output_grad,
    input_project,
    output_project,
    expand_weight,
    reduce_weight,
    first_gain,
    second_gain,
    biases,
    first_moment,
    second_moment,
    left_pairs,
    left_hidden,
    left_small,
    right_bases,
    segment_number,
    token_mask,
    owners,
):
    lay = Layout(dp_size, ranks, inputs.shape[0])
    layer_out, input_grad, sums = layer_call(
        lay,
        inputs,
        output_grad,
        first_gain.reshape(1, D),
        second_gain.reshape(1, D),
        biases.T,
        segment_number,
        token_mask,
        input_project,
        output_project,
        expand_weight,
        reduce_weight,
    )
    clipped, clip_norm, new_owned, copies, first_owned, second_owned, layer_out, input_grad = (
        update_call(
            inputs.shape[0],
            sums,
            biases.T,
            first_moment.T,
            second_moment.T,
            left_pairs,
            left_hidden,
            left_small,
            right_bases,
            owners,
            layer_out,
            input_grad,
        )
    )
    return (
        layer_out,
        input_grad,
        clipped.T,
        clip_norm.reshape(1),
        new_owned.T,
        copies.T,
        first_owned.T,
        second_owned.T,
    )


def solution(mesh):
    return jax.shard_map(
        partial(on_device, mesh.shape["dp"], mesh.shape["tensor"]),
        mesh=mesh,
        in_specs=(
            P(("dp", "tensor"), None),
            P(("dp", "tensor"), None),
            P(None, None, "tensor"),
            P("tensor", None),
            P(None, "tensor"),
            P("tensor", None),
            P(),
            P(),
            P(),
            P(),
            P(),
            P(),
            P(),
            P(),
            P(),
            P("dp"),
            P("dp"),
            P(),
        ),
        out_specs=(
            P(("dp", "tensor"), None),
            P(("dp", "tensor"), None),
            P(),
            P(),
            P("dp", None),
            P(),
            P("dp", None),
            P("dp", None),
        ),
        check_vma=False,
    )
```

```python
from functools import partial

import jax
import jax.numpy as jnp
from jax import lax
from jax.experimental import pallas as pl
from jax.experimental.pallas import tpu as pltpu
from jax.sharding import PartitionSpec as P

D = 1024
HEADS = 16
HD = 64
PAIR = 2 * HD
SEQ = 512
STEP = 10
FR = 64
DR = 16
BROWS = 160
AT_QUERY, AT_VALUE, AT_HIDDEN = 0, D, 2 * D
AT_OUT = 2 * D + FR * HD
AT_FIRST, AT_FFN, AT_SECOND = AT_OUT + D, AT_OUT + 2 * D, AT_OUT + 3 * D
FLAT = BROWS * HD

EPS_NORM = 1e-12
CLIP_LIMIT = 64.0
BETA_ONE = 0.9
BETA_TWO = 0.99
ADAM_EPS = 1e-08
LEARN_RATE = 0.2
HIGHEST = lax.Precision.HIGHEST
MESH_ID = pl.DeviceIdType.MESH
BF16 = jnp.bfloat16
F32 = jnp.float32

SUBS = 4
LAST_SUBS = 4
DIRECT = 2
RELAY_LAG, LAG = 2, 4
UNIT = 256
TILE = 256


def nn(a, b):
    return jnp.dot(a, b, preferred_element_type=F32)


def nt(a, b):
    return lax.dot_general(a, b, (((1,), (1,)), ((), ())), preferred_element_type=F32)


def tn(a, b):
    return lax.dot_general(a, b, (((0,), (0,)), ((), ())), preferred_element_type=F32)


def flip(value, bit):
    return value + bit - 2 * bit * ((value // bit) % 2)


class Layout:
    def __init__(self, dp_size, ranks, tokens):
        self.dp_size, self.ranks, self.tokens = dp_size, ranks, tokens
        self.block = 1
        while tokens % (2 * self.block) == 0 and SEQ % (2 * self.block) == 0:
            self.block *= 2
        self.blocks = tokens // self.block
        self.units = SEQ // self.block
        self.width = D // ranks
        self.pairs = self.width // PAIR
        self.hidden = FR * HD // ranks
        rows = ranks * tokens // SEQ
        self.span = 1
        for row in range(rows):
            first = row * self.units // self.blocks
            last = (row * self.units + self.units - 1) // self.blocks
            self.span = max(self.span, last - first + 1)
        self.quads = ranks == 4 and dp_size % 4 == 0


def layer_kernel(
    lay,
    x_hbm,
    og_hbm,
    gain1_hbm,
    gain2_hbm,
    biases_hbm,
    seg_hbm,
    val_hbm,
    wqkv_in,
    wo_in,
    w1_in,
    w2_in,
    out_hbm,
    ig_hbm,
    bsum,
    brow,
    x,
    og,
    out,
    ig,
    gain1,
    gain2,
    biases_t,
    seg,
    val,
    wqkv,
    wo_b,
    w1_b,
    w2_b,
    xkv,
    qbuf,
    kbuf,
    vbuf,
    pbuf,
    linv,
    mask,
    ctx,
    cgrad,
    abuf,
    bbuf,
    cbuf,
    r1buf,
    low,
    hid,
    gp,
    back,
    group_early,
    group_late,
    all_early,
    all_late,
    sem_local,
    sem_out,
    sem_own_s,
    sem_own_r,
    sem_y,
    sem_x,
    sem_z,
    sem_c,
    sem_w,
    sem_p,
    sem_hs,
    sem_hr,
    sem_gs,
    sem_gr,
    sem_as,
    sem_ar,
    sem_bs,
    sem_br,
    sem_up,
    sem_down,
):
    T, S, B, NB, NU = lay.ranks, lay.tokens, lay.block, lay.blocks, lay.units
    W, PP, F = lay.width, lay.pairs, lay.hidden
    dp = lax.axis_index("dp")
    t = lax.axis_index("tensor")
    quads = lay.quads

    def rank(o):
        r = (t + o) % 2
        if T > 2:
            r = r + 2 * ((t // 2 + o // 2) % 2)
        if T > 4:
            r = r + 4 * ((t // 4 + o // 4) % 2)
        return r

    if quads:
        big = wo_b

        def wo(r):
            return big.at[r, pl.ds(0, W)]

        def w1(r):
            return big.at[r, pl.ds(W, D)]

        def w2(r):
            return big.at[r, pl.ds(W + D, F)]
    else:

        def wo(r):
            return wo_b.at[r]

        def w1(r):
            return w1_b.at[r]

        def w2(r):
            return w2_b.at[r]

    def pieces(r):
        return [wqkv.at[r], wo(r), w1(r), w2(r)]

    sources = [wqkv_in, wo_in, w1_in, w2_in]

    def peer(o):
        return (dp, rank(o))

    def remote(src, dst, send, recv, device):
        return pltpu.make_async_remote_copy(
            src_ref=src,
            dst_ref=dst,
            send_sem=send,
            recv_sem=recv,
            device_id=device,
            device_id_type=MESH_ID,
        )

    barrier = pltpu.get_barrier_semaphore()
    others = [peer(o) for o in range(1, T)]
    heard = T - 1

    def greet(device):
        pl.semaphore_signal(barrier, inc=1, device_id=device, device_id_type=MESH_ID)

    if quads:
        others.append((flip(dp, 1), t))
        link, links = dp // 2, lay.dp_size // 2
        before, after = (dp - 2, t), (dp + 2, t)

        @pl.when(link > 0)
        def _():
            greet(before)

        @pl.when(link < links - 1)
        def _():
            greet(after)

        heard = heard + 1 + jnp.where(link > 0, 1, 0) + jnp.where(link < links - 1, 1, 0)
    else:
        others += [((dp + o) % lay.dp_size, t) for o in range(1, lay.dp_size)]
        heard = len(others)
    for device in others:
        greet(device)
    local = [
        pltpu.make_async_copy(src, dst, sem_local.at[i])
        for i, (src, dst) in enumerate(zip(sources, pieces(t)))
    ]
    x_copy = pltpu.make_async_copy(x_hbm, x, sem_out.at[3])
    x_copy.start()
    for copy in local:
        copy.start()
    og_copy = pltpu.make_async_copy(og_hbm, og, sem_out.at[2])
    og_copy.start()
    small = [
        pltpu.make_async_copy(src, dst, sem_out.at[4 + i])
        for i, (src, dst) in enumerate(
            [
                (biases_hbm, biases_t),
                (seg_hbm, seg),
                (val_hbm, val),
                (gain1_hbm, gain1),
                (gain2_hbm, gain2),
            ]
        )
    ]
    for copy in small:
        copy.start()

    row0 = (NB * t) // NU
    has_b = (NB * t + NB - 1) // NU != row0

    def place(j):
        u = NB * t + j
        row = u // NU
        return u, row, row - row0, u - row * NU

    def rows_at(w):
        return pl.ds(pl.multiple_of(w * B, B), B)

    def block_at(j):
        return pl.ds(j * B, B)

    pl.semaphore_wait(barrier, heard)

    x_copy.wait()

    def send_rows():
        for j in range(NB):
            u, row, slot, w = place(j)
            first = row * NU // NB
            last = (row * NU + NU - 1) // NB
            for o in range(lay.span):
                dest = first + o

                @pl.when((dest <= last) & (dest != t))
                def _():
                    remote(
                        x.at[block_at(j)],
                        xkv.at[row - (NB * dest) // NU, rows_at(w)],
                        sem_hs.at[j * lay.span + o],
                        sem_hr.at[(row - (NB * dest) // NU) * NU + w],
                        (dp, dest),
                    ).start()

    if quads:
        role = dp % 4
        relay = role == 3
        gy = role % 3
        gx = jnp.where(role == 1, 0, jnp.where(role == 3, 2, 1))
        gz = jnp.where(role == 2, 0, jnp.where(role == 3, 1, 2))
        far = rank(2)
        core, ynext = (dp, rank(1)), (dp, rank(2))
        xnext, znext = (flip(dp, 1), t), (flip(dp, 2), t)
        rounds = 4
        tail_step = (rounds - 1) * SUBS
        steps = tail_step + LAST_SUBS
        part_a, part_b, part_c = D // SUBS, UNIT // SUBS, UNIT // LAST_SUBS

        def chunk(idx, g, fn):
            n = g * steps + idx

            @pl.when((idx >= 0) & (idx < SUBS))
            def _():
                at = pl.ds(pl.multiple_of(idx * part_a, part_a), part_a)
                fn(lambda r: wqkv.at[r, g, at], n)

            @pl.when((idx >= SUBS) & (idx < tail_step))
            def _():
                row = ((idx // SUBS - 1) * 3 + g) * UNIT + (idx % SUBS) * part_b
                at = pl.ds(pl.multiple_of(row, part_b), part_b)
                fn(lambda r: big.at[r, at], n)

            @pl.when((idx >= tail_step) & (idx < steps))
            def _():
                row = ((rounds - 2) * 3 + g) * UNIT + (idx - tail_step) * part_c
                at = pl.ds(pl.multiple_of(row, part_c), part_c)
                fn(lambda r: big.at[r, at], n)

        relayed = steps - DIRECT
        g_direct = jnp.where(role == 1, 2, 1)
        is_served = (role == 1) | (role == 2)

        def send_y(idx):
            def go(view, n):
                remote(view(t), view(t), sem_y.at[idx], sem_w.at[n], ynext).start()

            chunk(idx, gy, go)

            def go_direct(view, n):
                remote(
                    view(t), view(t), sem_y.at[idx + DIRECT], sem_w.at[n], ynext
                ).start()

            @pl.when((idx >= relayed) & is_served)
            def _():
                chunk(idx, g_direct, go_direct)

        def to_core(view, n):
            remote(view(far), view(far), sem_c.at[n], sem_p.at[n], core).start()

        def arrived(view, n):
            remote(view(far), view(far), sem_c.at[n], sem_w.at[n], core).wait_recv()

        def to_x(view, n, idx):
            remote(view(far), view(far), sem_x.at[idx], sem_w.at[n], xnext).start()

        def to_z(view, n, idx):
            remote(view(far), view(far), sem_z.at[idx], sem_w.at[n], znext).start()

        def service(s, carry):
            def from_y(view, n):
                arrived(view, n)

                @pl.when(role != 3)
                def _():
                    to_x(view, n, s)
                    to_z(view, n, s)

                to_core(view, n)

            chunk(s, gy, from_y)
            send_y(s + SUBS)
            late = s - jnp.where(relay, RELAY_LAG, LAG)

            def from_x(view, n):
                arrived(view, n)

                @pl.when(relay & (late < relayed))
                def _():
                    to_z(view, n, late)

                to_core(view, n)

            def from_z(view, n):
                arrived(view, n)

                @pl.when(relay & (late < relayed))
                def _():
                    to_x(view, n, late)

                to_core(view, n)

            chunk(late, gx, from_x)
            chunk(late, gz, from_z)
            return carry

        def sent(idx, carry):
            def go(view, n):
                remote(view(t), view(t), sem_y.at[idx], sem_w.at[n], ynext).wait_send()

                @pl.when((role != 3) | (idx < relayed))
                def _():
                    remote(view(t), view(t), sem_x.at[idx], sem_w.at[n], xnext).wait_send()
                    remote(view(t), view(t), sem_z.at[idx], sem_w.at[n], znext).wait_send()

                @pl.when((idx >= relayed) & is_served)
                def _():
                    remote(
                        view(t), view(t), sem_y.at[idx + DIRECT], sem_w.at[n], ynext
                    ).wait_send()

                for g in range(3):
                    m = g * steps + idx
                    remote(view(t), view(t), sem_c.at[m], sem_p.at[m], core).wait_send()

            chunk(idx, gy, go)
            return carry

        def from_partner(units):
            for unit in units:
                p, g = unit // 3, unit % 3
                if p == 0:
                    view = wqkv.at[rank(3), 0, pl.ds(0, part_a)]
                else:
                    view = big.at[rank(3), pl.ds(0, part_c if p == rounds - 1 else part_b)]

                def go(idx, carry):
                    n = g * steps + idx
                    remote(view, view, sem_c.at[n], sem_p.at[n], core).wait_recv()
                    return carry

                if p == rounds - 1:
                    lax.fori_loop(tail_step, steps, go, 0)
                else:
                    lax.fori_loop(p * SUBS, (p + 1) * SUBS, go, 0)

        def own_copies(i):
            return remote(sources[i], pieces(t)[i], sem_own_s.at[i], sem_own_r.at[i], core)

        local[0].wait()
        lax.fori_loop(0, 2, lambda i, c: (send_y(i), c)[1], 0)
        send_rows()
        lax.fori_loop(2, SUBS, lambda i, c: (send_y(i), c)[1], 0)
        for i in range(4):
            own_copies(i).start()
        for i in range(1, 4):
            local[i].wait()

        first_unit = [0, 3, 4, 8, 12]

        def ready(i, o):
            @pl.when(o == 1)
            def _():
                remote(
                    sources[i], pieces(rank(1))[i], sem_own_s.at[i], sem_own_r.at[i], core
                ).wait_recv()

            @pl.when(o == 3)
            def _():
                from_partner(range(first_unit[i], first_unit[i + 1]))

    else:

        def own_copies(i, o):
            n = i * T + o
            return remote(sources[i], pieces(t)[i], sem_own_s.at[n], sem_own_r.at[n], peer(o))

        send_rows()
        for i in range(4):
            for o in range(1, T):
                own_copies(i, o).start()

        def ready(i, o):
            @pl.when(o == 0)
            def _():
                local[i].wait()

            @pl.when(o != 0)
            def _():
                n = i * T + o
                remote(
                    sources[i], pieces(rank(o))[i], sem_own_s.at[n], sem_own_r.at[n], peer(o)
                ).wait_recv()

    for copy in small:
        copy.wait()
    key_at = lax.broadcasted_iota(jnp.int32, (B, SEQ), 1)
    query_at = lax.broadcasted_iota(jnp.int32, (B, SEQ), 0)
    for j in range(NB):
        u, row, slot, w = place(j)
        keys_here = pl.ds(pl.multiple_of(row * SEQ, SEQ), SEQ)
        numbers = seg[keys_here].reshape(1, SEQ).astype(F32)
        keyed = jnp.where(val[keys_here].reshape(1, SEQ) == 1, numbers, -1.0)
        same = key_at == query_at + w * B
        own = jnp.sum(jnp.where(same, numbers, 0.0), axis=1, keepdims=True)
        mask[j] = jnp.where((own == keyed) | same, 0.0, -1e30)
        xkv[slot, rows_at(w)] = x[block_at(j)]

    bias_rows = biases_t[...].T
    for i in range(BROWS):
        brow[:, i * HD : (i + 1) * HD] = bias_rows[i : i + 1]

    head_lane = lax.broadcasted_iota(jnp.int32, (B, PAIR), 1) < HD

    def split_heads(values):
        nought = jnp.zeros_like(values)
        return jnp.concatenate(
            [jnp.where(head_lane, values, nought), jnp.where(head_lane, nought, values)], axis=0
        )

    def join_heads(values):
        return jnp.where(head_lane, values[:B], values[B:])

    ones = jnp.ones((SEQ, PAIR), BF16)

    slot_first = jnp.where(has_b & (t % 4 == 2), 1, 0)

    def project_query(r):
        bias = brow[:, pl.ds(pl.multiple_of(AT_QUERY + r * W, PAIR), W)]
        query = ((nn(x[...], wqkv[r, 0]) + bias) * HD**-0.5).astype(BF16)
        for i in range(PP):
            qbuf[r * PP + i] = query[:, i * PAIR : (i + 1) * PAIR]

    def project_keys(o, r):
        bias = brow[:, pl.ds(pl.multiple_of(AT_VALUE + r * W, PAIR), W)]

        def body(turn, carry):
            slot = (slot_first + turn) % 2

            @pl.when((slot == 0) | has_b)
            def _():
                for w in range(NU):
                    owner = ((row0 + slot) * NU + w) // NB

                    @pl.when((owner != t) & (o == 0))
                    def _():
                        remote(
                            x.at[block_at(0)],
                            xkv.at[slot, rows_at(w)],
                            sem_hs.at[0],
                            sem_hr.at[slot * NU + w],
                            (dp, owner),
                        ).wait_recv()

                rows = xkv[slot]
                keys = nn(rows, wqkv[r, 1]).astype(BF16)
                values = (nn(rows, wqkv[r, 2]) + bias).astype(BF16)
                for i in range(PP):
                    kbuf[r * PP + i, slot] = keys[:, i * PAIR : (i + 1) * PAIR]
                    vbuf[r * PP + i, slot] = values[:, i * PAIR : (i + 1) * PAIR]

            return carry

        lax.fori_loop(0, 2, body, 0)

    def attend(r, i):
        hp = r * PP + i
        for j in range(NB):
            u, row, slot, w = place(j)
            query = split_heads(qbuf[hp, block_at(j)])
            hide = mask[j]
            scores = nt(query, kbuf[hp, slot]) + jnp.concatenate([hide, hide], axis=0)
            peak = jnp.max(scores, axis=1, keepdims=True)
            probs = jnp.exp(scores - peak).astype(BF16)
            pbuf[hp, j * 2 * B : (j + 1) * 2 * B] = probs
            mixed = nn(probs, jnp.concatenate([vbuf[hp, slot], ones], axis=1))
            inverse = 1.0 / join_heads(mixed[:, PAIR:])
            linv[hp, block_at(j)] = inverse
            ctx[r, block_at(j), pl.ds(i * PAIR, PAIR)] = (
                join_heads(mixed[:, :PAIR]) * inverse
            ).astype(BF16)

    def project(o):
        ready(0, o)
        r = rank(o)
        project_query(r)
        project_keys(o, r)

    def attend_rank(o):
        for i in range(PP):
            attend(rank(o), i)

    def row_mean(values):
        return jnp.mean(values, axis=1, keepdims=True)

    def row_tiles(body, carry):
        for j in range(NB):
            carry = body(block_at(j), carry)
        return carry

    def norm_first(at, carry):
        values = abuf[at]
        centred = values - row_mean(values)
        root = lax.rsqrt(row_mean(centred * centred) + EPS_NORM)
        normed = centred * root
        r1buf[at] = root
        abuf[at] = normed
        first_normed = normed * gain1[...] + brow[:, AT_FIRST : AT_FIRST + D]
        low[at] = first_normed.astype(BF16)
        bbuf[at] = first_normed + brow[:, AT_FFN : AT_FFN + D]
        return carry

    def finish_attention():
        for o in range(T):
            ready(1, o)
        for n in range(0, D, TILE):
            total = nn(ctx[0], wo(0)[:, n : n + TILE])
            for r in range(1, T):
                total = total + nn(ctx[r], wo(r)[:, n : n + TILE])
            at = pl.ds(n, TILE)
            abuf[:, at] = x[:, at].astype(F32) + total + brow[:, AT_OUT + n : AT_OUT + n + TILE]
        row_tiles(norm_first, 0)

    def expand(o):
        ready(2, o)
        r = rank(o)
        for n in range(0, F, TILE):
            bias = brow[:, pl.ds(pl.multiple_of(AT_HIDDEN + r * F + n, PAIR), TILE)]
            pre = nn(low[...], w1(r)[:, n : n + TILE]) + bias
            cdf = 0.5 * (1.0 + lax.erf(pre * 0.5**0.5))
            density = jnp.exp(-0.5 * pre * pre) * 0.3989422804014327
            hid[r, :, pl.ds(n, TILE)] = (pre * cdf).astype(BF16)
            gp[r, :, pl.ds(n, TILE)] = (cdf + pre * density).astype(BF16)

    def reduce(o):
        ready(3, o)
        r = rank(o)
        for n in range(0, D, TILE):
            at = pl.ds(n, TILE)
            bbuf[:, at] = bbuf[:, at] + nn(hid[r], w2(r)[:, n : n + TILE])

    if quads:
        whole = [(k + 1) * SUBS + LAG - 1 for k in range(rounds - 1)] + [steps + LAG - 1]
        plan = [
            (project, [PLAN[0], PLAN[1], whole[0], whole[0] + 2]),
            (attend_rank, [PLAN[2], PLAN[3], whole[0] + 1, whole[0] + 3]),
            (expand, [whole[1] + 1, whole[1] + 2, whole[2], whole[2] + 1]),
            (reduce, [whole[1] + 3, whole[1] + 4]),
        ]

        def pass_on(place_in_chain, sem, to, s):
            @pl.when(s == 2 * place_in_chain)
            def _():
                @pl.when(place_in_chain > 0)
                def _():
                    pl.semaphore_wait(sem, 1)

                @pl.when(place_in_chain < links - 1)
                def _():
                    pl.semaphore_signal(sem, inc=1, device_id=to, device_id_type=MESH_ID)

        def step(s, carry):
            service(s, 0)
            pass_on(link, sem_up, after, s)
            pass_on(links - 1 - link, sem_down, before, s)

            @pl.when(s == whole[1])
            def _():
                finish_attention()

            for part, at_steps in plan:
                o = jnp.int32(-1)
                for k, at_step in enumerate(at_steps):
                    if at_step < whole[3]:
                        o = jnp.where(s == at_step, k, o)

                @pl.when(o >= 0)
                def _():
                    part(o)

            return carry

        lax.fori_loop(0, whole[3] + 1, step, 0)
        lax.fori_loop(2, T, lambda o, c: (reduce(o), c)[1], 0)
    else:

        def each_rank(part):
            lax.fori_loop(0, T, lambda o, c: (part(o), c)[1], 0)

        each_rank(project)
        each_rank(attend_rank)
        finish_attention()
        each_rank(expand)
        each_rank(reduce)

    nought_row = jnp.zeros((1, D), F32)
    og_copy.wait()

    def norm_second(at, carry):
        sum_up, sum_second = carry
        values = bbuf[at]
        centred = values - row_mean(values)
        root = lax.rsqrt(row_mean(centred * centred) + EPS_NORM)
        normed = centred * root
        out[at] = (normed * gain2[...] + brow[:, AT_SECOND : AT_SECOND + D]).astype(BF16)
        upstream = og[at].astype(F32)
        weighted = upstream * gain2[...]
        grad = root * (weighted - row_mean(weighted) - normed * row_mean(weighted * normed))
        bbuf[at] = grad
        low[at] = grad.astype(BF16)
        return (
            sum_up + jnp.sum(upstream, axis=0, keepdims=True),
            sum_second + jnp.sum(grad, axis=0, keepdims=True),
        )

    sum_up, sum_second = row_tiles(norm_second, (nought_row, nought_row))
    out_copy = pltpu.make_async_copy(out, out_hbm, sem_out.at[0])
    out_copy.start()
    bsum[:, AT_SECOND : AT_SECOND + D] = sum_up
    bsum[:, AT_FFN : AT_FFN + D] = sum_second

    def ffn_back(r, carry):
        for n in range(0, F, TILE):
            grad = nt(low[...], w2(r)[n : n + TILE, :]) * gp[r, :, pl.ds(n, TILE)].astype(F32)
            at = pl.ds(pl.multiple_of(AT_HIDDEN + r * F + n, PAIR), TILE)
            bsum[:, at] = jnp.sum(grad, axis=0, keepdims=True)
            hid[r, :, pl.ds(n, TILE)] = grad.astype(BF16)
        return carry

    lax.fori_loop(0, T, ffn_back, 0, unroll=4 if quads else 2)
    for n in range(0, D, TILE):
        total = nt(hid[0], w1(0)[n : n + TILE, :])
        for r in range(1, T):
            total = total + nt(hid[r], w1(r)[n : n + TILE, :])
        cbuf[:, pl.ds(n, TILE)] = total

    def first_back(at, carry):
        sum_normed, sum_first = carry
        grad = bbuf[at] + cbuf[at]
        normed = abuf[at]
        weighted = grad * gain1[...]
        first = r1buf[at] * (
            weighted - row_mean(weighted) - normed * row_mean(weighted * normed)
        )
        bbuf[at] = first
        low[at] = first.astype(BF16)
        return (
            sum_normed + jnp.sum(grad, axis=0, keepdims=True),
            sum_first + jnp.sum(first, axis=0, keepdims=True),
        )

    sum_normed, sum_first = row_tiles(first_back, (nought_row, nought_row))
    bsum[:, AT_FIRST : AT_FIRST + D] = sum_normed
    bsum[:, AT_OUT : AT_OUT + D] = sum_first

    class Totals:
        def __init__(self, number, start, amount, group, everyone):
            self.number, self.at = number, pl.ds(start, amount)
            self.group, self.everyone = group, everyone

        def copies(self, buffer, sems, me, peers):
            send, recv = sems
            return [
                remote(
                    buffer.at[me],
                    buffer.at[me],
                    send.at[self.number, k],
                    recv.at[self.number, me],
                    device,
                )
                for k, device in enumerate(peers)
            ]

        def gather(self, buffer, sems, me, peers):
            for copy in self.copies(buffer, sems, me, peers):
                copy.wait_send()
            for k in range(buffer.shape[0]):

                @pl.when(k != me)
                def _():
                    remote(
                        buffer.at[k], buffer.at[k], sems[0].at[0, 0], sems[1].at[self.number, k], peers[0]
                    ).wait_recv()

            total = buffer[0]
            for k in range(1, buffer.shape[0]):
                total = total + buffer[k]
            return total

        def start(self):
            self.group[t] = bsum[:, self.at]
            for copy in self.copies(self.group, (sem_as, sem_ar), t, in_group):
                copy.start()

        def middle(self):
            self.everyone[dp] = self.gather(self.group, (sem_as, sem_ar), t, in_group)
            for copy in self.copies(self.everyone, (sem_bs, sem_br), dp, in_dp):
                copy.start()

        def finish(self):
            bsum[:, self.at] = self.gather(self.everyone, (sem_bs, sem_br), dp, in_dp)

    in_group = [peer(o) for o in range(1, T)]
    in_dp = [((dp + o) % lay.dp_size, t) for o in range(1, lay.dp_size)]
    early = Totals(0, AT_VALUE, FLAT - AT_VALUE, group_early, all_early)
    late = Totals(1, AT_QUERY, AT_VALUE, group_late, all_late)

    for r in range(T):
        grad = nt(low[...], wo(r)[...]).astype(BF16)
        cgrad[r] = grad
        bsum[:, AT_VALUE + r * W : AT_VALUE + (r + 1) * W] = jnp.sum(
            grad.astype(F32), axis=0, keepdims=True
        )
    early.start()

    lone = jnp.where(place(1)[1] != place(0)[1], 0, NB - 1)
    pair_at = jnp.where(lone == 0, 1, 0)
    slot_pair = (NB * t + pair_at) // NU - row0
    slot_lone = (NB * t + lone) // NU - row0
    slot_kept = jnp.where(has_b, slot_pair, 1)

    def attend_back(r, i, first_block, amount, slot):
        hp = r * PP + i
        lanes = pl.ds(i * PAIR, PAIR)
        queries, upstreams, deltas = [], [], []
        for k in range(amount):
            at = rows_at(first_block + k)
            scaled = cgrad[r, at, lanes].astype(F32) * linv[hp, at]
            upstreams.append(split_heads(scaled.astype(BF16)))
            deltas.append(split_heads(scaled * ctx[r, at, lanes].astype(F32)))
            queries.append(split_heads(qbuf[hp, at]))
        upstream, query = jnp.concatenate(upstreams), jnp.concatenate(queries)
        delta = jnp.sum(jnp.concatenate(deltas), axis=1, keepdims=True)
        probs = pbuf[hp, pl.ds(pl.multiple_of(first_block * 2 * B, 2 * B), amount * 2 * B)]
        score = (probs.astype(F32) * (nt(upstream, vbuf[hp, slot]) - delta)).astype(BF16)
        value_grad = nn(upstream.T, probs)
        key_grad = nn(query.T, score)
        joined = nn(score, kbuf[hp, slot]) * HD**-0.5
        total = jnp.zeros((1, PAIR), F32)
        for k in range(amount):
            grad = join_heads(joined[k * 2 * B : (k + 1) * 2 * B])
            qbuf[hp, rows_at(first_block + k)] = grad.astype(BF16)
            total = total + jnp.sum(grad, axis=0, keepdims=True)
        return key_grad.astype(BF16).T, value_grad.astype(BF16).T, total

    def rank_back_pair(r, carry):
        for i in range(PP):
            keys, values, total = attend_back(r, i, pair_at, 2, slot_pair)
            kbuf[r * PP + i, slot_kept] = keys
            vbuf[r * PP + i, slot_kept] = values
            bsum[:, pl.ds(pl.multiple_of(AT_QUERY + r * W + i * PAIR, PAIR), PAIR)] = total

        @pl.when(r == T // 2 - 1)
        def _():
            early.middle()

        return carry

    def rank_back_lone(r, carry):
        for i in range(PP):
            hp = r * PP + i
            keys, values, total = attend_back(r, i, lone, 1, slot_lone)
            at = pl.ds(pl.multiple_of(AT_QUERY + r * W + i * PAIR, PAIR), PAIR)
            bsum[:, at] = bsum[:, at] + total
            kept = [jnp.where(has_b, jnp.zeros_like(keys), buf[hp, 1]) for buf in (kbuf, vbuf)]
            kbuf[hp, slot_lone] = keys + kept[0]
            vbuf[hp, slot_lone] = values + kept[1]
        return carry

    def wide(buffer, r, *at):
        return jnp.concatenate([buffer[(r * PP + i, *at)] for i in range(PP)], axis=1)

    half = SEQ // 2

    def share_copy(slot, w, k):
        u = (row0 + slot) * NU + w
        owner = u // NB
        first = (row0 + slot) * NU // NB
        place_of = t - first - jnp.where(t > owner, 1, 0)
        number = (u - owner * NB) * (lay.span - 1) + place_of
        at = pl.ds(pl.multiple_of(k * TILE, TILE), TILE)
        return remote(
            xkv.at[slot, rows_at(w), at],
            back.at[number, :, at],
            sem_gs.at[slot * NU + w, k],
            sem_gr.at[number, k],
            (dp, owner),
        )

    def send_shares(slot, rows, first_unit, amount):
        def body(k, carry):
            at = pl.ds(pl.multiple_of(k * TILE, TILE), TILE)
            total = nt(wide(kbuf, 0, slot, rows), wqkv[0, 1, at])
            total = total + nt(wide(vbuf, 0, slot, rows), wqkv[0, 2, at])
            for r in range(1, T):
                total = total + nt(wide(kbuf, r, slot, rows), wqkv[r, 1, at])
                total = total + nt(wide(vbuf, r, slot, rows), wqkv[r, 2, at])
            xkv[slot, rows, at] = total.astype(BF16)
            for n in range(amount):
                w = first_unit + n
                owner = ((row0 + slot) * NU + w) // NB

                @pl.when(owner != t)
                def _():
                    share_copy(slot, w, k).start()

            return carry

        lax.fori_loop(0, D // TILE, body, 0)

    def send_half(slot, part):
        rows = pl.ds(pl.multiple_of(part * half, half), half)
        send_shares(slot, rows, part * (NU // 2), NU // 2)

    lax.fori_loop(0, T, rank_back_pair, 0)
    part_first = jnp.where(lone == 0, 1, 0)

    lax.fori_loop(0, T, rank_back_lone, 0, unroll=4 if quads else 2)
    late.start()

    def halves(k, carry):
        @pl.when(has_b)
        def _():
            send_half(slot_pair, (part_first + k) % 2)

        return carry

    lax.fori_loop(0, 2, halves, 0)
    late.middle()
    send_shares(slot_lone, pl.ds(0, SEQ), 0, NU)

    for n in range(0, D, TILE):
        total = nt(wide(qbuf, 0), wqkv[0, 0, pl.ds(n, TILE)])
        for r in range(1, T):
            total = total + nt(wide(qbuf, r), wqkv[r, 0, pl.ds(n, TILE)])
        at = pl.ds(n, TILE)
        bbuf[:, at] = bbuf[:, at] + total

    for j in range(NB):
        u, row, slot, w = place(j)
        bbuf[block_at(j)] = bbuf[block_at(j)] + xkv[slot, rows_at(w)].astype(F32)
    early.finish()

    for j in range(NB):
        u, row, slot, w = place(j)
        first = row * NU // NB
        last = (row * NU + NU - 1) // NB
        for o in range(lay.span):
            dest = first + o

            @pl.when((dest <= last) & (dest != t))
            def _():
                remote(
                    x.at[block_at(j)],
                    xkv.at[0, rows_at(0)],
                    sem_hs.at[j * lay.span + o],
                    sem_hr.at[0],
                    (dp, dest),
                ).wait_send()

    if quads:
        for i in range(4):
            own_copies(i).wait_send()
        lax.fori_loop(0, steps, sent, 0)
    else:
        for i in range(4):
            for o in range(1, T):
                own_copies(i, o).wait_send()

    for j in range(NB):
        u, row, slot, w = place(j)
        first = row * NU // NB
        last = (row * NU + NU - 1) // NB
        for o in range(lay.span - 1):
            number = j * (lay.span - 1) + o

            @pl.when(first + o < last)
            def _():
                sender = first + o + jnp.where(first + o >= t, 1, 0)
                for k in range(D // TILE):
                    at = pl.ds(k * TILE, TILE)
                    remote(
                        xkv.at[0, rows_at(0), at],
                        back.at[number, :, at],
                        sem_gs.at[0, k],
                        sem_gr.at[number, k],
                        (dp, sender),
                    ).wait_recv()
                bbuf[block_at(j)] = bbuf[block_at(j)] + back[number].astype(F32)

        ig[block_at(j)] = bbuf[block_at(j)].astype(BF16)

    ig_copy = pltpu.make_async_copy(ig, ig_hbm, sem_out.at[1])
    ig_copy.start()
    late.finish()

    out_copy.wait()
    ig_copy.wait()
    for slot in range(2):
        for w in range(NU):
            owner = ((row0 + slot) * NU + w) // NB

            @pl.when((owner != t) & ((slot == 0) | has_b))
            def _():
                lax.fori_loop(0, D // TILE, lambda k, c: (share_copy(slot, w, k).wait_send(), c)[1], 0)


def layer_call(lay, *args):
    T, S = lay.ranks, lay.tokens
    hp = HEADS // 2
    vmem = pltpu.VMEM
    if lay.quads:
        wide = [
            vmem((T, lay.width + D + lay.hidden, D), BF16),
            vmem((16, PAIR), BF16),
            vmem((16, PAIR), BF16),
        ]
    else:
        wide = [
            vmem((T, lay.width, D), BF16),
            vmem((T, D, lay.hidden), BF16),
            vmem((T, lay.hidden, D), BF16),
        ]
    dma = pltpu.SemaphoreType.DMA
    steps = 3 * SUBS + LAST_SUBS
    own = 4 if lay.quads else 4 * T
    sharers = lay.blocks * max(lay.span - 1, 1)
    scratch = (
        [vmem((1, FLAT), F32)]
        + [vmem((S, D), BF16)] * 4
        + [vmem((1, D), F32)] * 2
        + [vmem((HD, BROWS), F32)]
        + [vmem((T * S,), jnp.int32)] * 2
        + [vmem((T, 3, D, lay.width), BF16)]
        + wide
        + [
            vmem((2, SEQ, D), BF16),
            vmem((hp, S, PAIR), BF16),
            vmem((hp, 2, SEQ, PAIR), BF16),
            vmem((hp, 2, SEQ, PAIR), BF16),
            vmem((hp, lay.blocks * 2 * lay.block, SEQ), BF16),
            vmem((hp, S, PAIR), F32),
            vmem((lay.blocks, lay.block, SEQ), F32),
            vmem((T, S, lay.width), BF16),
            vmem((T, S, lay.width), BF16),
            vmem((S, D), F32),
            vmem((S, D), F32),
            vmem((S, D), F32),
            vmem((S, 1), F32),
            vmem((S, D), BF16),
            vmem((T, S, lay.hidden), BF16),
            vmem((T, S, lay.hidden), BF16),
            vmem((sharers, lay.block, D), BF16),
            vmem((T, 1, FLAT - AT_VALUE), F32),
            vmem((T, 1, AT_VALUE), F32),
            vmem((lay.dp_size, 1, FLAT - AT_VALUE), F32),
            vmem((lay.dp_size, 1, AT_VALUE), F32),
            dma((4,)),
            dma((9,)),
            dma((own,)),
            dma((own,)),
            dma((steps + DIRECT,)),
            dma((steps,)),
            dma((steps,)),
            dma((3 * steps,)),
            dma((3 * steps,)),
            dma((3 * steps,)),
            dma((lay.blocks * lay.span,)),
            dma((2 * lay.units,)),
            dma((2 * lay.units, D // TILE)),
            dma((sharers, D // TILE)),
            dma((2, T)),
            dma((2, T)),
            dma((2, lay.dp_size)),
            dma((2, lay.dp_size)),
            pltpu.SemaphoreType.REGULAR,
            pltpu.SemaphoreType.REGULAR,
        ]
    )
    in_vmem = pl.BlockSpec(memory_space=pltpu.VMEM)
    anywhere = pl.BlockSpec(memory_space=pl.ANY)
    return pl.pallas_call(
        partial(layer_kernel, lay),
        out_shape=(
            jax.ShapeDtypeStruct((S, D), BF16),
            jax.ShapeDtypeStruct((S, D), BF16),
            jax.ShapeDtypeStruct((1, FLAT), F32),
        ),
        in_specs=[anywhere] * 11,
        out_specs=(anywhere, anywhere, in_vmem),
        scratch_shapes=scratch,
        compiler_params=pltpu.CompilerParams(
            collective_id=0, has_side_effects=True, vmem_limit_bytes=VMEM_BYTES
        ),
        name="layer",
    )(*args)


VMEM_BYTES = 63 * 2**20
PLAN = [2, 5, 3, 6]
PARTS = 1


def update_kernel(
    raw,
    biases,
    moment_one,
    moment_two,
    left_pairs,
    left_hidden,
    left_small,
    right_bases,
    owners,
    out_in,
    ig_in,
    clipped_out,
    norm_out,
    new_out,
    copies_out,
    one_out,
    two_out,
    out_out,
    ig_out,
    rows,
    left,
    wide,
    sems,
):
    amount = out_in.shape[0] // PARTS
    parts = [pl.ds(k * amount, amount) for k in range(PARTS)]
    fetches = [
        pltpu.make_async_copy(src.at[at], wide.at[i, at], sems.at[0, i, k])
        for i, src in enumerate((out_in, ig_in))
        for k, at in enumerate(parts)
    ]
    stores = [
        pltpu.make_async_copy(wide.at[i, at], dst.at[at], sems.at[1, i, k])
        for i, dst in enumerate((out_out, ig_out))
        for k, at in enumerate(parts)
    ]
    for fetch in fetches:
        fetch.start()
    sums = raw[...]
    norm = jnp.sqrt(jnp.sum(sums * sums, keepdims=True))
    norm_out[...] = norm
    for i in range(BROWS):
        rows[i : i + 1] = sums[:, i * HD : (i + 1) * HD]
    clipped = rows[...].T * (CLIP_LIMIT / jnp.maximum(norm, CLIP_LIMIT))
    clipped_out[...] = clipped
    dp = lax.axis_index("dp")
    tail = 2 * HEADS + FR
    layout = [(0, 2 * HEADS, left_pairs), (2 * HEADS, FR, left_hidden)]
    layout += [(tail + k * DR, DR, left_small.at[k]) for k in range(4)]
    left[...] = jnp.zeros_like(left)
    for begin, amount, basis in layout:
        left[begin : begin + amount, begin : begin + amount] = basis[...]
    for fetch, store in zip(fetches, stores):
        fetch.wait()
        store.start()
    column = lax.broadcasted_iota(jnp.int32, (HD, BROWS), 1)

    def per_matrix(choose):
        result = choose(0)
        for k in range(1, len(layout)):
            result = jnp.where(column >= layout[k][0], choose(k), result)
        return result

    def product(a, b, over_a, over_b):
        return lax.dot_general(
            a,
            b,
            (((over_a,), (over_b,)), ((), ())),
            precision=HIGHEST,
            preferred_element_type=F32,
        )

    half = product(clipped, left[...], 1, 0)
    rotated = per_matrix(lambda k: product(right_bases[k], half, 0, 0))
    one = BETA_ONE * moment_one[...] + (1.0 - BETA_ONE) * rotated
    two = BETA_TWO * moment_two[...] + (1.0 - BETA_TWO) * rotated * rotated
    direction = (
        one / (1.0 - BETA_ONE**STEP) / (jnp.sqrt(two / (1.0 - BETA_TWO**STEP)) + ADAM_EPS)
    )
    half = per_matrix(lambda k: product(right_bases[k], direction, 1, 0))
    new = biases[...] - LEARN_RATE * product(half, left[...], 1, 1)
    copies_out[...] = new.astype(BF16)
    mine = per_matrix(lambda k: jnp.where(owners[k] == dp, 1.0, 0.0)) > 0.5
    new_out[...] = jnp.where(mine, new, 0.0)
    one_out[...] = jnp.where(mine, one, 0.0)
    two_out[...] = jnp.where(mine, two, 0.0)
    for store in stores:
        store.wait()


def update_call(tokens, *args):
    in_vmem = pl.BlockSpec(memory_space=pltpu.VMEM)
    anywhere = pl.BlockSpec(memory_space=pl.ANY)
    block = jax.ShapeDtypeStruct((HD, BROWS), F32)
    wide = jax.ShapeDtypeStruct((tokens, D), BF16)
    return pl.pallas_call(
        update_kernel,
        out_shape=(
            block,
            jax.ShapeDtypeStruct((1, 1), F32),
            block,
            jax.ShapeDtypeStruct((HD, BROWS), BF16),
            block,
            block,
            wide,
            wide,
        ),
        in_specs=[in_vmem] * 8 + [pl.BlockSpec(memory_space=pltpu.SMEM)] + [anywhere] * 2,
        out_specs=(in_vmem,) * 6 + (anywhere,) * 2,
        scratch_shapes=[
            pltpu.VMEM((BROWS, HD), F32),
            pltpu.VMEM((BROWS, BROWS), F32),
            pltpu.VMEM((2, tokens, D), BF16),
            pltpu.SemaphoreType.DMA((2, 2, PARTS)),
        ],
        name="update",
    )(*args)


def on_device(
    dp_size,
    ranks,
    inputs,
    output_grad,
    input_project,
    output_project,
    expand_weight,
    reduce_weight,
    first_gain,
    second_gain,
    biases,
    first_moment,
    second_moment,
    left_pairs,
    left_hidden,
    left_small,
    right_bases,
    segment_number,
    token_mask,
    owners,
):
    lay = Layout(dp_size, ranks, inputs.shape[0])
    layer_out, input_grad, sums = layer_call(
        lay,
        inputs,
        output_grad,
        first_gain.reshape(1, D),
        second_gain.reshape(1, D),
        biases.T,
        segment_number,
        token_mask,
        input_project,
        output_project,
        expand_weight,
        reduce_weight,
    )
    clipped, clip_norm, new_owned, copies, first_owned, second_owned, layer_out, input_grad = (
        update_call(
            inputs.shape[0],
            sums,
            biases.T,
            first_moment.T,
            second_moment.T,
            left_pairs,
            left_hidden,
            left_small,
            right_bases,
            owners,
            layer_out,
            input_grad,
        )
    )
    return (
        layer_out,
        input_grad,
        clipped.T,
        clip_norm.reshape(1),
        new_owned.T,
        copies.T,
        first_owned.T,
        second_owned.T,
    )


def solution(mesh):
    return jax.shard_map(
        partial(on_device, mesh.shape["dp"], mesh.shape["tensor"]),
        mesh=mesh,
        in_specs=(
            P(("dp", "tensor"), None),
            P(("dp", "tensor"), None),
            P(None, None, "tensor"),
            P("tensor", None),
            P(None, "tensor"),
            P("tensor", None),
            P(),
            P(),
            P(),
            P(),
            P(),
            P(),
            P(),
            P(),
            P(),
            P("dp"),
            P("dp"),
            P(),
        ),
        out_specs=(
            P(("dp", "tensor"), None),
            P(("dp", "tensor"), None),
            P(),
            P(),
            P("dp", None),
            P(),
            P("dp", None),
            P("dp", None),
        ),
        check_vma=False,
    )
```

```python
from functools import partial

import jax
import jax.numpy as jnp
from jax import lax
from jax.experimental import pallas as pl
from jax.experimental.pallas import tpu as pltpu
from jax.sharding import PartitionSpec as P

D = 1024
HEADS = 16
HD = 64
PAIR = 2 * HD
SEQ = 512
STEP = 10
FR = 64
DR = 16
BROWS = 160
AT_QUERY, AT_VALUE, AT_HIDDEN = 0, D, 2 * D
AT_OUT = 2 * D + FR * HD
AT_FIRST, AT_FFN, AT_SECOND = AT_OUT + D, AT_OUT + 2 * D, AT_OUT + 3 * D
FLAT = BROWS * HD

EPS_NORM = 1e-12
CLIP_LIMIT = 64.0
BETA_ONE = 0.9
BETA_TWO = 0.99
ADAM_EPS = 1e-08
LEARN_RATE = 0.2
HIGHEST = lax.Precision.HIGHEST
MESH_ID = pl.DeviceIdType.MESH
BF16 = jnp.bfloat16
F32 = jnp.float32

SUBS = 4
LAST_SUBS = 4
DIRECT = 2
RELAY_LAG, LAG = 2, 4
UNIT = 256
TILE = 256


def nn(a, b):
    return jnp.dot(a, b, preferred_element_type=F32)


def nt(a, b):
    return lax.dot_general(a, b, (((1,), (1,)), ((), ())), preferred_element_type=F32)


def tn(a, b):
    return lax.dot_general(a, b, (((0,), (0,)), ((), ())), preferred_element_type=F32)


def flip(value, bit):
    return value + bit - 2 * bit * ((value // bit) % 2)


class Layout:
    def __init__(self, dp_size, ranks, tokens):
        self.dp_size, self.ranks, self.tokens = dp_size, ranks, tokens
        self.block = 1
        while tokens % (2 * self.block) == 0 and SEQ % (2 * self.block) == 0:
            self.block *= 2
        self.blocks = tokens // self.block
        self.units = SEQ // self.block
        self.width = D // ranks
        self.pairs = self.width // PAIR
        self.hidden = FR * HD // ranks
        rows = ranks * tokens // SEQ
        self.span = 1
        for row in range(rows):
            first = row * self.units // self.blocks
            last = (row * self.units + self.units - 1) // self.blocks
            self.span = max(self.span, last - first + 1)
        self.quads = ranks == 4 and dp_size % 4 == 0


def layer_kernel(
    lay,
    x_hbm,
    og_hbm,
    gain1_hbm,
    gain2_hbm,
    biases_hbm,
    seg_hbm,
    val_hbm,
    wqkv_in,
    wo_in,
    w1_in,
    w2_in,
    out_hbm,
    ig_hbm,
    bsum,
    brow,
    x,
    og,
    out,
    ig,
    gain1,
    gain2,
    biases_t,
    seg,
    val,
    wqkv,
    wo_b,
    w1_b,
    w2_b,
    xkv,
    qbuf,
    kbuf,
    vbuf,
    pbuf,
    linv,
    mask,
    ctx,
    cgrad,
    abuf,
    bbuf,
    cbuf,
    r1buf,
    low,
    hid,
    gp,
    back,
    group_early,
    group_late,
    all_early,
    all_late,
    sem_local,
    sem_out,
    sem_own_s,
    sem_own_r,
    sem_y,
    sem_x,
    sem_z,
    sem_c,
    sem_w,
    sem_p,
    sem_hs,
    sem_hr,
    sem_gs,
    sem_gr,
    sem_as,
    sem_ar,
    sem_bs,
    sem_br,
    sem_up,
    sem_down,
):
    T, S, B, NB, NU = lay.ranks, lay.tokens, lay.block, lay.blocks, lay.units
    W, PP, F = lay.width, lay.pairs, lay.hidden
    dp = lax.axis_index("dp")
    t = lax.axis_index("tensor")
    quads = lay.quads

    def rank(o):
        r = (t + o) % 2
        if T > 2:
            r = r + 2 * ((t // 2 + o // 2) % 2)
        if T > 4:
            r = r + 4 * ((t // 4 + o // 4) % 2)
        return r

    if quads:
        big = wo_b

        def wo(r):
            return big.at[r, pl.ds(0, W)]

        def w1(r):
            return big.at[r, pl.ds(W, D)]

        def w2(r):
            return big.at[r, pl.ds(W + D, F)]
    else:

        def wo(r):
            return wo_b.at[r]

        def w1(r):
            return w1_b.at[r]

        def w2(r):
            return w2_b.at[r]

    def pieces(r):
        return [wqkv.at[r], wo(r), w1(r), w2(r)]

    sources = [wqkv_in, wo_in, w1_in, w2_in]

    def peer(o):
        return (dp, rank(o))

    def remote(src, dst, send, recv, device):
        return pltpu.make_async_remote_copy(
            src_ref=src,
            dst_ref=dst,
            send_sem=send,
            recv_sem=recv,
            device_id=device,
            device_id_type=MESH_ID,
        )

    barrier = pltpu.get_barrier_semaphore()
    others = [peer(o) for o in range(1, T)]
    heard = T - 1

    def greet(device):
        pl.semaphore_signal(barrier, inc=1, device_id=device, device_id_type=MESH_ID)

    if quads:
        others.append((flip(dp, 1), t))
        link, links = dp // 2, lay.dp_size // 2
        before, after = (dp - 2, t), (dp + 2, t)

        @pl.when(link > 0)
        def _():
            greet(before)

        @pl.when(link < links - 1)
        def _():
            greet(after)

        heard = heard + 1 + jnp.where(link > 0, 1, 0) + jnp.where(link < links - 1, 1, 0)
    else:
        others += [((dp + o) % lay.dp_size, t) for o in range(1, lay.dp_size)]
        heard = len(others)
    for device in others:
        greet(device)
    local = [
        pltpu.make_async_copy(src, dst, sem_local.at[i])
        for i, (src, dst) in enumerate(zip(sources, pieces(t)))
    ]
    x_copy = pltpu.make_async_copy(x_hbm, x, sem_out.at[3])
    x_copy.start()
    for copy in local:
        copy.start()
    og_copy = pltpu.make_async_copy(og_hbm, og, sem_out.at[2])
    og_copy.start()
    small = [
        pltpu.make_async_copy(src, dst, sem_out.at[4 + i])
        for i, (src, dst) in enumerate(
            [
                (biases_hbm, biases_t),
                (seg_hbm, seg),
                (val_hbm, val),
                (gain1_hbm, gain1),
                (gain2_hbm, gain2),
            ]
        )
    ]
    for copy in small:
        copy.start()

    row0 = (NB * t) // NU
    has_b = (NB * t + NB - 1) // NU != row0

    def place(j):
        u = NB * t + j
        row = u // NU
        return u, row, row - row0, u - row * NU

    def rows_at(w):
        return pl.ds(pl.multiple_of(w * B, B), B)

    def block_at(j):
        return pl.ds(j * B, B)

    pl.semaphore_wait(barrier, heard)

    x_copy.wait()

    def send_rows():
        for j in range(NB):
            u, row, slot, w = place(j)
            first = row * NU // NB
            last = (row * NU + NU - 1) // NB
            for o in range(lay.span):
                dest = first + o

                @pl.when((dest <= last) & (dest != t))
                def _():
                    remote(
                        x.at[block_at(j)],
                        xkv.at[row - (NB * dest) // NU, rows_at(w)],
                        sem_hs.at[j * lay.span + o],
                        sem_hr.at[(row - (NB * dest) // NU) * NU + w],
                        (dp, dest),
                    ).start()

    if quads:
        role = dp % 4
        relay = role == 3
        gy = role % 3
        gx = jnp.where(role == 1, 0, jnp.where(role == 3, 2, 1))
        gz = jnp.where(role == 2, 0, jnp.where(role == 3, 1, 2))
        far = rank(2)
        core, ynext = (dp, rank(1)), (dp, rank(2))
        xnext, znext = (flip(dp, 1), t), (flip(dp, 2), t)
        rounds = 4
        tail_step = (rounds - 1) * SUBS
        steps = tail_step + LAST_SUBS
        part_a, part_b, part_c = D // SUBS, UNIT // SUBS, UNIT // LAST_SUBS

        def chunk(idx, g, fn):
            n = g * steps + idx

            @pl.when((idx >= 0) & (idx < SUBS))
            def _():
                at = pl.ds(pl.multiple_of(idx * part_a, part_a), part_a)
                fn(lambda r: wqkv.at[r, g, at], n)

            @pl.when((idx >= SUBS) & (idx < tail_step))
            def _():
                row = ((idx // SUBS - 1) * 3 + g) * UNIT + (idx % SUBS) * part_b
                at = pl.ds(pl.multiple_of(row, part_b), part_b)
                fn(lambda r: big.at[r, at], n)

            @pl.when((idx >= tail_step) & (idx < steps))
            def _():
                row = ((rounds - 2) * 3 + g) * UNIT + (idx - tail_step) * part_c
                at = pl.ds(pl.multiple_of(row, part_c), part_c)
                fn(lambda r: big.at[r, at], n)

        relayed = steps - DIRECT
        g_direct = jnp.where(role == 1, 2, 1)
        is_served = (role == 1) | (role == 2)

        def send_y(idx):
            def go(view, n):
                remote(view(t), view(t), sem_y.at[idx], sem_w.at[n], ynext).start()

            chunk(idx, gy, go)

            def go_direct(view, n):
                remote(
                    view(t), view(t), sem_y.at[idx + DIRECT], sem_w.at[n], ynext
                ).start()

            @pl.when((idx >= relayed) & is_served)
            def _():
                chunk(idx, g_direct, go_direct)

        def to_core(view, n):
            remote(view(far), view(far), sem_c.at[n], sem_p.at[n], core).start()

        def arrived(view, n):
            remote(view(far), view(far), sem_c.at[n], sem_w.at[n], core).wait_recv()

        def to_x(view, n, idx):
            remote(view(far), view(far), sem_x.at[idx], sem_w.at[n], xnext).start()

        def to_z(view, n, idx):
            remote(view(far), view(far), sem_z.at[idx], sem_w.at[n], znext).start()

        def service(s, carry):
            def from_y(view, n):
                arrived(view, n)

                @pl.when(role != 3)
                def _():
                    to_x(view, n, s)
                    to_z(view, n, s)

                to_core(view, n)

            chunk(s, gy, from_y)
            send_y(s + SUBS)
            late = s - jnp.where(relay, RELAY_LAG, LAG)

            def from_x(view, n):
                arrived(view, n)

                @pl.when(relay & (late < relayed))
                def _():
                    to_z(view, n, late)

                to_core(view, n)

            def from_z(view, n):
                arrived(view, n)

                @pl.when(relay & (late < relayed))
                def _():
                    to_x(view, n, late)

                to_core(view, n)

            chunk(late, gx, from_x)
            chunk(late, gz, from_z)
            return carry

        def sent(idx, carry):
            def go(view, n):
                remote(view(t), view(t), sem_y.at[idx], sem_w.at[n], ynext).wait_send()

                @pl.when((role != 3) | (idx < relayed))
                def _():
                    remote(view(t), view(t), sem_x.at[idx], sem_w.at[n], xnext).wait_send()
                    remote(view(t), view(t), sem_z.at[idx], sem_w.at[n], znext).wait_send()

                @pl.when((idx >= relayed) & is_served)
                def _():
                    remote(
                        view(t), view(t), sem_y.at[idx + DIRECT], sem_w.at[n], ynext
                    ).wait_send()

                for g in range(3):
                    m = g * steps + idx
                    remote(view(t), view(t), sem_c.at[m], sem_p.at[m], core).wait_send()

            chunk(idx, gy, go)
            return carry

        def from_partner(units):
            for unit in units:
                p, g = unit // 3, unit % 3
                if p == 0:
                    view = wqkv.at[rank(3), 0, pl.ds(0, part_a)]
                else:
                    view = big.at[rank(3), pl.ds(0, part_c if p == rounds - 1 else part_b)]

                def go(idx, carry):
                    n = g * steps + idx
                    remote(view, view, sem_c.at[n], sem_p.at[n], core).wait_recv()
                    return carry

                if p == rounds - 1:
                    lax.fori_loop(tail_step, steps, go, 0)
                else:
                    lax.fori_loop(p * SUBS, (p + 1) * SUBS, go, 0)

        def own_copies(i):
            return remote(sources[i], pieces(t)[i], sem_own_s.at[i], sem_own_r.at[i], core)

        local[0].wait()
        lax.fori_loop(0, 2, lambda i, c: (send_y(i), c)[1], 0)
        send_rows()
        lax.fori_loop(2, SUBS, lambda i, c: (send_y(i), c)[1], 0)
        for i in range(4):
            own_copies(i).start()
        for i in range(1, 4):
            local[i].wait()

        first_unit = [0, 3, 4, 8, 12]

        def ready(i, o):
            @pl.when(o == 1)
            def _():
                remote(
                    sources[i], pieces(rank(1))[i], sem_own_s.at[i], sem_own_r.at[i], core
                ).wait_recv()

            @pl.when(o == 3)
            def _():
                from_partner(range(first_unit[i], first_unit[i + 1]))

    else:

        def own_copies(i, o):
            n = i * T + o
            return remote(sources[i], pieces(t)[i], sem_own_s.at[n], sem_own_r.at[n], peer(o))

        send_rows()
        for i in range(4):
            for o in range(1, T):
                own_copies(i, o).start()

        def ready(i, o):
            @pl.when(o == 0)
            def _():
                local[i].wait()

            @pl.when(o != 0)
            def _():
                n = i * T + o
                remote(
                    sources[i], pieces(rank(o))[i], sem_own_s.at[n], sem_own_r.at[n], peer(o)
                ).wait_recv()

    for copy in small:
        copy.wait()
    key_at = lax.broadcasted_iota(jnp.int32, (B, SEQ), 1)
    query_at = lax.broadcasted_iota(jnp.int32, (B, SEQ), 0)
    for j in range(NB):
        u, row, slot, w = place(j)
        keys_here = pl.ds(pl.multiple_of(row * SEQ, SEQ), SEQ)
        numbers = seg[keys_here].reshape(1, SEQ).astype(F32)
        keyed = jnp.where(val[keys_here].reshape(1, SEQ) == 1, numbers, -1.0)
        same = key_at == query_at + w * B
        own = jnp.sum(jnp.where(same, numbers, 0.0), axis=1, keepdims=True)
        mask[j] = jnp.where((own == keyed) | same, 0.0, -1e30)
        xkv[slot, rows_at(w)] = x[block_at(j)]

    bias_rows = biases_t[...].T
    for i in range(BROWS):
        brow[:, i * HD : (i + 1) * HD] = bias_rows[i : i + 1]

    head_lane = lax.broadcasted_iota(jnp.int32, (B, PAIR), 1) < HD

    def split_heads(values):
        nought = jnp.zeros_like(values)
        return jnp.concatenate(
            [jnp.where(head_lane, values, nought), jnp.where(head_lane, nought, values)], axis=0
        )

    def join_heads(values):
        return jnp.where(head_lane, values[:B], values[B:])

    ones = jnp.ones((SEQ, PAIR), BF16)

    slot_first = jnp.where(has_b & (t % 4 == 2), 1, 0)

    def project_query(r):
        bias = brow[:, pl.ds(pl.multiple_of(AT_QUERY + r * W, PAIR), W)]
        query = ((nn(x[...], wqkv[r, 0]) + bias) * HD**-0.5).astype(BF16)
        for i in range(PP):
            qbuf[r * PP + i] = query[:, i * PAIR : (i + 1) * PAIR]

    def project_keys(o, r):
        bias = brow[:, pl.ds(pl.multiple_of(AT_VALUE + r * W, PAIR), W)]

        def body(turn, carry):
            slot = (slot_first + turn) % 2

            @pl.when((slot == 0) | has_b)
            def _():
                for w in range(NU):
                    owner = ((row0 + slot) * NU + w) // NB

                    @pl.when((owner != t) & (o == 0))
                    def _():
                        remote(
                            x.at[block_at(0)],
                            xkv.at[slot, rows_at(w)],
                            sem_hs.at[0],
                            sem_hr.at[slot * NU + w],
                            (dp, owner),
                        ).wait_recv()

                rows = xkv[slot]
                keys = nn(rows, wqkv[r, 1]).astype(BF16)
                values = (nn(rows, wqkv[r, 2]) + bias).astype(BF16)
                for i in range(PP):
                    kbuf[r * PP + i, slot] = keys[:, i * PAIR : (i + 1) * PAIR]
                    vbuf[r * PP + i, slot] = values[:, i * PAIR : (i + 1) * PAIR]

            return carry

        lax.fori_loop(0, 2, body, 0)

    def attend(r, i):
        hp = r * PP + i
        for j in range(NB):
            u, row, slot, w = place(j)
            query = split_heads(qbuf[hp, block_at(j)])
            hide = mask[j]
            scores = nt(query, kbuf[hp, slot]) + jnp.concatenate([hide, hide], axis=0)
            peak = jnp.max(scores, axis=1, keepdims=True)
            probs = jnp.exp(scores - peak).astype(BF16)
            pbuf[hp, j * 2 * B : (j + 1) * 2 * B] = probs
            mixed = nn(probs, jnp.concatenate([vbuf[hp, slot], ones], axis=1))
            inverse = 1.0 / join_heads(mixed[:, PAIR:])
            linv[hp, block_at(j)] = inverse
            ctx[r, block_at(j), pl.ds(i * PAIR, PAIR)] = (
                join_heads(mixed[:, :PAIR]) * inverse
            ).astype(BF16)

    def project(o):
        ready(0, o)
        r = rank(o)
        project_query(r)
        project_keys(o, r)

    def attend_rank(o):
        for i in range(PP):
            attend(rank(o), i)

    def row_mean(values):
        return jnp.mean(values, axis=1, keepdims=True)

    def row_tiles(body, carry):
        for j in range(NB):
            carry = body(block_at(j), carry)
        return carry

    def norm_first(at, carry):
        values = abuf[at]
        centred = values - row_mean(values)
        root = lax.rsqrt(row_mean(centred * centred) + EPS_NORM)
        normed = centred * root
        r1buf[at] = root
        abuf[at] = normed
        first_normed = normed * gain1[...] + brow[:, AT_FIRST : AT_FIRST + D]
        low[at] = first_normed.astype(BF16)
        bbuf[at] = first_normed + brow[:, AT_FFN : AT_FFN + D]
        return carry

    def finish_attention():
        for o in range(T):
            ready(1, o)
        for n in range(0, D, TILE):
            total = nn(ctx[0], wo(0)[:, n : n + TILE])
            for r in range(1, T):
                total = total + nn(ctx[r], wo(r)[:, n : n + TILE])
            at = pl.ds(n, TILE)
            abuf[:, at] = x[:, at].astype(F32) + total + brow[:, AT_OUT + n : AT_OUT + n + TILE]
        row_tiles(norm_first, 0)

    def expand(o):
        ready(2, o)
        r = rank(o)
        for n in range(0, F, TILE):
            bias = brow[:, pl.ds(pl.multiple_of(AT_HIDDEN + r * F + n, PAIR), TILE)]
            pre = nn(low[...], w1(r)[:, n : n + TILE]) + bias
            cdf = 0.5 * (1.0 + lax.erf(pre * 0.5**0.5))
            density = jnp.exp(-0.5 * pre * pre) * 0.3989422804014327
            hid[r, :, pl.ds(n, TILE)] = (pre * cdf).astype(BF16)
            gp[r, :, pl.ds(n, TILE)] = (cdf + pre * density).astype(BF16)

    def reduce(o):
        ready(3, o)
        r = rank(o)
        for n in range(0, D, TILE):
            at = pl.ds(n, TILE)
            bbuf[:, at] = bbuf[:, at] + nn(hid[r], w2(r)[:, n : n + TILE])

    if quads:
        whole = [(k + 1) * SUBS + LAG - 1 for k in range(rounds - 1)] + [steps + LAG - 1]
        plan = [
            (project, [PLAN[0], PLAN[1], whole[0], whole[0] + 2]),
            (attend_rank, [PLAN[2], PLAN[3], whole[0] + 1, whole[0] + 3]),
            (expand, [whole[1] + 1, whole[1] + 2, whole[2], whole[2] + 1]),
            (reduce, [whole[1] + 3, whole[1] + 4]),
        ]

        def pass_on(place_in_chain, sem, to, s):
            @pl.when(s == 2 * place_in_chain)
            def _():
                @pl.when(place_in_chain > 0)
                def _():
                    pl.semaphore_wait(sem, 1)

                @pl.when(place_in_chain < links - 1)
                def _():
                    pl.semaphore_signal(sem, inc=1, device_id=to, device_id_type=MESH_ID)

        def step(s, carry):
            service(s, 0)
            pass_on(link, sem_up, after, s)
            pass_on(links - 1 - link, sem_down, before, s)

            @pl.when(s == whole[1])
            def _():
                finish_attention()

            for part, at_steps in plan:
                o = jnp.int32(-1)
                for k, at_step in enumerate(at_steps):
                    if at_step < whole[3]:
                        o = jnp.where(s == at_step, k, o)

                @pl.when(o >= 0)
                def _():
                    part(o)

            return carry

        lax.fori_loop(0, whole[3] + 1, step, 0)
        lax.fori_loop(2, T, lambda o, c: (reduce(o), c)[1], 0)
    else:

        def each_rank(part):
            lax.fori_loop(0, T, lambda o, c: (part(o), c)[1], 0)

        each_rank(project)
        each_rank(attend_rank)
        finish_attention()
        each_rank(expand)
        each_rank(reduce)

    nought_row = jnp.zeros((1, D), F32)
    og_copy.wait()

    def norm_second(at, carry):
        sum_up, sum_second = carry
        values = bbuf[at]
        centred = values - row_mean(values)
        root = lax.rsqrt(row_mean(centred * centred) + EPS_NORM)
        normed = centred * root
        out[at] = (normed * gain2[...] + brow[:, AT_SECOND : AT_SECOND + D]).astype(BF16)
        upstream = og[at].astype(F32)
        weighted = upstream * gain2[...]
        grad = root * (weighted - row_mean(weighted) - normed * row_mean(weighted * normed))
        bbuf[at] = grad
        low[at] = grad.astype(BF16)
        return (
            sum_up + jnp.sum(upstream, axis=0, keepdims=True),
            sum_second + jnp.sum(grad, axis=0, keepdims=True),
        )

    sum_up, sum_second = row_tiles(norm_second, (nought_row, nought_row))
    out_copy = pltpu.make_async_copy(out, out_hbm, sem_out.at[0])
    out_copy.start()
    bsum[:, AT_SECOND : AT_SECOND + D] = sum_up
    bsum[:, AT_FFN : AT_FFN + D] = sum_second

    def ffn_back(r, carry):
        for n in range(0, F, TILE):
            grad = nt(low[...], w2(r)[n : n + TILE, :]) * gp[r, :, pl.ds(n, TILE)].astype(F32)
            at = pl.ds(pl.multiple_of(AT_HIDDEN + r * F + n, PAIR), TILE)
            bsum[:, at] = jnp.sum(grad, axis=0, keepdims=True)
            hid[r, :, pl.ds(n, TILE)] = grad.astype(BF16)
        return carry

    lax.fori_loop(0, T, ffn_back, 0, unroll=4)
    for n in range(0, D, TILE):
        total = nt(hid[0], w1(0)[n : n + TILE, :])
        for r in range(1, T):
            total = total + nt(hid[r], w1(r)[n : n + TILE, :])
        cbuf[:, pl.ds(n, TILE)] = total

    def first_back(at, carry):
        sum_normed, sum_first = carry
        grad = bbuf[at] + cbuf[at]
        normed = abuf[at]
        weighted = grad * gain1[...]
        first = r1buf[at] * (
            weighted - row_mean(weighted) - normed * row_mean(weighted * normed)
        )
        bbuf[at] = first
        low[at] = first.astype(BF16)
        return (
            sum_normed + jnp.sum(grad, axis=0, keepdims=True),
            sum_first + jnp.sum(first, axis=0, keepdims=True),
        )

    sum_normed, sum_first = row_tiles(first_back, (nought_row, nought_row))
    bsum[:, AT_FIRST : AT_FIRST + D] = sum_normed
    bsum[:, AT_OUT : AT_OUT + D] = sum_first

    class Totals:
        def __init__(self, number, start, amount, group, everyone):
            self.number, self.at = number, pl.ds(start, amount)
            self.group, self.everyone = group, everyone

        def copies(self, buffer, sems, me, peers):
            send, recv = sems
            return [
                remote(
                    buffer.at[me],
                    buffer.at[me],
                    send.at[self.number, k],
                    recv.at[self.number, me],
                    device,
                )
                for k, device in enumerate(peers)
            ]

        def gather(self, buffer, sems, me, peers):
            for copy in self.copies(buffer, sems, me, peers):
                copy.wait_send()
            for k in range(buffer.shape[0]):

                @pl.when(k != me)
                def _():
                    remote(
                        buffer.at[k], buffer.at[k], sems[0].at[0, 0], sems[1].at[self.number, k], peers[0]
                    ).wait_recv()

            total = buffer[0]
            for k in range(1, buffer.shape[0]):
                total = total + buffer[k]
            return total

        def start(self):
            self.group[t] = bsum[:, self.at]
            for copy in self.copies(self.group, (sem_as, sem_ar), t, in_group):
                copy.start()

        def middle(self):
            self.everyone[dp] = self.gather(self.group, (sem_as, sem_ar), t, in_group)
            for copy in self.copies(self.everyone, (sem_bs, sem_br), dp, in_dp):
                copy.start()

        def finish(self):
            bsum[:, self.at] = self.gather(self.everyone, (sem_bs, sem_br), dp, in_dp)

    in_group = [peer(o) for o in range(1, T)]
    in_dp = [((dp + o) % lay.dp_size, t) for o in range(1, lay.dp_size)]
    early = Totals(0, AT_VALUE, FLAT - AT_VALUE, group_early, all_early)
    late = Totals(1, AT_QUERY, AT_VALUE, group_late, all_late)

    for r in range(T):
        grad = nt(low[...], wo(r)[...]).astype(BF16)
        cgrad[r] = grad
        bsum[:, AT_VALUE + r * W : AT_VALUE + (r + 1) * W] = jnp.sum(
            grad.astype(F32), axis=0, keepdims=True
        )
    early.start()

    lone = jnp.where(place(1)[1] != place(0)[1], 0, NB - 1)
    pair_at = jnp.where(lone == 0, 1, 0)
    slot_pair = (NB * t + pair_at) // NU - row0
    slot_lone = (NB * t + lone) // NU - row0
    slot_kept = jnp.where(has_b, slot_pair, 1)

    def attend_back(r, i, first_block, amount, slot):
        hp = r * PP + i
        lanes = pl.ds(i * PAIR, PAIR)
        queries, upstreams, deltas = [], [], []
        for k in range(amount):
            at = rows_at(first_block + k)
            scaled = cgrad[r, at, lanes].astype(F32) * linv[hp, at]
            upstreams.append(split_heads(scaled.astype(BF16)))
            deltas.append(split_heads(scaled * ctx[r, at, lanes].astype(F32)))
            queries.append(split_heads(qbuf[hp, at]))
        upstream, query = jnp.concatenate(upstreams), jnp.concatenate(queries)
        delta = jnp.sum(jnp.concatenate(deltas), axis=1, keepdims=True)
        probs = pbuf[hp, pl.ds(pl.multiple_of(first_block * 2 * B, 2 * B), amount * 2 * B)]
        score = (probs.astype(F32) * (nt(upstream, vbuf[hp, slot]) - delta)).astype(BF16)
        value_grad = nn(upstream.T, probs)
        key_grad = nn(query.T, score)
        joined = nn(score, kbuf[hp, slot]) * HD**-0.5
        total = jnp.zeros((1, PAIR), F32)
        for k in range(amount):
            grad = join_heads(joined[k * 2 * B : (k + 1) * 2 * B])
            qbuf[hp, rows_at(first_block + k)] = grad.astype(BF16)
            total = total + jnp.sum(grad, axis=0, keepdims=True)
        return key_grad.astype(BF16).T, value_grad.astype(BF16).T, total

    def rank_back_pair(r, carry):
        for i in range(PP):
            keys, values, total = attend_back(r, i, pair_at, 2, slot_pair)
            kbuf[r * PP + i, slot_kept] = keys
            vbuf[r * PP + i, slot_kept] = values
            bsum[:, pl.ds(pl.multiple_of(AT_QUERY + r * W + i * PAIR, PAIR), PAIR)] = total

        @pl.when(r == T // 2 - 1)
        def _():
            early.middle()

        return carry

    def rank_back_lone(r, carry):
        for i in range(PP):
            hp = r * PP + i
            keys, values, total = attend_back(r, i, lone, 1, slot_lone)
            at = pl.ds(pl.multiple_of(AT_QUERY + r * W + i * PAIR, PAIR), PAIR)
            bsum[:, at] = bsum[:, at] + total
            kept = [jnp.where(has_b, jnp.zeros_like(keys), buf[hp, 1]) for buf in (kbuf, vbuf)]
            kbuf[hp, slot_lone] = keys + kept[0]
            vbuf[hp, slot_lone] = values + kept[1]
        return carry

    def wide(buffer, r, *at):
        return jnp.concatenate([buffer[(r * PP + i, *at)] for i in range(PP)], axis=1)

    half = SEQ // 2

    def share_copy(slot, w, k):
        u = (row0 + slot) * NU + w
        owner = u // NB
        first = (row0 + slot) * NU // NB
        place_of = t - first - jnp.where(t > owner, 1, 0)
        number = (u - owner * NB) * (lay.span - 1) + place_of
        at = pl.ds(pl.multiple_of(k * TILE, TILE), TILE)
        return remote(
            xkv.at[slot, rows_at(w), at],
            back.at[number, :, at],
            sem_gs.at[slot * NU + w, k],
            sem_gr.at[number, k],
            (dp, owner),
        )

    def send_shares(slot, rows, first_unit, amount):
        def body(k, carry):
            at = pl.ds(pl.multiple_of(k * TILE, TILE), TILE)
            total = nt(wide(kbuf, 0, slot, rows), wqkv[0, 1, at])
            total = total + nt(wide(vbuf, 0, slot, rows), wqkv[0, 2, at])
            for r in range(1, T):
                total = total + nt(wide(kbuf, r, slot, rows), wqkv[r, 1, at])
                total = total + nt(wide(vbuf, r, slot, rows), wqkv[r, 2, at])
            xkv[slot, rows, at] = total.astype(BF16)
            for n in range(amount):
                w = first_unit + n
                owner = ((row0 + slot) * NU + w) // NB

                @pl.when(owner != t)
                def _():
                    share_copy(slot, w, k).start()

            return carry

        lax.fori_loop(0, D // TILE, body, 0)

    def send_half(slot, part):
        rows = pl.ds(pl.multiple_of(part * half, half), half)
        send_shares(slot, rows, part * (NU // 2), NU // 2)

    lax.fori_loop(0, T, rank_back_pair, 0)
    part_first = jnp.where(lone == 0, 1, 0)

    lax.fori_loop(0, T, rank_back_lone, 0, unroll=2)
    late.start()

    def halves(k, carry):
        @pl.when(has_b)
        def _():
            send_half(slot_pair, (part_first + k) % 2)

        return carry

    lax.fori_loop(0, 2, halves, 0)
    late.middle()
    send_shares(slot_lone, pl.ds(0, SEQ), 0, NU)

    for n in range(0, D, TILE):
        total = nt(wide(qbuf, 0), wqkv[0, 0, pl.ds(n, TILE)])
        for r in range(1, T):
            total = total + nt(wide(qbuf, r), wqkv[r, 0, pl.ds(n, TILE)])
        at = pl.ds(n, TILE)
        bbuf[:, at] = bbuf[:, at] + total

    for j in range(NB):
        u, row, slot, w = place(j)
        bbuf[block_at(j)] = bbuf[block_at(j)] + xkv[slot, rows_at(w)].astype(F32)
    early.finish()

    for j in range(NB):
        u, row, slot, w = place(j)
        first = row * NU // NB
        last = (row * NU + NU - 1) // NB
        for o in range(lay.span):
            dest = first + o

            @pl.when((dest <= last) & (dest != t))
            def _():
                remote(
                    x.at[block_at(j)],
                    xkv.at[0, rows_at(0)],
                    sem_hs.at[j * lay.span + o],
                    sem_hr.at[0],
                    (dp, dest),
                ).wait_send()

    if quads:
        for i in range(4):
            own_copies(i).wait_send()
        lax.fori_loop(0, steps, sent, 0)
    else:
        for i in range(4):
            for o in range(1, T):
                own_copies(i, o).wait_send()

    for j in range(NB):
        u, row, slot, w = place(j)
        first = row * NU // NB
        last = (row * NU + NU - 1) // NB
        for o in range(lay.span - 1):
            number = j * (lay.span - 1) + o

            @pl.when(first + o < last)
            def _():
                sender = first + o + jnp.where(first + o >= t, 1, 0)
                for k in range(D // TILE):
                    at = pl.ds(k * TILE, TILE)
                    remote(
                        xkv.at[0, rows_at(0), at],
                        back.at[number, :, at],
                        sem_gs.at[0, k],
                        sem_gr.at[number, k],
                        (dp, sender),
                    ).wait_recv()
                bbuf[block_at(j)] = bbuf[block_at(j)] + back[number].astype(F32)

        ig[block_at(j)] = bbuf[block_at(j)].astype(BF16)

    ig_copy = pltpu.make_async_copy(ig, ig_hbm, sem_out.at[1])
    ig_copy.start()
    late.finish()

    out_copy.wait()
    ig_copy.wait()
    for slot in range(2):
        for w in range(NU):
            owner = ((row0 + slot) * NU + w) // NB

            @pl.when((owner != t) & ((slot == 0) | has_b))
            def _():
                lax.fori_loop(0, D // TILE, lambda k, c: (share_copy(slot, w, k).wait_send(), c)[1], 0)


def layer_call(lay, *args):
    T, S = lay.ranks, lay.tokens
    hp = HEADS // 2
    vmem = pltpu.VMEM
    if lay.quads:
        wide = [
            vmem((T, lay.width + D + lay.hidden, D), BF16),
            vmem((16, PAIR), BF16),
            vmem((16, PAIR), BF16),
        ]
    else:
        wide = [
            vmem((T, lay.width, D), BF16),
            vmem((T, D, lay.hidden), BF16),
            vmem((T, lay.hidden, D), BF16),
        ]
    dma = pltpu.SemaphoreType.DMA
    steps = 3 * SUBS + LAST_SUBS
    own = 4 if lay.quads else 4 * T
    sharers = lay.blocks * max(lay.span - 1, 1)
    scratch = (
        [vmem((1, FLAT), F32)]
        + [vmem((S, D), BF16)] * 4
        + [vmem((1, D), F32)] * 2
        + [vmem((HD, BROWS), F32)]
        + [vmem((T * S,), jnp.int32)] * 2
        + [vmem((T, 3, D, lay.width), BF16)]
        + wide
        + [
            vmem((2, SEQ, D), BF16),
            vmem((hp, S, PAIR), BF16),
            vmem((hp, 2, SEQ, PAIR), BF16),
            vmem((hp, 2, SEQ, PAIR), BF16),
            vmem((hp, lay.blocks * 2 * lay.block, SEQ), BF16),
            vmem((hp, S, PAIR), F32),
            vmem((lay.blocks, lay.block, SEQ), F32),
            vmem((T, S, lay.width), BF16),
            vmem((T, S, lay.width), BF16),
            vmem((S, D), F32),
            vmem((S, D), F32),
            vmem((S, D), F32),
            vmem((S, 1), F32),
            vmem((S, D), BF16),
            vmem((T, S, lay.hidden), BF16),
            vmem((T, S, lay.hidden), BF16),
            vmem((sharers, lay.block, D), BF16),
            vmem((T, 1, FLAT - AT_VALUE), F32),
            vmem((T, 1, AT_VALUE), F32),
            vmem((lay.dp_size, 1, FLAT - AT_VALUE), F32),
            vmem((lay.dp_size, 1, AT_VALUE), F32),
            dma((4,)),
            dma((9,)),
            dma((own,)),
            dma((own,)),
            dma((steps + DIRECT,)),
            dma((steps,)),
            dma((steps,)),
            dma((3 * steps,)),
            dma((3 * steps,)),
            dma((3 * steps,)),
            dma((lay.blocks * lay.span,)),
            dma((2 * lay.units,)),
            dma((2 * lay.units, D // TILE)),
            dma((sharers, D // TILE)),
            dma((2, T)),
            dma((2, T)),
            dma((2, lay.dp_size)),
            dma((2, lay.dp_size)),
            pltpu.SemaphoreType.REGULAR,
            pltpu.SemaphoreType.REGULAR,
        ]
    )
    in_vmem = pl.BlockSpec(memory_space=pltpu.VMEM)
    anywhere = pl.BlockSpec(memory_space=pl.ANY)
    return pl.pallas_call(
        partial(layer_kernel, lay),
        out_shape=(
            jax.ShapeDtypeStruct((S, D), BF16),
            jax.ShapeDtypeStruct((S, D), BF16),
            jax.ShapeDtypeStruct((1, FLAT), F32),
        ),
        in_specs=[anywhere] * 11,
        out_specs=(anywhere, anywhere, in_vmem),
        scratch_shapes=scratch,
        compiler_params=pltpu.CompilerParams(
            collective_id=0, has_side_effects=True, vmem_limit_bytes=VMEM_BYTES
        ),
        name="layer",
    )(*args)


VMEM_BYTES = 63 * 2**20
PLAN = [2, 5, 3, 6]
PARTS = 4


def update_kernel(
    raw,
    biases,
    moment_one,
    moment_two,
    left_pairs,
    left_hidden,
    left_small,
    right_bases,
    owners,
    out_in,
    ig_in,
    clipped_out,
    norm_out,
    new_out,
    copies_out,
    one_out,
    two_out,
    out_out,
    ig_out,
    rows,
    left,
    wide,
    sems,
):
    amount = out_in.shape[0] // PARTS
    parts = [pl.ds(k * amount, amount) for k in range(PARTS)]
    fetches = [
        pltpu.make_async_copy(src.at[at], wide.at[i, at], sems.at[0, i, k])
        for i, src in enumerate((out_in, ig_in))
        for k, at in enumerate(parts)
    ]
    stores = [
        pltpu.make_async_copy(wide.at[i, at], dst.at[at], sems.at[1, i, k])
        for i, dst in enumerate((out_out, ig_out))
        for k, at in enumerate(parts)
    ]
    for fetch in fetches:
        fetch.start()
    sums = raw[...]
    norm = jnp.sqrt(jnp.sum(sums * sums, keepdims=True))
    norm_out[...] = norm
    for i in range(BROWS):
        rows[i : i + 1] = sums[:, i * HD : (i + 1) * HD]
    clipped = rows[...].T * (CLIP_LIMIT / jnp.maximum(norm, CLIP_LIMIT))
    clipped_out[...] = clipped
    dp = lax.axis_index("dp")
    tail = 2 * HEADS + FR
    layout = [(0, 2 * HEADS, left_pairs), (2 * HEADS, FR, left_hidden)]
    layout += [(tail + k * DR, DR, left_small.at[k]) for k in range(4)]
    left[...] = jnp.zeros_like(left)
    for begin, amount, basis in layout:
        left[begin : begin + amount, begin : begin + amount] = basis[...]
    for fetch, store in zip(fetches, stores):
        fetch.wait()
        store.start()
    column = lax.broadcasted_iota(jnp.int32, (HD, BROWS), 1)

    def per_matrix(choose):
        result = choose(0)
        for k in range(1, len(layout)):
            result = jnp.where(column >= layout[k][0], choose(k), result)
        return result

    def product(a, b, over_a, over_b):
        return lax.dot_general(
            a,
            b,
            (((over_a,), (over_b,)), ((), ())),
            precision=HIGHEST,
            preferred_element_type=F32,
        )

    half = product(clipped, left[...], 1, 0)
    rotated = per_matrix(lambda k: product(right_bases[k], half, 0, 0))
    one = BETA_ONE * moment_one[...] + (1.0 - BETA_ONE) * rotated
    two = BETA_TWO * moment_two[...] + (1.0 - BETA_TWO) * rotated * rotated
    direction = (
        one / (1.0 - BETA_ONE**STEP) / (jnp.sqrt(two / (1.0 - BETA_TWO**STEP)) + ADAM_EPS)
    )
    half = per_matrix(lambda k: product(right_bases[k], direction, 1, 0))
    new = biases[...] - LEARN_RATE * product(half, left[...], 1, 1)
    copies_out[...] = new.astype(BF16)
    mine = per_matrix(lambda k: jnp.where(owners[k] == dp, 1.0, 0.0)) > 0.5
    new_out[...] = jnp.where(mine, new, 0.0)
    one_out[...] = jnp.where(mine, one, 0.0)
    two_out[...] = jnp.where(mine, two, 0.0)
    for store in stores:
        store.wait()


def update_call(tokens, *args):
    in_vmem = pl.BlockSpec(memory_space=pltpu.VMEM)
    anywhere = pl.BlockSpec(memory_space=pl.ANY)
    block = jax.ShapeDtypeStruct((HD, BROWS), F32)
    wide = jax.ShapeDtypeStruct((tokens, D), BF16)
    return pl.pallas_call(
        update_kernel,
        out_shape=(
            block,
            jax.ShapeDtypeStruct((1, 1), F32),
            block,
            jax.ShapeDtypeStruct((HD, BROWS), BF16),
            block,
            block,
            wide,
            wide,
        ),
        in_specs=[in_vmem] * 8 + [pl.BlockSpec(memory_space=pltpu.SMEM)] + [anywhere] * 2,
        out_specs=(in_vmem,) * 6 + (anywhere,) * 2,
        scratch_shapes=[
            pltpu.VMEM((BROWS, HD), F32),
            pltpu.VMEM((BROWS, BROWS), F32),
            pltpu.VMEM((2, tokens, D), BF16),
            pltpu.SemaphoreType.DMA((2, 2, PARTS)),
        ],
        name="update",
    )(*args)


def on_device(
    dp_size,
    ranks,
    inputs,
    output_grad,
    input_project,
    output_project,
    expand_weight,
    reduce_weight,
    first_gain,
    second_gain,
    biases,
    first_moment,
    second_moment,
    left_pairs,
    left_hidden,
    left_small,
    right_bases,
    segment_number,
    token_mask,
    owners,
):
    lay = Layout(dp_size, ranks, inputs.shape[0])
    layer_out, input_grad, sums = layer_call(
        lay,
        inputs,
        output_grad,
        first_gain.reshape(1, D),
        second_gain.reshape(1, D),
        biases.T,
        segment_number,
        token_mask,
        input_project,
        output_project,
        expand_weight,
        reduce_weight,
    )
    clipped, clip_norm, new_owned, copies, first_owned, second_owned, layer_out, input_grad = (
        update_call(
            inputs.shape[0],
            sums,
            biases.T,
            first_moment.T,
            second_moment.T,
            left_pairs,
            left_hidden,
            left_small,
            right_bases,
            owners,
            layer_out,
            input_grad,
        )
    )
    return (
        layer_out,
        input_grad,
        clipped.T,
        clip_norm.reshape(1),
        new_owned.T,
        copies.T,
        first_owned.T,
        second_owned.T,
    )


def solution(mesh):
    return jax.shard_map(
        partial(on_device, mesh.shape["dp"], mesh.shape["tensor"]),
        mesh=mesh,
        in_specs=(
            P(("dp", "tensor"), None),
            P(("dp", "tensor"), None),
            P(None, None, "tensor"),
            P("tensor", None),
            P(None, "tensor"),
            P("tensor", None),
            P(),
            P(),
            P(),
            P(),
            P(),
            P(),
            P(),
            P(),
            P(),
            P("dp"),
            P("dp"),
            P(),
        ),
        out_specs=(
            P(("dp", "tensor"), None),
            P(("dp", "tensor"), None),
            P(),
            P(),
            P("dp", None),
            P(),
            P("dp", None),
            P("dp", None),
        ),
        check_vma=False,
    )
```
